32 devices in a mesh: grp: 4 (over y, x), tok: 4 (over z), fs: 2 (over core).
Axes of the slice: x: 2, y: 2, z: 4, core: 2. Of those that a mesh axis runs over, the one named last changes fastest.
Arguments:
- hidden_in: bfloat16 [8192, 2304], P(('grp', 'tok', 'fs')), may hold values from -6 to 6
- cotangent: bfloat16 [8192, 2304], P(('grp', 'tok', 'fs')), may hold values from -6 to 6
- block_start: int32 [4, 16], P('grp'), may hold values from 0 to 1152, as said below
- query_weight: bfloat16 [2304, 2304], P(('tok', 'fs')), may hold values from -0.125 to 0.125
- key_weight: bfloat16 [2304, 2304], P(('tok', 'fs')), may hold values from -0.125 to 0.125
- value_weight: bfloat16 [2304, 2304], P(('tok', 'fs')), may hold values from -0.125 to 0.125
- output_weight: bfloat16 [2304, 2304], P(('tok', 'fs')), may hold values from -2 to 2
- gate_weight: bfloat16 [2304, 5760], P(('tok', 'fs')), may hold values from -0.125 to 0.125
- up_weight: bfloat16 [2304, 5760], P(('tok', 'fs')), may hold values from -0.125 to 0.125
- down_weight: bfloat16 [5760, 2304], P(('tok', 'fs')), may hold values from -0.3125 to 0.3125
- first_gain: bfloat16 [2304], P(('tok', 'fs')), may hold values from 0.099609375 to 1.8984375
- second_gain: bfloat16 [2304], P(('tok', 'fs')), may hold values from 0.099609375 to 1.8984375
Outputs:
- layer_output: bfloat16 [8192, 2304], P(('grp', 'tok', 'fs'))
- input_grad: float32 [8192, 2304], P(('grp', 'tok', 'fs'))
- query_grad: float32 [2304, 2304], P(('grp', 'tok', 'fs'))
- key_grad: float32 [2304, 2304], P(('grp', 'tok', 'fs'))
- value_grad: float32 [2304, 2304], P(('grp', 'tok', 'fs'))
- output_grad: float32 [2304, 2304], P(('grp', 'tok', 'fs'))
- gate_grad: float32 [2304, 5760], P(('grp', 'tok', 'fs'))
- up_grad: float32 [2304, 5760], P(('grp', 'tok', 'fs'))
- down_grad: float32 [5760, 2304], P(('grp', 'tok', 'fs'))
- first_gain_grad: float32 [2304], P(('grp', 'tok', 'fs'))
- second_gain_grad: float32 [2304], P(('grp', 'tok', 'fs'))
The draws below stay inside these ranges and needn't reach their ends.
Inputs may be any that keep to these rules, and one draw needn't show every extreme that they name: `block_start`: in each group, the first 8 entries are 0, 128, ..., 896 in some order, and each following run of 2 entries holds the starts 1024 + j * 128 for j = 0 to 1, in some order.
All inputs are finite; a program needn't handle non-finite values.
Results may differ from the reference program's by a relative error of at most 0.019.
Values may be sent and summed in bfloat16 or wider, within the bound.
No kernel may reach another device: no remote copies, remote signals or barrier semaphores. Data moves between devices by JAX's collectives and lax.ppermute only.
A program may use at most 704 MiB of HBM per device.

```python
import math
import jax
import jax.numpy as jnp
from jax import lax

D = 2304
HEADS = 36
HEAD_DIM = 64
FF = 5760
BLOCK = 128
PROMPT = 1024
CONT = 256
GROUP_TOK = 2048
TOKENS = 8192
N_GRP = 4


def draw_block_start(key, part):
    key = jax.random.fold_in(key, 11)
    prompt_blocks = PROMPT // BLOCK
    cont_blocks = CONT // BLOCK
    number = (GROUP_TOK - PROMPT) // CONT
    first_keys = jax.random.split(jax.random.fold_in(key, 1), N_GRP)
    prompt_order = jax.vmap(lambda one_key: jax.random.permutation(one_key, prompt_blocks))(first_keys)
    later_keys = jax.random.split(jax.random.fold_in(key, 2), N_GRP * number)
    cont_order = jax.vmap(lambda one_key: jax.random.permutation(one_key, cont_blocks))(later_keys)
    cont_order = cont_order.reshape(N_GRP, number * cont_blocks)
    return jnp.concatenate([prompt_order * BLOCK, PROMPT + cont_order * BLOCK], axis=1).astype(jnp.int32)


def levels(key, extent, shards, low, largest):
    loudness = 1.0
    for position, shards_of in shards:
        heights = jax.random.uniform(jax.random.fold_in(jax.random.fold_in(key, 6), position), (shards_of,), jnp.float32, low / len(shards), largest / len(shards))
        loudness = loudness * jnp.repeat(jnp.exp(heights), extent[position] // shards_of).reshape((-1,) + (1,) * (len(extent) - 1 - position))
    return loudness


def noise(rng, shape, scale, limit, cuts=(), held_as=jnp.bfloat16):
    values = scale * jax.random.normal(rng, shape, jnp.float32)
    if cuts:
        values = values * levels(rng, shape, cuts, -0.22, 0.18)
    return jnp.clip(values, -limit, limit).astype(held_as)


def setup_inputs(seed: int = 0) -> dict:
    streams_of = jax.random.split(jax.random.key(seed), 13)
    hidden_in = noise(streams_of[0], (TOKENS, D), 1.0, 6.0, ((0, 32),))
    cotangent = noise(streams_of[1], (TOKENS, D), 1.0, 6.0, ((0, 32),))
    block_start = draw_block_start(jax.random.fold_in(streams_of[12], 71), 0)
    query_weight = noise(streams_of[3], (D, D), D ** -0.5, 0.125, ((0, 8),))
    key_weight = noise(streams_of[4], (D, D), D ** -0.5, 0.125, ((0, 8),))
    value_weight = noise(streams_of[5], (D, D), D ** -0.5, 0.125, ((0, 8),))
    output_weight = noise(streams_of[6], (D, D), (max(D // 256, 1)) ** -0.5, 2.0, ((0, 8),))
    gate_weight = noise(streams_of[7], (D, FF), D ** -0.5, 0.125, ((0, 8),))
    up_weight = noise(streams_of[8], (D, FF), D ** -0.5, 0.125, ((0, 8),))
    down_weight = noise(streams_of[9], (FF, D), (max(FF // 16, 1)) ** -0.5, 0.3125, ((0, 8),))
    first_gain = jnp.clip(1.0 + 0.18 * jax.random.normal(streams_of[10], (D,), jnp.float32), 0.099609375, 1.8984375).astype(jnp.bfloat16)
    second_gain = jnp.clip(1.0 + 0.18 * jax.random.normal(streams_of[11], (D,), jnp.float32), 0.099609375, 1.8984375).astype(jnp.bfloat16)
    return dict(hidden_in=hidden_in, cotangent=cotangent, block_start=block_start, query_weight=query_weight, key_weight=key_weight, value_weight=value_weight, output_weight=output_weight, gate_weight=gate_weight, up_weight=up_weight, down_weight=down_weight, first_gain=first_gain, second_gain=second_gain)


@jax.custom_vjp
def low(v):
    return lax.optimization_barrier(v.astype(jnp.bfloat16)).astype(jnp.float32)

@jax.custom_vjp
def low_back(v):
    return v

def low_keep(v):
    return (low(v), None)

def low_pass(kept, grad):
    return (grad,)

def back_keep(v):
    return (v, None)

def back_low(kept, grad):
    return (low(grad),)
low.defvjp(low_keep, low_pass)
low_back.defvjp(back_keep, back_low)
EPS = 1e-05
RESIDUAL = 1.4 / math.sqrt(40.0)
NEGATIVE = -1e+30

def rope_tables(positions, head_size):
    half = head_size // 2
    freq = 10000.0 ** (-(jnp.arange(half, dtype=jnp.float32) * 2.0) / head_size)
    angle = positions.astype(jnp.float32)[:, None] * freq[None, :]
    return (jnp.cos(angle)[:, None, :], jnp.sin(angle)[:, None, :])

def rotate(field, cosine, sine):
    half = field.shape[-1] // 2
    first = field[..., :half]
    second = field[..., half:]
    return jnp.concatenate([first * cosine - second * sine, second * cosine + first * sine], axis=-1)

def row_norm(values):
    return values * lax.rsqrt(lax.optimization_barrier(jnp.mean(values * values, axis=-1, keepdims=True)) + EPS)

def product(left, right):
    return jnp.dot(left, right, precision=lax.Precision.HIGHEST)

def layer_forward(hidden, weights, cosine, sine, positions, segments):
    query_w, key_w, value_w, output_w, gate_w, up_w, down_w, gain_one, gain_two = weights
    count = hidden.shape[0]
    h_one = low(row_norm(hidden) * gain_one)
    queries = low_back(product(h_one, query_w)).reshape(count, HEADS, HEAD_DIM)
    keys = low_back(product(h_one, key_w)).reshape(count, HEADS, HEAD_DIM)
    values = low(low_back(product(h_one, value_w))).reshape(count, HEADS, HEAD_DIM)
    queries = low(rotate(queries, cosine, sine))
    keys = low(rotate(keys, cosine, sine))
    scale = 1.0 / math.sqrt(HEAD_DIM)
    size = math.gcd(512, count)

    def attend(block):
        query_block, query_pos, query_seg = block
        raw = jnp.einsum('qhd,khd->hqk', query_block, keys, precision=lax.Precision.HIGHEST)
        scores = low_back(raw * scale)
        visible = (positions[None, :] <= query_pos[:, None]) & ((segments[None, :] == 0) | (segments[None, :] == query_seg[:, None]))
        scores = jnp.where(visible[None], scores, NEGATIVE)
        peak = lax.optimization_barrier(jnp.max(scores, axis=-1, keepdims=True))
        expo = jnp.exp(scores - peak)
        probs = low(expo / lax.optimization_barrier(jnp.sum(expo, axis=-1, keepdims=True)))
        return jnp.einsum('hqk,khd->qhd', probs, values, precision=lax.Precision.HIGHEST)
    blocks = (queries.reshape(count // size, size, HEADS, HEAD_DIM), positions.reshape(count // size, size), segments.reshape(count // size, size))
    mixed = lax.map(jax.checkpoint(attend), blocks).reshape(count, HEADS * HEAD_DIM)
    mixed = low(low_back(mixed))
    branch = low_back(product(mixed, output_w))
    second_in = hidden + RESIDUAL * branch
    h_two = low(row_norm(second_in) * gain_two)
    gate = low_back(product(h_two, gate_w))
    up_val = low_back(product(h_two, up_w))
    act = low(jax.nn.silu(gate) * up_val)
    feed = low_back(product(act, down_w))
    return second_in + RESIDUAL * feed

def reference(hidden_in, cotangent, block_start, query_weight, key_weight, value_weight, output_weight, gate_weight, up_weight, down_weight, first_gain, second_gain):
    weights = tuple((item.astype(jnp.float32) for item in (query_weight, key_weight, value_weight, output_weight, gate_weight, up_weight, down_weight, first_gain, second_gain)))
    row_ids = jnp.arange(GROUP_TOK, dtype=jnp.int32)
    segments = jnp.where(row_ids < PROMPT, 0, 1 + (row_ids - PROMPT) // CONT).astype(jnp.int32)
    inputs = hidden_in.astype(jnp.float32).reshape(N_GRP, GROUP_TOK, D)
    cotangents = cotangent.astype(jnp.float32).reshape(N_GRP, GROUP_TOK, D)
    positions = (block_start[:, :, None] + jnp.arange(BLOCK, dtype=jnp.int32)[None, None, :]).reshape(N_GRP, GROUP_TOK).astype(jnp.int32)

    def one_group(totals, item):
        hidden, grad_out, group_pos = item
        cosine, sine = rope_tables(group_pos, HEAD_DIM)

        def forward(values_in, params):
            return layer_forward(values_in, params, cosine, sine, group_pos, segments)
        result, pull = jax.vjp(forward, hidden, weights)
        grad_in, grad_params = pull(grad_out)
        totals = tuple((total + grad for total, grad in zip(totals, grad_params)))
        return (totals, (result.astype(jnp.bfloat16), grad_in))
    start = tuple((jnp.zeros_like(item) for item in weights))
    totals, (outputs, input_grads) = lax.scan(one_group, start, (inputs, cotangents, positions))
    return (outputs.reshape(TOKENS, D), input_grads.reshape(TOKENS, D), totals[0], totals[1], totals[2], totals[3], totals[4], totals[5], totals[6], totals[7], totals[8])
```

```python
import functools
import math

import jax
import jax.numpy as jnp
from jax import lax
from jax.experimental import pallas as pl
from jax.experimental.pallas import tpu as pltpu
from jax.sharding import PartitionSpec as P

HEAD_DIM = 64
BLOCK = 128
PROMPT = 1024
CONT = 256


EPS = 1e-05
RESIDUAL = 1.4 / math.sqrt(40.0)
NEGATIVE = -1e30
GROUP_HEADS = 4

ALL = ("grp", "tok", "fs")
LAYER = ("grp", "fs")
PIECE = 64
TILE = 256
PAIR = 2 * HEAD_DIM
SLAB = 3 * PAIR
BF = jnp.bfloat16
F32 = jnp.float32


def turn(field):
    lane = lax.broadcasted_iota(jnp.int32, field.shape, 1)
    return jnp.where(
        lane % HEAD_DIM < HEAD_DIM // 2,
        pltpu.roll(field, PAIR - HEAD_DIM // 2, 1),
        pltpu.roll(field, HEAD_DIM // 2, 1),
    )


def table_row(piece):
    prompt_pieces = PROMPT // PIECE
    cont_pieces = CONT // PIECE
    return jnp.where(
        piece < prompt_pieces,
        piece,
        prompt_pieces + lax.rem(jnp.maximum(piece - prompt_pieces, 0), cont_pieces),
    )


def head_tiles(index_ref, total, run_tile):
    pair = pl.program_id(0)
    side = index_ref[total // PIECE]
    own = pair < 2
    prompt_tiles = PROMPT // TILE
    for tile in range(prompt_tiles):
        mine = side == (0 if tile % 4 in (0, 3) else 1)
        for head in range(2):
            keep = own if head else jnp.logical_or(own, mine)

            @pl.when(keep)
            def _(tile=tile, head=head):
                run_tile(tile * TILE, tile * TILE, head)

    later = (total - PROMPT) // TILE

    def body(step, carry):
        mine = (step * 2 >= later).astype(jnp.int32) == side
        for head in range(2):
            keep = own if head else jnp.logical_or(own, mine)

            @pl.when(keep)
            def _(head=head):
                run_tile(pl.multiple_of(PROMPT + step * TILE, TILE), PROMPT, head)

        return carry

    lax.fori_loop(0, later, body, 0)


def lanes_of(head, shape):
    lane = lax.broadcasted_iota(jnp.int32, shape, 1)
    return lane < HEAD_DIM if head == 0 else lane >= HEAD_DIM


def nt_dot(left, right):
    return lax.dot_general(left, right, (((1,), (1,)), ((), ())), preferred_element_type=F32)


def tn_dot(left, right):
    return lax.dot_general(left, right, (((0,), (0,)), ((), ())), preferred_element_type=F32)


def nn_dot(left, right):
    return lax.dot_general(left, right, (((1,), (0,)), ((), ())), preferred_element_type=F32)


def attend_kernel(index_ref, raw_ref, cos_ref, sin_ref, out_ref, kept_ref, mixed):
    total = out_ref.shape[0]
    pieces = total // PIECE
    pair = pl.program_id(0)

    def rope(field, row):
        cosine = cos_ref[pl.ds(row, PIECE), :]
        sine = sin_ref[pl.ds(row, PIECE), :]
        return field * cosine + turn(field) * sine

    @pl.when(pair < 2)
    def _():
        def body(piece, carry):
            source = pl.multiple_of(index_ref[piece], PIECE)
            row = pl.multiple_of(table_row(piece) * PIECE, PIECE)
            target = pl.ds(pl.multiple_of(piece * PIECE, PIECE), PIECE)
            query = rope(raw_ref[pl.ds(source, PIECE), 0:PAIR], row)
            key = rope(raw_ref[pl.ds(source, PIECE), PAIR : 2 * PAIR], row)
            value = raw_ref[pl.ds(source, PIECE), 2 * PAIR : 3 * PAIR]
            kept_ref[0, target, 0:PAIR] = query.astype(BF)
            kept_ref[0, target, PAIR : 2 * PAIR] = key.astype(BF)
            kept_ref[0, target, 2 * PAIR : 3 * PAIR] = value.astype(BF)
            return carry

        lax.fori_loop(0, pieces, body, 0)

    @pl.when(pair == 2)
    def _():
        def body(piece, carry):
            source = pl.multiple_of(index_ref[piece], PIECE)
            row = pl.multiple_of(table_row(piece) * PIECE, PIECE)
            target = pl.ds(pl.multiple_of(piece * PIECE, PIECE), PIECE)
            both = rope(raw_ref[pl.ds(source, PIECE), 0:PAIR], row)
            value = raw_ref[pl.ds(source, PIECE), PAIR : 2 * PAIR]
            low = lanes_of(0, both.shape)
            kept_ref[0, target, 0:PAIR] = jnp.where(low, both, 0.0).astype(BF)
            kept_ref[0, target, PAIR : 2 * PAIR] = jnp.where(
                low, pltpu.roll(both, HEAD_DIM, 1), 0.0
            ).astype(BF)
            kept_ref[0, target, 2 * PAIR : 3 * PAIR] = jnp.where(low, value, 0.0).astype(BF)
            return carry

        lax.fori_loop(0, pieces, body, 0)

    mixed[...] = jnp.zeros_like(mixed)
    scale = 1.0 / math.sqrt(HEAD_DIM)

    def run_tile(start, prefix, head):
        rows = pl.ds(start, TILE)
        query = kept_ref[0, rows, 0:PAIR]
        mask = lanes_of(head, query.shape)
        query = jnp.where(mask, query.astype(F32) * scale, 0.0).astype(BF)
        seen = lax.broadcasted_iota(jnp.int32, (TILE, TILE), 1) <= lax.broadcasted_iota(
            jnp.int32, (TILE, TILE), 0
        )
        near = jnp.where(seen, nt_dot(query, kept_ref[0, rows, PAIR : 2 * PAIR]), NEGATIVE)
        peak = jnp.max(near, axis=1, keepdims=True)
        if prefix:
            far = nt_dot(query, kept_ref[0, 0:prefix, PAIR : 2 * PAIR])
            peak = jnp.maximum(peak, jnp.max(far, axis=1, keepdims=True))
        near = jnp.exp(near - peak)
        count = jnp.sum(near, axis=1, keepdims=True)
        out = nn_dot(near.astype(BF), kept_ref[0, rows, 2 * PAIR : 3 * PAIR])
        if prefix:
            far = jnp.exp(far - peak)
            count = count + jnp.sum(far, axis=1, keepdims=True)
            out = out + nn_dot(far.astype(BF), kept_ref[0, 0:prefix, 2 * PAIR : 3 * PAIR])
        mixed[rows, :] = jnp.where(mask, out / count, mixed[rows, :])

    head_tiles(index_ref, total, run_tile)

    def back(piece, carry):
        source = pl.multiple_of(index_ref[piece], PIECE)
        target = pl.ds(pl.multiple_of(piece * PIECE, PIECE), PIECE)
        out_ref[pl.ds(source, PIECE), :] = mixed[target, :].astype(BF)
        return carry

    lax.fori_loop(0, pieces, back, 0)


def attend(index, raw, cosine, sine):
    total = raw.shape[0]
    return pl.pallas_call(
        attend_kernel,
        grid_spec=pltpu.PrefetchScalarGridSpec(
            num_scalar_prefetch=1,
            grid=(3,),
            in_specs=[
                pl.BlockSpec((total, SLAB), lambda j, index: (0, j)),
                pl.BlockSpec(cosine.shape, lambda j, index: (0, 0)),
                pl.BlockSpec(sine.shape, lambda j, index: (0, 0)),
            ],
            out_specs=[
                pl.BlockSpec((total, PAIR), lambda j, index: (0, j)),
                pl.BlockSpec((1, total, SLAB), lambda j, index: (j, 0, 0)),
            ],
            scratch_shapes=[pltpu.VMEM((total, PAIR), F32)],
        ),
        out_shape=[
            jax.ShapeDtypeStruct((total, 3 * PAIR), BF),
            jax.ShapeDtypeStruct((3, total, SLAB), BF),
        ],
        compiler_params=pltpu.CompilerParams(vmem_limit_bytes=40 << 20),
        cost_estimate=pl.CostEstimate(
            flops=10 * 2 * 7680 * 256 * 128, bytes_accessed=20 << 20, transcendentals=9 << 20
        ),
        name="attend",
    )(index, raw, cosine, sine)


def attend_back_kernel(
    index_ref, kept_ref, outer_ref, cos_ref, sin_ref, grad_ref, outer, grad_q, grad_k, grad_v
):
    total = outer.shape[0]
    pieces = total // PIECE
    pair = pl.program_id(0)

    def sort(piece, carry):
        source = pl.multiple_of(index_ref[piece], PIECE)
        target = pl.ds(pl.multiple_of(piece * PIECE, PIECE), PIECE)
        outer[target, :] = outer_ref[pl.ds(source, PIECE), :]
        return carry

    lax.fori_loop(0, pieces, sort, 0)
    grad_q[...] = jnp.zeros_like(grad_q)
    grad_k[...] = jnp.zeros_like(grad_k)
    grad_v[...] = jnp.zeros_like(grad_v)
    scale = 1.0 / math.sqrt(HEAD_DIM)

    def run_tile(start, prefix, head):
        rows = pl.ds(start, TILE)
        query = kept_ref[0, rows, 0:PAIR]
        mask = lanes_of(head, query.shape)
        query = jnp.where(mask, query.astype(F32) * scale, 0.0).astype(BF)
        away = jnp.where(mask, outer[rows, :].astype(F32), 0.0).astype(BF)
        seen = lax.broadcasted_iota(jnp.int32, (TILE, TILE), 0) <= lax.broadcasted_iota(
            jnp.int32, (TILE, TILE), 1
        )
        near_key = kept_ref[0, rows, PAIR : 2 * PAIR]
        near = jnp.where(seen, nt_dot(near_key, query), NEGATIVE)
        peak = jnp.max(near, axis=0, keepdims=True)
        if prefix:
            far_key = kept_ref[0, 0:prefix, PAIR : 2 * PAIR]
            far = nt_dot(far_key, query)
            peak = jnp.maximum(peak, jnp.max(far, axis=0, keepdims=True))
        near = jnp.exp(near - peak)
        count = jnp.sum(near, axis=0, keepdims=True)
        if prefix:
            far = jnp.exp(far - peak)
            count = count + jnp.sum(far, axis=0, keepdims=True)
        inverse = 1.0 / count
        near = near * inverse
        near_pull = nt_dot(kept_ref[0, rows, 2 * PAIR : 3 * PAIR], away)
        delta = jnp.sum(near * near_pull, axis=0, keepdims=True)
        if prefix:
            far = far * inverse
            far_pull = nt_dot(kept_ref[0, 0:prefix, 2 * PAIR : 3 * PAIR], away)
            delta = delta + jnp.sum(far * far_pull, axis=0, keepdims=True)
        grad_v[rows, :] += nn_dot(near.astype(BF), away)
        near = (near * (near_pull - delta)).astype(BF)
        grad_k[rows, :] += nn_dot(near, query)
        part = tn_dot(near, near_key)
        if prefix:
            grad_v[0:prefix, :] += nn_dot(far.astype(BF), away)
            far = (far * (far_pull - delta)).astype(BF)
            grad_k[0:prefix, :] += nn_dot(far, query)
            part = part + tn_dot(far, far_key)
        grad_q[rows, :] = jnp.where(mask, part * scale, grad_q[rows, :])

    head_tiles(index_ref, total, run_tile)

    def unrope(field, row):
        cosine = cos_ref[pl.ds(row, PIECE), :]
        sine = sin_ref[pl.ds(row, PIECE), :]
        return field * cosine - turn(field) * sine

    @pl.when(pair < 2)
    def _():
        def back(piece, carry):
            source = pl.ds(pl.multiple_of(index_ref[piece], PIECE), PIECE)
            row = pl.multiple_of(table_row(piece) * PIECE, PIECE)
            here = pl.ds(pl.multiple_of(piece * PIECE, PIECE), PIECE)
            grad_ref[source, 0:PAIR] = unrope(grad_q[here, :], row).astype(BF)
            grad_ref[source, PAIR : 2 * PAIR] = unrope(grad_k[here, :], row).astype(BF)
            grad_ref[source, 2 * PAIR : 3 * PAIR] = grad_v[here, :].astype(BF)
            return carry

        lax.fori_loop(0, pieces, back, 0)

    @pl.when(pair == 2)
    def _():
        def back(piece, carry):
            source = pl.ds(pl.multiple_of(index_ref[piece], PIECE), PIECE)
            row = pl.multiple_of(table_row(piece) * PIECE, PIECE)
            here = pl.ds(pl.multiple_of(piece * PIECE, PIECE), PIECE)
            low = lanes_of(0, (PIECE, PAIR))
            both = jnp.where(low, grad_q[here, :], pltpu.roll(grad_k[here, :], HEAD_DIM, 1))
            grad_ref[source, 0:PAIR] = unrope(both, row).astype(BF)
            grad_ref[source, PAIR : 2 * PAIR] = grad_v[here, :].astype(BF)
            grad_ref[source, 2 * PAIR : 3 * PAIR] = jnp.zeros((PIECE, PAIR), BF)
            return carry

        lax.fori_loop(0, pieces, back, 0)


def attend_back(index, kept, outer, cosine, sine, columns):
    total = outer.shape[0]
    return pl.pallas_call(
        attend_back_kernel,
        grid_spec=pltpu.PrefetchScalarGridSpec(
            num_scalar_prefetch=1,
            grid=(3,),
            in_specs=[
                pl.BlockSpec((1, total, SLAB), lambda j, index: (j, 0, 0)),
                pl.BlockSpec((total, PAIR), lambda j, index: (0, j)),
                pl.BlockSpec(cosine.shape, lambda j, index: (0, 0)),
                pl.BlockSpec(sine.shape, lambda j, index: (0, 0)),
            ],
            out_specs=pl.BlockSpec((total, SLAB), lambda j, index: (0, j)),
            scratch_shapes=[
                pltpu.VMEM((total, PAIR), BF),
                pltpu.VMEM((total, PAIR), F32),
                pltpu.VMEM((total, PAIR), F32),
                pltpu.VMEM((total, PAIR), F32),
            ],
        ),
        out_shape=jax.ShapeDtypeStruct((total, columns), BF),
        compiler_params=pltpu.CompilerParams(vmem_limit_bytes=48 << 20),
        cost_estimate=pl.CostEstimate(
            flops=25 * 2 * 7680 * 256 * 128, bytes_accessed=20 << 20, transcendentals=9 << 20
        ),
        name="attend_back",
    )(index, kept, outer, cosine, sine)


def make_layered(mesh):
    n_grp, n_tok, n_fs = (mesh.shape[axis] for axis in ALL)

    def device(grp, tok, fs):
        return (grp * n_tok + tok) * n_fs + fs

    def permutation(move):
        return [
            (device(g, t, f), device(*move(g, t, f)))
            for g in range(n_grp)
            for t in range(n_tok)
            for f in range(n_fs)
        ]

    def send(array, move):
        return lax.ppermute(array, ALL, permutation(move))

    def cross(step):
        return lambda g, t, f: (g ^ step, t, f)

    def sibling(g, t, f):
        return (g, t, 1 - f)

    def local(
        hidden_in,
        cotangent,
        block_start,
        query_weight,
        key_weight,
        value_weight,
        output_weight,
        gate_weight,
        up_weight,
        down_weight,
        first_gain,
        second_gain,
    ):
        rows, width = hidden_in.shape
        ff_width = gate_weight.shape[1]
        g, t, f = (lax.axis_index(axis) for axis in ALL)
        even = f == 0
        ranks = n_grp * n_fs
        total = rows * ranks
        quarter = rows // n_grp


        def shuffle_in(array):
            parts = array.reshape(n_grp, quarter, width)
            result = jnp.zeros_like(parts)
            for turn_by in range(n_grp):
                piece = lax.dynamic_index_in_dim(parts, g ^ t ^ turn_by, 0, keepdims=True)
                piece = send(piece, lambda g, t, f: (g ^ t ^ turn_by, g, f))
                result = lax.dynamic_update_slice_in_dim(result, piece, g ^ t ^ turn_by, 0)
            return result.reshape(rows, width)

        def shuffle_out(array):
            parts = array.reshape(n_tok, quarter, width)
            result = jnp.zeros_like(parts)
            for turn_by in range(n_grp):
                piece = lax.dynamic_index_in_dim(parts, g ^ t ^ turn_by, 0, keepdims=True)
                piece = send(piece, lambda g, t, f: (t, g ^ t ^ turn_by, f))
                result = lax.dynamic_update_slice_in_dim(result, piece, g ^ t ^ turn_by, 0)
            return result.reshape(rows, width)


        def layer_gather(array):
            half = array.shape[0] // 2
            by_x = send(array, cross(1))
            by_y = send(array, cross(2))
            by_xy = jnp.concatenate(
                [send(by_x[:half], cross(2)), send(by_y[half:], cross(1))], axis=0
            )
            mine = [array, by_x, by_y, by_xy]
            return jnp.concatenate(mine + [send(part, sibling) for part in mine], axis=0)

        def layer_sum(array):
            half = array.shape[0] // 2
            both = array[:half].astype(F32) + send(array[half:], sibling).astype(F32)
            parts = both.astype(BF).reshape(n_grp, rows, array.shape[1])
            return both[:rows] + sum(
                send(parts[step], cross(step)).astype(F32) for step in range(1, n_grp)
            )

        xs = shuffle_in(hidden_in)
        gain_one = lax.all_gather(first_gain, ("tok", "fs"), axis=0, tiled=True).astype(F32)
        gain_two = lax.all_gather(second_gain, ("tok", "fs"), axis=0, tiled=True).astype(F32)


        head_span = width // n_grp
        own_span = 4 * HEAD_DIM

        def rank_columns(side):
            picked = [
                lax.dynamic_slice_in_dim(weight, g * head_span, head_span, 1)
                for weight in (query_weight, key_weight, value_weight)
            ]
            first = side * (own_span + HEAD_DIM)
            spans = [(first, PAIR), (first + PAIR, PAIR), (own_span, HEAD_DIM)]
            return jnp.concatenate(
                [weight[:, at : at + size] for at, size in spans for weight in picked], axis=1
            )

        def pair_rows(zero_block, one_block):
            mine = jnp.where(even, zero_block, one_block)
            other = send(jnp.where(even, one_block, zero_block), sibling)
            return jnp.concatenate(
                [jnp.where(even, mine, other), jnp.where(even, other, mine)], axis=0
            )

        qkv_weight = lax.all_gather(
            pair_rows(rank_columns(0), rank_columns(1)), "tok", axis=0, tiled=True
        )
        out_rows = output_weight.shape[0] // n_grp
        out_weight = lax.all_gather(
            lax.dynamic_slice_in_dim(output_weight, g * out_rows, out_rows, 0),
            "tok",
            axis=0,
            tiled=True,
        )
        out_weight = lax.all_to_all(out_weight, "grp", 0, 0, tiled=True)
        half_head = HEAD_DIM // 2
        swapped = send(
            jnp.where(even, out_weight[own_span:], out_weight[:half_head]), sibling
        )
        out_weight = jnp.concatenate(
            [
                jnp.where(even, out_weight[:own_span], out_weight[half_head:]),
                jnp.where(even, out_weight[own_span:], swapped),
                jnp.where(even, swapped, out_weight[:half_head]),
                jnp.zeros((HEAD_DIM, width), BF),
            ],
            axis=0,
        )

        ff_piece = ff_width // (ranks * n_tok)

        def ff_columns(weight, side):
            return jnp.concatenate(
                [
                    lax.dynamic_slice_in_dim(
                        weight, (step * n_fs + side) * n_grp * ff_piece + g * ff_piece, ff_piece, 1
                    )
                    for step in range(n_tok)
                ],
                axis=1,
            )

        def ff_weight(weight):
            return lax.all_gather(
                pair_rows(ff_columns(weight, 0), ff_columns(weight, 1)), "tok", axis=0, tiled=True
            )

        gate_w = ff_weight(gate_weight)
        up_w = ff_weight(up_weight)
        down_w = lax.all_gather(
            lax.dynamic_slice_in_dim(down_weight, g * ff_piece, ff_piece, 0),
            "tok",
            axis=0,
            tiled=True,
        )


        starts = lax.dynamic_index_in_dim(
            lax.all_gather(block_start, "grp", axis=0, tiled=True), t, 0, keepdims=False
        )
        number = jnp.arange(total // BLOCK, dtype=jnp.int32)
        prompt_blocks = PROMPT // BLOCK
        cont_blocks = CONT // BLOCK
        place = jnp.where(
            number < prompt_blocks,
            starts // BLOCK,
            prompt_blocks
            + (number - prompt_blocks) // cont_blocks * cont_blocks
            + (starts - PROMPT) // BLOCK,
        )
        order = jnp.sum(
            jnp.where(place[None, :] == number[:, None], number[None, :], 0), axis=1
        )
        pieces = (
            order[:, None] * (BLOCK // PIECE) + jnp.arange(BLOCK // PIECE, dtype=jnp.int32)
        ).reshape(-1)
        from_t = pieces // ranks
        from_f = pieces // n_grp % n_fs
        from_g = pieces % n_grp
        index = jnp.concatenate(
            [
                (((from_f ^ f) * n_grp + (from_g ^ g)) * n_tok + from_t) * PIECE,
                f[None].astype(jnp.int32),
            ]
        ).astype(jnp.int32)
        lane = jnp.arange(PAIR, dtype=jnp.int32)
        half_head_lane = lane % (HEAD_DIM // 2)
        freq = 10000.0 ** (-(half_head_lane.astype(F32) * 2.0) / HEAD_DIM)
        angle = jnp.arange(PROMPT + CONT, dtype=F32)[:, None] * freq[None, :]
        cosine = jnp.cos(angle)
        sine = jnp.where(lane[None, :] % HEAD_DIM < HEAD_DIM // 2, -jnp.sin(angle), jnp.sin(angle))


        hidden = xs.astype(F32)
        scale_one = lax.rsqrt(jnp.mean(hidden * hidden, axis=1, keepdims=True) + EPS)
        normed_one = hidden * scale_one
        h_one = layer_gather((normed_one * gain_one[None, :]).astype(BF))
        raw = jnp.dot(h_one, qkv_weight, preferred_element_type=F32)
        attn_out, kept = attend(index, raw, cosine, sine)
        branch = layer_sum(jnp.dot(attn_out, out_weight, preferred_element_type=F32).astype(BF))
        second_in = hidden + RESIDUAL * branch
        scale_two = lax.rsqrt(jnp.mean(second_in * second_in, axis=1, keepdims=True) + EPS)
        normed_two = second_in * scale_two
        h_two = layer_gather((normed_two * gain_two[None, :]).astype(BF))
        gate = jnp.dot(h_two, gate_w, preferred_element_type=F32)
        up_val = jnp.dot(h_two, up_w, preferred_element_type=F32)
        sigma = jax.nn.sigmoid(gate)
        silu = gate * sigma
        act = (silu * up_val).astype(BF)
        feed = layer_sum(jnp.dot(act, down_w, preferred_element_type=F32).astype(BF))
        layer_output = shuffle_out((second_in + RESIDUAL * feed).astype(BF))


        grad_out = shuffle_in(cotangent).astype(F32)
        grad_m = layer_gather((RESIDUAL * grad_out).astype(BF))
        grad_act = nt_dot(grad_m, down_w)
        down_grad = lax.psum_scatter(
            tn_dot(act, grad_m).astype(BF).reshape(n_tok, ff_piece, width),
            "tok",
            scatter_dimension=0,
            tiled=True,
        )[0]
        down_grad = send(
            down_grad, lambda g, t, f: (t, (n_grp * f + g) // n_fs, (n_grp * f + g) % n_fs)
        ).astype(F32)
        grad_gate = (grad_act * up_val * (sigma * (1.0 + gate * (1.0 - sigma)))).astype(BF)
        grad_up = (grad_act * silu).astype(BF)

        def to_rows(grad):
            columns = grad.shape[1]
            grad = grad.astype(BF).reshape(n_grp, n_tok, width // (n_grp * n_tok), columns)
            grad = grad.transpose(1, 0, 2, 3).reshape(n_tok, width // n_tok, columns)
            grad = lax.psum_scatter(grad, "tok", scatter_dimension=0, tiled=True)
            grad = grad.reshape(ranks, width // (ranks * n_tok), columns)
            return lax.all_to_all(grad, LAYER, 0, 0, tiled=True)

        def ff_grad(grad):
            got = to_rows(grad).reshape(n_grp, n_fs, -1, n_tok, ff_piece)
            return got.transpose(2, 3, 1, 0, 4).reshape(-1, ff_width).astype(F32)

        gate_grad = ff_grad(tn_dot(h_two, grad_gate))
        up_grad = ff_grad(tn_dot(h_two, grad_up))
        grad_h2 = layer_sum((nt_dot(grad_gate, gate_w) + nt_dot(grad_up, up_w)).astype(BF))
        gain_two_sum = jnp.sum(grad_h2 * normed_two, axis=0)
        pulled = grad_h2 * gain_two[None, :]
        grad_second = (
            grad_out
            + scale_two * pulled
            - scale_two**3 * second_in * jnp.mean(pulled * second_in, axis=1, keepdims=True)
        )
        grad_z = layer_gather((RESIDUAL * grad_second).astype(BF))
        grad_attn = nt_dot(grad_z, out_weight).astype(BF)
        out_full = tn_dot(attn_out, grad_z)
        shared = out_full[own_span : own_span + HEAD_DIM]
        got = send(
            jnp.where(even, shared[half_head:], shared[:half_head]).astype(BF), sibling
        ).astype(F32)
        kept_half = jnp.where(even, shared[:half_head], shared[half_head:]) + got
        out_full = jnp.where(
            even,
            jnp.concatenate([out_full[:own_span], kept_half], axis=0),
            jnp.concatenate([kept_half, out_full[:own_span]], axis=0),
        )
        output_grad = lax.psum_scatter(
            out_full.astype(BF).reshape(n_tok, -1, width), "tok", scatter_dimension=0, tiled=True
        )[0]
        output_grad = send(
            output_grad, lambda g, t, f: (g, (n_tok * f + t) // n_fs, (n_tok * f + t) % n_fs)
        ).astype(F32)

        grads = attend_back(index, kept, grad_attn, cosine, sine, qkv_weight.shape[1])
        grad_h1 = layer_sum(nt_dot(grads, qkv_weight).astype(BF))
        gain_one_sum = jnp.sum(grad_h1 * normed_one, axis=0)
        pulled = grad_h1 * gain_one[None, :]
        input_grad = (
            grad_second
            + scale_one * pulled
            - scale_one**3 * hidden * jnp.mean(pulled * hidden, axis=1, keepdims=True)
        )
        input_grad = shuffle_out(input_grad.astype(BF)).astype(F32)
        got = to_rows(tn_dot(h_one, grads)).astype(F32)
        own_rows = got.shape[1]
        got = got.reshape(n_grp, n_fs, own_rows, got.shape[2])

        def projection_grad(which):
            def own(side):
                return [
                    got[:, side, :, SLAB * pair + PAIR * which : SLAB * pair + PAIR * (which + 1)]
                    for pair in range(2)
                ]

            at = 2 * SLAB + HEAD_DIM * which
            shared = got[:, 0, :, at : at + HEAD_DIM] + got[:, 1, :, at : at + HEAD_DIM]
            whole = jnp.concatenate(own(0) + [shared] + own(1), axis=2)
            return whole.transpose(1, 0, 2).reshape(own_rows, width)

        gains = jnp.stack([gain_one_sum, gain_two_sum], axis=1).reshape(
            n_grp * n_tok * n_fs, -1
        )
        gains = jnp.sum(lax.all_to_all(gains, ALL, 0, 0, tiled=True), axis=0).reshape(-1, 2)
        return (
            layer_output,
            input_grad,
            projection_grad(0),
            projection_grad(1),
            projection_grad(2),
            output_grad,
            gate_grad,
            up_grad,
            down_grad,
            gains[:, 0],
            gains[:, 1],
        )

    return local


def spread(block, axis, source):
    block = jnp.where(lax.axis_index(axis) == source, block, jnp.zeros_like(block))
    return lax.psum(block, axis)


def rope_tables(positions, head_size):
    half = head_size // 2
    freq = 10000.0 ** (-(jnp.arange(half, dtype=jnp.float32) * 2.0) / head_size)
    angle = positions.astype(jnp.float32)[:, None] * freq[None, :]
    return (jnp.cos(angle)[:, None, :], jnp.sin(angle)[:, None, :])


def rotate(field, cosine, sine):
    half = field.shape[-1] // 2
    first = field[..., :half]
    second = field[..., half:]
    return jnp.concatenate(
        [first * cosine - second * sine, second * cosine + first * sine], axis=-1
    )


def unrotate(grad, cosine, sine):
    half = grad.shape[-1] // 2
    first = grad[..., :half]
    second = grad[..., half:]
    return jnp.concatenate(
        [first * cosine + second * sine, second * cosine - first * sine], axis=-1
    )


def row_norm(values):
    return values * lax.rsqrt(jnp.mean(values * values, axis=-1, keepdims=True) + EPS)


def swish_product(gate, up_val):
    return jax.nn.silu(gate) * up_val


def contract_rows(left, right):
    return lax.dot_general(
        left, right, (((0,), (0,)), ((), ())), preferred_element_type=jnp.float32
    )


def contract_cols(left, right):
    return lax.dot_general(
        left, right, (((1,), (1,)), ((), ())), preferred_element_type=jnp.float32
    )


def weight_sums(left, right):
    return lax.psum_scatter(
        contract_rows(left, right), ("grp", "tok", "fs"), scatter_dimension=0, tiled=True
    )


def spread_local(
    hidden_in,
    cotangent,
    block_start,
    query_weight,
    key_weight,
    value_weight,
    output_weight,
    gate_weight,
    up_weight,
    down_weight,
    first_gain,
    second_gain,
):
    local_rows, width = hidden_in.shape
    ff_width = gate_weight.shape[1]
    head_size = HEAD_DIM
    heads = width // head_size
    group_width = GROUP_HEADS * head_size
    group_count = heads // GROUP_HEADS
    scale = 1.0 / math.sqrt(head_size)
    device = lax.axis_index(("tok", "fs"))
    holders = -(-PROMPT // local_rows)
    prompt_rows = holders * local_rows
    starts = block_start[0]
    offsets = jnp.arange(BLOCK, dtype=jnp.int32)
    local_starts = lax.dynamic_slice_in_dim(
        starts, device * (local_rows // BLOCK), local_rows // BLOCK
    )
    my_pos = (local_starts[:, None] + offsets[None, :]).reshape(local_rows)
    prompt_pos = (starts[: prompt_rows // BLOCK][:, None] + offsets[None, :]).reshape(prompt_rows)
    my_row = device * local_rows + jnp.arange(local_rows, dtype=jnp.int32)
    my_seg = jnp.where(my_row < PROMPT, 0, 1 + (my_row - PROMPT) // CONT)
    prompt_row = jnp.arange(prompt_rows, dtype=jnp.int32)
    prompt_seen = (prompt_row[None, :] < PROMPT) & (prompt_pos[None, :] <= my_pos[:, None])
    local_seen = (
        (my_seg[None, :] == my_seg[:, None])
        & (my_seg[None, :] > 0)
        & (my_pos[None, :] <= my_pos[:, None])
    )
    visible = jnp.concatenate([prompt_seen, local_seen], axis=1)
    cosine, sine = rope_tables(my_pos, head_size)
    hidden = hidden_in.astype(jnp.float32)
    normed_one, pull_one = jax.vjp(row_norm, hidden)
    zero_rows = jnp.zeros((local_rows, width), jnp.float32)
    pieces = (
        lax.all_gather(query_weight, ("tok", "fs"), axis=0, tiled=True),
        lax.all_gather(key_weight, ("tok", "fs"), axis=0, tiled=True),
        lax.all_gather(value_weight, ("tok", "fs"), axis=0, tiled=True),
        lax.all_gather(first_gain, ("tok", "fs"), axis=0, tiled=True),
    )
    normed = normed_one
    scaled = (normed * pieces[3].astype(jnp.float32)[None, :]).astype(jnp.bfloat16)
    kept = scaled
    query_acc = jnp.dot(scaled, pieces[0], preferred_element_type=jnp.float32)
    key_acc = jnp.dot(scaled, pieces[1], preferred_element_type=jnp.float32)
    value_acc = jnp.dot(scaled, pieces[2], preferred_element_type=jnp.float32)
    kept_one = kept
    queries = (
        rotate(query_acc.reshape(local_rows, heads, head_size), cosine, sine)
        .astype(jnp.bfloat16)
        .reshape(local_rows, width)
    )
    keys = (
        rotate(key_acc.reshape(local_rows, heads, head_size), cosine, sine)
        .astype(jnp.bfloat16)
        .reshape(local_rows, width)
    )
    values = value_acc.astype(jnp.bfloat16)
    paired = jnp.stack([keys, values])
    received = []
    for root in range(holders):
        received.append(spread(paired, ("tok", "fs"), root))
    gathered = jnp.concatenate(received, axis=1)
    all_keys = jnp.concatenate([gathered[0], keys], axis=0)
    all_values = jnp.concatenate([gathered[1], values], axis=0)
    total_keys = all_keys.shape[0]

    def head_slice(array, index):
        return lax.dynamic_slice_in_dim(array, index * group_width, group_width, 1).reshape(
            array.shape[0], GROUP_HEADS, head_size
        )

    def scores_of(index):
        raw = (
            jnp.einsum(
                "qhd,khd->hqk",
                head_slice(queries, index),
                head_slice(all_keys, index),
                preferred_element_type=jnp.float32,
            )
            * scale
        )
        return jnp.where(visible[None], raw, NEGATIVE)

    def attend_group(index, carry):
        mixed, peaks, totals = carry
        scores = scores_of(index)
        peak = jnp.max(scores, axis=-1, keepdims=True)
        expo = jnp.exp(scores - peak)
        total = jnp.sum(expo, axis=-1, keepdims=True)
        probs = (expo / total).astype(jnp.bfloat16)
        block_out = jnp.einsum(
            "hqk,khd->qhd", probs, head_slice(all_values, index), preferred_element_type=jnp.float32
        ).reshape(local_rows, group_width)
        mixed = lax.dynamic_update_slice_in_dim(mixed, block_out, index * group_width, 1)
        peaks = lax.dynamic_update_slice_in_dim(peaks, peak[None, :, :, 0], index, 0)
        totals = lax.dynamic_update_slice_in_dim(totals, total[None, :, :, 0], index, 0)
        return (mixed, peaks, totals)

    stats_zero = jnp.zeros((group_count, GROUP_HEADS, local_rows), jnp.float32)
    mixed, peaks, totals = lax.fori_loop(
        0, group_count, attend_group, (zero_rows, stats_zero, stats_zero)
    )
    attention_out = mixed.astype(jnp.bfloat16)
    branch = jnp.dot(
        attention_out,
        lax.all_gather(output_weight, ("tok", "fs"), axis=0, tiled=True),
        preferred_element_type=jnp.float32,
    )
    second_in = hidden + RESIDUAL * branch
    normed_two, pull_two = jax.vjp(row_norm, second_in)
    retained = ()
    pieces = (
        lax.all_gather(gate_weight, ("tok", "fs"), axis=0, tiled=True),
        lax.all_gather(up_weight, ("tok", "fs"), axis=0, tiled=True),
        lax.all_gather(second_gain, ("tok", "fs"), axis=0, tiled=True),
    )
    start = jnp.int32(0)
    stored = retained
    normed = normed_two
    scaled = (normed * pieces[2].astype(jnp.float32)[None, :]).astype(jnp.bfloat16)
    kept = scaled
    stored = tuple(
        (
            lax.dynamic_update_slice_in_dim(buffer, piece, start, 0)
            for buffer, piece in zip(stored, pieces)
        )
    )
    gate_acc, up_acc, kept_two, stored = (
        jnp.dot(scaled, pieces[0], preferred_element_type=jnp.float32),
        jnp.dot(scaled, pieces[1], preferred_element_type=jnp.float32),
        kept,
        stored,
    )
    swish, pull_swish = jax.vjp(swish_product, gate_acc, up_acc)
    act = swish.astype(jnp.bfloat16)
    down_store = ()
    piece = lax.all_gather(down_weight, ("tok", "fs"), axis=0, tiled=True)
    start = jnp.int32(0)
    stored_down = down_store
    total_acc = jnp.dot(act, piece, preferred_element_type=jnp.float32)
    stored_down = tuple(
        (lax.dynamic_update_slice_in_dim(buffer, piece, start, 0) for buffer in stored_down)
    )
    feed, stored_down = (total_acc, stored_down)
    layer_output = (second_in + RESIDUAL * feed).astype(jnp.bfloat16)
    grad_out = cotangent.astype(jnp.float32)
    grad_m = (RESIDUAL * grad_out).astype(jnp.bfloat16)
    grad_act = contract_cols(grad_m, lax.all_gather(down_weight, ("tok", "fs"), axis=0, tiled=True))
    down_grad = weight_sums(act, grad_m)
    grad_gate_f, grad_up_f = pull_swish(grad_act)
    grad_gate = grad_gate_f.astype(jnp.bfloat16)
    grad_up = grad_up_f.astype(jnp.bfloat16)
    pieces = (
        lax.all_gather(gate_weight, ("tok", "fs"), axis=0, tiled=True),
        lax.all_gather(up_weight, ("tok", "fs"), axis=0, tiled=True),
        lax.all_gather(second_gain, ("tok", "fs"), axis=0, tiled=True),
    )
    section = contract_cols(grad_gate, pieces[0]) + contract_cols(grad_up, pieces[1])
    normed = normed_two
    grad_normed = section * pieces[2].astype(jnp.float32)[None, :]
    gain_sum = jnp.sum(section * normed, axis=0)
    grad_n2 = grad_normed
    gain_two = gain_sum
    both_grads = jnp.concatenate([grad_gate, grad_up], axis=1)
    mixer_grad = weight_sums(kept_two, both_grads)
    grad_second = grad_out + pull_two(grad_n2)[0]
    grad_z = (RESIDUAL * grad_second).astype(jnp.bfloat16)
    output_full = contract_rows(attention_out, grad_z)
    grad_attn = contract_cols(
        grad_z, lax.all_gather(output_weight, ("tok", "fs"), axis=0, tiled=True)
    ).astype(jnp.bfloat16)

    def attend_back(index, carry):
        grad_q, grad_k, grad_v = carry
        query_g = head_slice(queries, index)
        key_g = head_slice(all_keys, index)
        value_g = head_slice(all_values, index)
        outer_g = head_slice(grad_attn, index)
        scores = scores_of(index)
        peak = lax.dynamic_index_in_dim(peaks, index, 0, keepdims=False)[:, :, None]
        total = lax.dynamic_index_in_dim(totals, index, 0, keepdims=False)[:, :, None]
        probs = jnp.exp(scores - peak) / total
        grad_probs = jnp.einsum(
            "qhd,khd->hqk", outer_g, value_g, preferred_element_type=jnp.float32
        )
        grad_scores = (
            probs * (grad_probs - jnp.sum(grad_probs * probs, axis=-1, keepdims=True))
        ).astype(jnp.bfloat16)
        query_part = (
            jnp.einsum("hqk,khd->qhd", grad_scores, key_g, preferred_element_type=jnp.float32)
            * scale
        )
        key_part = (
            jnp.einsum("hqk,qhd->khd", grad_scores, query_g, preferred_element_type=jnp.float32)
            * scale
        )
        value_part = jnp.einsum(
            "hqk,qhd->khd", probs.astype(jnp.bfloat16), outer_g, preferred_element_type=jnp.float32
        )
        grad_q = lax.dynamic_update_slice_in_dim(
            grad_q, query_part.reshape(local_rows, group_width), index * group_width, 1
        )
        grad_k = lax.dynamic_update_slice_in_dim(
            grad_k, key_part.reshape(total_keys, group_width), index * group_width, 1
        )
        grad_v = lax.dynamic_update_slice_in_dim(
            grad_v, value_part.reshape(total_keys, group_width), index * group_width, 1
        )
        return (grad_q, grad_k, grad_v)

    zero_keys = jnp.zeros((total_keys, width), jnp.float32)
    grad_q, grad_k, grad_v = lax.fori_loop(
        0, group_count, attend_back, (zero_rows, zero_keys, zero_keys)
    )
    share_k, share_v = (
        lax.psum_scatter(
            grad_k[:prompt_rows].astype(jnp.bfloat16),
            ("tok", "fs"),
            scatter_dimension=1,
            tiled=True,
        ).astype(jnp.float32),
        lax.psum_scatter(
            grad_v[:prompt_rows].astype(jnp.bfloat16),
            ("tok", "fs"),
            scatter_dimension=1,
            tiled=True,
        ).astype(jnp.float32),
    )
    prompt_dk, prompt_dv = (
        lax.all_gather(share_k.astype(jnp.bfloat16), ("tok", "fs"), axis=1, tiled=True).astype(
            share_k.dtype
        ),
        lax.all_gather(share_v.astype(jnp.bfloat16), ("tok", "fs"), axis=1, tiled=True).astype(
            share_v.dtype
        ),
    )
    holder = jnp.minimum(device, holders - 1)
    owned = device < holders
    mine_k = (
        jnp.where(
            owned, lax.dynamic_slice_in_dim(prompt_dk, holder * local_rows, local_rows, 0), 0.0
        )
        + grad_k[prompt_rows:]
    )
    mine_v = (
        jnp.where(
            owned, lax.dynamic_slice_in_dim(prompt_dv, holder * local_rows, local_rows, 0), 0.0
        )
        + grad_v[prompt_rows:]
    )
    grad_qraw = (
        unrotate(grad_q.reshape(local_rows, heads, head_size), cosine, sine)
        .reshape(local_rows, width)
        .astype(jnp.bfloat16)
    )
    grad_kraw = (
        unrotate(mine_k.reshape(local_rows, heads, head_size), cosine, sine)
        .reshape(local_rows, width)
        .astype(jnp.bfloat16)
    )
    grad_vraw = mine_v.astype(jnp.bfloat16)
    pieces = (
        lax.all_gather(query_weight, ("tok", "fs"), axis=0, tiled=True),
        lax.all_gather(key_weight, ("tok", "fs"), axis=0, tiled=True),
        lax.all_gather(value_weight, ("tok", "fs"), axis=0, tiled=True),
        lax.all_gather(first_gain, ("tok", "fs"), axis=0, tiled=True),
    )
    section = (
        contract_cols(grad_qraw, pieces[0])
        + contract_cols(grad_kraw, pieces[1])
        + contract_cols(grad_vraw, pieces[2])
    )
    normed = normed_one
    grad_normed = section * pieces[3].astype(jnp.float32)[None, :]
    gain_sum = jnp.sum(section * normed, axis=0)
    three_grads = jnp.concatenate([grad_qraw, grad_kraw, grad_vraw], axis=1)
    attention_grad = weight_sums(kept_one, three_grads)
    input_grad = grad_second + pull_one(grad_normed)[0]
    output_grad, first_gain_grad, second_gain_grad = (
        lax.psum_scatter(output_full, ("grp", "tok", "fs"), scatter_dimension=0, tiled=True),
        lax.psum_scatter(gain_sum, ("grp", "tok", "fs"), scatter_dimension=0, tiled=True),
        lax.psum_scatter(gain_two, ("grp", "tok", "fs"), scatter_dimension=0, tiled=True),
    )
    return (
        layer_output,
        input_grad,
        attention_grad[:, :width],
        attention_grad[:, width : 2 * width],
        attention_grad[:, 2 * width :],
        output_grad,
        mixer_grad[:, :ff_width],
        mixer_grad[:, ff_width:],
        down_grad,
        first_gain_grad,
        second_gain_grad,
    )


def solution(mesh):
    layered = mesh.shape["grp"] == mesh.shape["tok"] == 4 and mesh.shape["fs"] == 2
    return jax.shard_map(
        make_layered(mesh) if layered else spread_local,
        mesh=mesh,
        in_specs=(
            P(("grp", "tok", "fs"), None),
            P(("grp", "tok", "fs"), None),
            P("grp", None),
            P(("tok", "fs"), None),
            P(("tok", "fs"), None),
            P(("tok", "fs"), None),
            P(("tok", "fs"), None),
            P(("tok", "fs"), None),
            P(("tok", "fs"), None),
            P(("tok", "fs"), None),
            P(("tok", "fs")),
            P(("tok", "fs")),
        ),
        out_specs=(
            P(("grp", "tok", "fs"), None),
            P(("grp", "tok", "fs"), None),
            P(("grp", "tok", "fs"), None),
            P(("grp", "tok", "fs"), None),
            P(("grp", "tok", "fs"), None),
            P(("grp", "tok", "fs"), None),
            P(("grp", "tok", "fs"), None),
            P(("grp", "tok", "fs"), None),
            P(("grp", "tok", "fs"), None),
            P(("grp", "tok", "fs")),
            P(("grp", "tok", "fs")),
        ),
        check_vma=False,
    )
```

```python
import functools
import math

import jax
import jax.numpy as jnp
from jax import lax
from jax.experimental import pallas as pl
from jax.experimental.pallas import tpu as pltpu
from jax.sharding import PartitionSpec as P

HEAD_DIM = 64
BLOCK = 128
PROMPT = 1024
CONT = 256


EPS = 1e-05
RESIDUAL = 1.4 / math.sqrt(40.0)
NEGATIVE = -1e30
GROUP_HEADS = 4

ALL = ("grp", "tok", "fs")
LAYER = ("grp", "fs")
PIECE = 64
TILE = 256
PAIR = 2 * HEAD_DIM
SLAB = 3 * PAIR
BF = jnp.bfloat16
F32 = jnp.float32


def turn(field):
    lane = lax.broadcasted_iota(jnp.int32, field.shape, 1)
    return jnp.where(
        lane % HEAD_DIM < HEAD_DIM // 2,
        pltpu.roll(field, PAIR - HEAD_DIM // 2, 1),
        pltpu.roll(field, HEAD_DIM // 2, 1),
    )


def table_row(piece):
    prompt_pieces = PROMPT // PIECE
    cont_pieces = CONT // PIECE
    return jnp.where(
        piece < prompt_pieces,
        piece,
        prompt_pieces + lax.rem(jnp.maximum(piece - prompt_pieces, 0), cont_pieces),
    )


def head_tiles(pair, index_ref, total, run_tile):
    side = index_ref[total // PIECE]
    own = pair < 2
    prompt_tiles = PROMPT // TILE
    for tile in range(prompt_tiles):
        mine = side == (0 if tile % 4 in (0, 3) else 1)
        for head in range(2):
            keep = own if head else jnp.logical_or(own, mine)

            @pl.when(keep)
            def _(tile=tile, head=head):
                run_tile(tile * TILE, tile * TILE, head)

    later = (total - PROMPT) // TILE

    def body(step, carry):
        mine = (step * 2 >= later).astype(jnp.int32) == side
        for head in range(2):
            keep = own if head else jnp.logical_or(own, mine)

            @pl.when(keep)
            def _(head=head):
                run_tile(pl.multiple_of(PROMPT + step * TILE, TILE), PROMPT, head)

        return carry

    lax.fori_loop(0, later, body, 0)


def lanes_of(head, shape):
    lane = lax.broadcasted_iota(jnp.int32, shape, 1)
    return lane < HEAD_DIM if head == 0 else lane >= HEAD_DIM


def nt_dot(left, right):
    return lax.dot_general(left, right, (((1,), (1,)), ((), ())), preferred_element_type=F32)


def tn_dot(left, right):
    return lax.dot_general(left, right, (((0,), (0,)), ((), ())), preferred_element_type=F32)


def nn_dot(left, right):
    return lax.dot_general(left, right, (((1,), (0,)), ((), ())), preferred_element_type=F32)


def attend_kernel(index_ref, raw_ref, cos_ref, sin_ref, out_ref, kept_ref, mixed):
    total = out_ref.shape[0]
    pieces = total // PIECE
    pair = pl.program_id(0)

    def rope(field, row):
        cosine = cos_ref[pl.ds(row, PIECE), :]
        sine = sin_ref[pl.ds(row, PIECE), :]
        return field * cosine + turn(field) * sine

    @pl.when(pair < 2)
    def _():
        def body(piece, carry):
            source = pl.multiple_of(index_ref[piece], PIECE)
            row = pl.multiple_of(table_row(piece) * PIECE, PIECE)
            target = pl.ds(pl.multiple_of(piece * PIECE, PIECE), PIECE)
            query = rope(raw_ref[pl.ds(source, PIECE), 0:PAIR], row)
            key = rope(raw_ref[pl.ds(source, PIECE), PAIR : 2 * PAIR], row)
            value = raw_ref[pl.ds(source, PIECE), 2 * PAIR : 3 * PAIR]
            kept_ref[0, target, 0:PAIR] = query.astype(BF)
            kept_ref[0, target, PAIR : 2 * PAIR] = key.astype(BF)
            kept_ref[0, target, 2 * PAIR : 3 * PAIR] = value.astype(BF)
            return carry

        lax.fori_loop(0, pieces, body, 0)

    @pl.when(pair == 2)
    def _():
        def body(piece, carry):
            source = pl.multiple_of(index_ref[piece], PIECE)
            row = pl.multiple_of(table_row(piece) * PIECE, PIECE)
            target = pl.ds(pl.multiple_of(piece * PIECE, PIECE), PIECE)
            both = rope(raw_ref[pl.ds(source, PIECE), 0:PAIR], row)
            value = raw_ref[pl.ds(source, PIECE), PAIR : 2 * PAIR]
            low = lanes_of(0, both.shape)
            kept_ref[0, target, 0:PAIR] = jnp.where(low, both, 0.0).astype(BF)
            kept_ref[0, target, PAIR : 2 * PAIR] = jnp.where(
                low, pltpu.roll(both, HEAD_DIM, 1), 0.0
            ).astype(BF)
            kept_ref[0, target, 2 * PAIR : 3 * PAIR] = jnp.where(low, value, 0.0).astype(BF)
            return carry

        lax.fori_loop(0, pieces, body, 0)

    mixed[...] = jnp.zeros_like(mixed)
    scale = 1.0 / math.sqrt(HEAD_DIM)

    def run_tile(start, prefix, head):
        rows = pl.ds(start, TILE)
        query = kept_ref[0, rows, 0:PAIR]
        mask = lanes_of(head, query.shape)
        query = jnp.where(mask, query.astype(F32) * scale, 0.0).astype(BF)
        seen = lax.broadcasted_iota(jnp.int32, (TILE, TILE), 1) <= lax.broadcasted_iota(
            jnp.int32, (TILE, TILE), 0
        )
        near = jnp.where(seen, nt_dot(query, kept_ref[0, rows, PAIR : 2 * PAIR]), NEGATIVE)
        peak = jnp.max(near, axis=1, keepdims=True)
        if prefix:
            far = nt_dot(query, kept_ref[0, 0:prefix, PAIR : 2 * PAIR])
            peak = jnp.maximum(peak, jnp.max(far, axis=1, keepdims=True))
        near = jnp.exp(near - peak)
        count = jnp.sum(near, axis=1, keepdims=True)
        out = nn_dot(near.astype(BF), kept_ref[0, rows, 2 * PAIR : 3 * PAIR])
        if prefix:
            far = jnp.exp(far - peak)
            count = count + jnp.sum(far, axis=1, keepdims=True)
            out = out + nn_dot(far.astype(BF), kept_ref[0, 0:prefix, 2 * PAIR : 3 * PAIR])
        mixed[rows, :] = jnp.where(mask, out / count, mixed[rows, :])

    head_tiles(pair, index_ref, total, run_tile)

    def back(piece, carry):
        source = pl.multiple_of(index_ref[piece], PIECE)
        target = pl.ds(pl.multiple_of(piece * PIECE, PIECE), PIECE)
        out_ref[pl.ds(source, PIECE), :] = mixed[target, :].astype(BF)
        return carry

    lax.fori_loop(0, pieces, back, 0)


def attend(index, raw, cosine, sine):
    total = raw.shape[0]
    return pl.pallas_call(
        attend_kernel,
        grid_spec=pltpu.PrefetchScalarGridSpec(
            num_scalar_prefetch=1,
            grid=(3,),
            in_specs=[
                pl.BlockSpec((total, SLAB), lambda j, index: (0, j)),
                pl.BlockSpec(cosine.shape, lambda j, index: (0, 0)),
                pl.BlockSpec(sine.shape, lambda j, index: (0, 0)),
            ],
            out_specs=[
                pl.BlockSpec((total, PAIR), lambda j, index: (0, j)),
                pl.BlockSpec((1, total, SLAB), lambda j, index: (j, 0, 0)),
            ],
            scratch_shapes=[pltpu.VMEM((total, PAIR), F32)],
        ),
        out_shape=[
            jax.ShapeDtypeStruct((total, 3 * PAIR), BF),
            jax.ShapeDtypeStruct((3, total, SLAB), BF),
        ],
        compiler_params=pltpu.CompilerParams(vmem_limit_bytes=40 << 20),
        cost_estimate=pl.CostEstimate(
            flops=0, bytes_accessed=1 << 20, transcendentals=0
        ),
        name="attend",
    )(index, raw, cosine, sine)


def attend_back_kernel(
    first, index_ref, kept_ref, outer_ref, cos_ref, sin_ref, grad_ref, outer, grad_q, grad_k, grad_v
):
    total = outer.shape[0]
    pieces = total // PIECE
    pair = pl.program_id(0) + first

    def sort(piece, carry):
        source = pl.multiple_of(index_ref[piece], PIECE)
        target = pl.ds(pl.multiple_of(piece * PIECE, PIECE), PIECE)
        outer[target, :] = outer_ref[pl.ds(source, PIECE), :]
        return carry

    lax.fori_loop(0, pieces, sort, 0)
    grad_q[...] = jnp.zeros_like(grad_q)
    grad_k[...] = jnp.zeros_like(grad_k)
    grad_v[...] = jnp.zeros_like(grad_v)
    scale = 1.0 / math.sqrt(HEAD_DIM)

    def run_tile(start, prefix, head):
        rows = pl.ds(start, TILE)
        query = kept_ref[0, rows, 0:PAIR]
        mask = lanes_of(head, query.shape)
        query = jnp.where(mask, query.astype(F32) * scale, 0.0).astype(BF)
        away = jnp.where(mask, outer[rows, :].astype(F32), 0.0).astype(BF)
        seen = lax.broadcasted_iota(jnp.int32, (TILE, TILE), 0) <= lax.broadcasted_iota(
            jnp.int32, (TILE, TILE), 1
        )
        near_key = kept_ref[0, rows, PAIR : 2 * PAIR]
        near = jnp.where(seen, nt_dot(near_key, query), NEGATIVE)
        peak = jnp.max(near, axis=0, keepdims=True)
        if prefix:
            far_key = kept_ref[0, 0:prefix, PAIR : 2 * PAIR]
            far = nt_dot(far_key, query)
            peak = jnp.maximum(peak, jnp.max(far, axis=0, keepdims=True))
        near = jnp.exp(near - peak)
        count = jnp.sum(near, axis=0, keepdims=True)
        if prefix:
            far = jnp.exp(far - peak)
            count = count + jnp.sum(far, axis=0, keepdims=True)
        inverse = 1.0 / count
        near = near * inverse
        near_pull = nt_dot(kept_ref[0, rows, 2 * PAIR : 3 * PAIR], away)
        delta = jnp.sum(near * near_pull, axis=0, keepdims=True)
        if prefix:
            far = far * inverse
            far_pull = nt_dot(kept_ref[0, 0:prefix, 2 * PAIR : 3 * PAIR], away)
            delta = delta + jnp.sum(far * far_pull, axis=0, keepdims=True)
        grad_v[rows, :] += nn_dot(near.astype(BF), away)
        near = (near * (near_pull - delta)).astype(BF)
        grad_k[rows, :] += nn_dot(near, query)
        part = tn_dot(near, near_key)
        if prefix:
            grad_v[0:prefix, :] += nn_dot(far.astype(BF), away)
            far = (far * (far_pull - delta)).astype(BF)
            grad_k[0:prefix, :] += nn_dot(far, query)
            part = part + tn_dot(far, far_key)
        grad_q[rows, :] = jnp.where(mask, part * scale, grad_q[rows, :])

    head_tiles(pair, index_ref, total, run_tile)

    def unrope(field, row):
        cosine = cos_ref[pl.ds(row, PIECE), :]
        sine = sin_ref[pl.ds(row, PIECE), :]
        return field * cosine - turn(field) * sine

    @pl.when(pair < 2)
    def _():
        def back(piece, carry):
            source = pl.ds(pl.multiple_of(index_ref[piece], PIECE), PIECE)
            row = pl.multiple_of(table_row(piece) * PIECE, PIECE)
            here = pl.ds(pl.multiple_of(piece * PIECE, PIECE), PIECE)
            grad_ref[source, 0:PAIR] = unrope(grad_q[here, :], row).astype(BF)
            grad_ref[source, PAIR : 2 * PAIR] = unrope(grad_k[here, :], row).astype(BF)
            grad_ref[source, 2 * PAIR : 3 * PAIR] = grad_v[here, :].astype(BF)
            return carry

        lax.fori_loop(0, pieces, back, 0)

    @pl.when(pair == 2)
    def _():
        def back(piece, carry):
            source = pl.ds(pl.multiple_of(index_ref[piece], PIECE), PIECE)
            row = pl.multiple_of(table_row(piece) * PIECE, PIECE)
            here = pl.ds(pl.multiple_of(piece * PIECE, PIECE), PIECE)
            low = lanes_of(0, (PIECE, PAIR))
            both = jnp.where(low, grad_q[here, :], pltpu.roll(grad_k[here, :], HEAD_DIM, 1))
            grad_ref[source, 0:PAIR] = unrope(both, row).astype(BF)
            grad_ref[source, PAIR : 2 * PAIR] = grad_v[here, :].astype(BF)
            grad_ref[source, 2 * PAIR : 3 * PAIR] = jnp.zeros((PIECE, PAIR), BF)
            return carry

        lax.fori_loop(0, pieces, back, 0)


def attend_back(first, count, index, kept, outer, cosine, sine, columns):
    total = outer.shape[0]
    return pl.pallas_call(
        functools.partial(attend_back_kernel, first),
        grid_spec=pltpu.PrefetchScalarGridSpec(
            num_scalar_prefetch=1,
            grid=(count,),
            in_specs=[
                pl.BlockSpec((1, total, SLAB), lambda j, index: (j + first, 0, 0)),
                pl.BlockSpec((total, PAIR), lambda j, index: (0, j + first)),
                pl.BlockSpec(cosine.shape, lambda j, index: (0, 0)),
                pl.BlockSpec(sine.shape, lambda j, index: (0, 0)),
            ],
            out_specs=pl.BlockSpec((total, SLAB), lambda j, index: (0, j)),
            scratch_shapes=[
                pltpu.VMEM((total, PAIR), BF),
                pltpu.VMEM((total, PAIR), F32),
                pltpu.VMEM((total, PAIR), F32),
                pltpu.VMEM((total, PAIR), F32),
            ],
        ),
        out_shape=jax.ShapeDtypeStruct((total, columns), BF),
        compiler_params=pltpu.CompilerParams(vmem_limit_bytes=48 << 20),
        cost_estimate=pl.CostEstimate(
            flops=0, bytes_accessed=1 << 20, transcendentals=0
        ),
        name="attend_back",
    )(index, kept, outer, cosine, sine)


def after(array, *earlier):
    leaves = [array] + jax.tree.leaves(earlier)
    place = pl.BlockSpec(memory_space=pl.ANY)
    return pl.pallas_call(
        lambda *refs: None,
        in_specs=[place] * len(leaves),
        out_specs=place,
        out_shape=jax.ShapeDtypeStruct(array.shape, array.dtype),
        input_output_aliases={0: 0},
        name="after",
    )(*leaves)


def make_layered(mesh):
    n_grp, n_tok, n_fs = (mesh.shape[axis] for axis in ALL)

    def device(grp, tok, fs):
        return (grp * n_tok + tok) * n_fs + fs

    def permutation(move):
        return [
            (device(g, t, f), device(*move(g, t, f)))
            for g in range(n_grp)
            for t in range(n_tok)
            for f in range(n_fs)
        ]

    def send(array, move):
        return lax.ppermute(array, ALL, permutation(move))

    def cross(step):
        return lambda g, t, f: (g ^ step, t, f)

    def sibling(g, t, f):
        return (g, t, 1 - f)

    def local(
        hidden_in,
        cotangent,
        block_start,
        query_weight,
        key_weight,
        value_weight,
        output_weight,
        gate_weight,
        up_weight,
        down_weight,
        first_gain,
        second_gain,
    ):
        rows, width = hidden_in.shape
        ff_width = gate_weight.shape[1]
        g, t, f = (lax.axis_index(axis) for axis in ALL)
        even = f == 0
        ranks = n_grp * n_fs
        total = rows * ranks
        quarter = rows // n_grp


        def spread_in(array):
            return lax.all_to_all(array.reshape(n_grp, quarter, width), "grp", 0, 0, tiled=True)

        def shuffle_in(parts):
            return lax.all_to_all(parts, "tok", 0, 0, tiled=True).reshape(rows, width)

        def shuffle_out(*arrays):
            parts = [array.reshape(n_tok, quarter, width) for array in arrays]
            results = [jnp.zeros_like(part) for part in parts]
            for turn_by in range(n_grp):
                away = g ^ t ^ turn_by
                pieces = [lax.dynamic_index_in_dim(part, away, 0, keepdims=True) for part in parts]
                piece = send(
                    jnp.concatenate(pieces, axis=1),
                    lambda g, t, f, turn_by=turn_by: (t, g ^ t ^ turn_by, f),
                )
                for i, result in enumerate(results):
                    results[i] = lax.dynamic_update_slice_in_dim(
                        result, piece[:, i * quarter : (i + 1) * quarter], away, 0
                    )
            return [result.reshape(rows, width) for result in results]


        def layer_pieces(array):
            half = array.shape[0] // 2
            by_x = send(array, cross(1))
            by_y = send(array, cross(2))
            return array, by_x, by_y, send(by_x[:half], cross(2)), send(by_y[half:], cross(1))

        def layer_join(array, by_x, by_y, *by_xy):
            mine = [array, by_x, by_y, jnp.concatenate(by_xy, axis=0)]
            return jnp.concatenate(mine + [send(part, sibling) for part in mine], axis=0)

        def layer_gather(array):
            return layer_join(*layer_pieces(array))

        def pair_sum(rows_of):
            away = send(rows_of(1).astype(BF), sibling)
            here = rows_of(0)
            away = away.reshape(n_grp, rows, -1)
            here = here.reshape(n_grp, rows, -1)
            parts = [(here[step] + away[step].astype(F32)).astype(BF) for step in (3, 1, 2)]
            return here[0], away[0], parts

        def layer_send(sums, *earlier):
            here, away, parts = sums
            if earlier:
                parts = [after(part, *earlier) for part in parts]
            return here, away, [send(part, cross(step)) for part, step in zip(parts, (3, 1, 2))]

        def layer_add(parts, beside=None):
            here, away, got = parts
            if beside is not None:
                got = [after(part, beside) for part in got]
            return here + away.astype(F32) + sum(part.astype(F32) for part in got)

        def layer_sum(rows_of, beside=None):
            return layer_add(layer_send(pair_sum(rows_of)), beside)

        def halves(*arrays):
            half = arrays[0].shape[0] // 2
            return lambda which: [array[which * half : (which + 1) * half] for array in arrays]

        extra = 8
        gains_here = jnp.concatenate([first_gain, second_gain])
        span = gains_here.shape[0]
        gains_here = jnp.pad(gains_here[None, :], ((0, extra - 1), (0, width - span)))
        hidden_parts = spread_in(hidden_in)
        cotangent_parts = spread_in(after(cotangent, hidden_parts))
        arrived = lax.all_to_all(
            jnp.concatenate(
                [hidden_parts, jnp.broadcast_to(gains_here[None], (n_tok, extra, width))], axis=1
            ),
            "tok",
            0,
            0,
            tiled=True,
        )
        gains_mine = arrived[:, quarter, :span]
        gains_other = send(gains_mine, sibling)
        gains_all = jnp.stack(
            [jnp.where(even, gains_mine, gains_other), jnp.where(even, gains_other, gains_mine)],
            axis=1,
        ).astype(F32).reshape(n_tok * n_fs, 2, -1)
        gain_one = gains_all[:, 0].reshape(width)
        gain_two = gains_all[:, 1].reshape(width)
        starts = send(block_start, lambda g, t, f: (t, g, f))[0]
        xs = arrived[:, :quarter].reshape(rows, width)
        cotangent_here = shuffle_in(after(cotangent_parts, xs))


        head_span = width // n_grp
        own_span = 4 * HEAD_DIM

        def rank_columns(side):
            picked = [
                lax.dynamic_slice_in_dim(weight, g * head_span, head_span, 1)
                for weight in (query_weight, key_weight, value_weight)
            ]
            first = side * (own_span + HEAD_DIM)
            spans = [(first, PAIR), (first + PAIR, PAIR), (own_span, HEAD_DIM)]
            return jnp.concatenate(
                [weight[:, at : at + size] for at, size in spans for weight in picked], axis=1
            )

        def pair_rows(zero_block, one_block):
            mine = jnp.where(even, zero_block, one_block)
            other = send(jnp.where(even, one_block, zero_block), sibling)
            return jnp.concatenate(
                [jnp.where(even, mine, other), jnp.where(even, other, mine)], axis=0
            )

        def gather_rows(array, *earlier):
            array = after(array, *earlier)
            return array, lax.all_gather(array, "tok", axis=0, tiled=True)

        turn_one, qkv_weight = gather_rows(
            pair_rows(rank_columns(0), rank_columns(1)), xs
        )
        ff_piece = ff_width // (ranks * n_tok)
        ff_tall = -(-ff_piece // 64) * 64
        ff_wide = ff_tall * n_tok

        def ff_columns(side):
            parts = [
                lax.dynamic_slice_in_dim(
                    weight, (step * n_fs + side) * n_grp * ff_piece + g * ff_piece, ff_piece, 1
                )
                for weight in (gate_weight, up_weight)
                for step in range(n_tok)
            ]
            zeros = jnp.zeros((gate_weight.shape[0], ff_tall - ff_piece), BF)
            return jnp.concatenate([item for part in parts for item in (part, zeros)], axis=1)

        ff_inputs = (
            pair_rows(ff_columns(0), ff_columns(1)),
            jnp.pad(
                lax.dynamic_slice_in_dim(down_weight, g * ff_piece, ff_piece, 0),
                ((0, ff_tall - ff_piece), (0, 0)),
            ),
        )

        hidden = after(xs, *ff_inputs).astype(F32)
        scale_one = lax.rsqrt(jnp.mean(hidden * hidden, axis=1, keepdims=True) + EPS)
        normed_one = hidden * scale_one
        h_one = layer_gather((normed_one * gain_one[None, :]).astype(BF))
        out_rows = output_weight.shape[0] // n_grp
        turn_two, out_weight = gather_rows(
            lax.dynamic_slice_in_dim(output_weight, g * out_rows, out_rows, 0), turn_one, h_one
        )
        grad_out = cotangent_here.astype(F32)
        grad_m_pieces = layer_pieces(after((RESIDUAL * grad_out).astype(BF), h_one))
        grad_m = layer_join(*grad_m_pieces)
        raw = nn_dot(after(h_one, *grad_m_pieces[1:3]), qkv_weight)
        out_weight = lax.all_to_all(after(out_weight, raw), "grp", 0, 0, tiled=True)
        half_head = HEAD_DIM // 2
        swapped = send(
            jnp.where(even, out_weight[own_span:], out_weight[:half_head]), sibling
        )
        out_weight = jnp.concatenate(
            [
                jnp.where(even, out_weight[:own_span], out_weight[half_head:]),
                jnp.where(even, out_weight[own_span:], swapped),
                jnp.where(even, swapped, out_weight[:half_head]),
                jnp.zeros((HEAD_DIM, width), BF),
            ],
            axis=0,
        )

        _, ff_weight = gather_rows(ff_inputs[0], turn_two)
        _, down_w = gather_rows(ff_inputs[1], ff_inputs[0], turn_two)


        number = jnp.arange(total // BLOCK, dtype=jnp.int32)
        prompt_blocks = PROMPT // BLOCK
        cont_blocks = CONT // BLOCK
        place = jnp.where(
            number < prompt_blocks,
            starts // BLOCK,
            prompt_blocks
            + (number - prompt_blocks) // cont_blocks * cont_blocks
            + (starts - PROMPT) // BLOCK,
        )
        order = jnp.sum(
            jnp.where(place[None, :] == number[:, None], number[None, :], 0), axis=1
        )
        pieces = (
            order[:, None] * (BLOCK // PIECE) + jnp.arange(BLOCK // PIECE, dtype=jnp.int32)
        ).reshape(-1)
        from_t = pieces // ranks
        from_f = pieces // n_grp % n_fs
        from_g = pieces % n_grp
        index = jnp.concatenate(
            [
                (((from_f ^ f) * n_grp + (from_g ^ g)) * n_tok + from_t) * PIECE,
                f[None].astype(jnp.int32),
            ]
        ).astype(jnp.int32)
        lane = jnp.arange(PAIR, dtype=jnp.int32)
        half_head_lane = lane % (HEAD_DIM // 2)
        freq = 10000.0 ** (-(half_head_lane.astype(F32) * 2.0) / HEAD_DIM)
        angle = jnp.arange(PROMPT + CONT, dtype=F32)[:, None] * freq[None, :]
        cosine = jnp.cos(angle)
        sine = jnp.where(lane[None, :] % HEAD_DIM < HEAD_DIM // 2, -jnp.sin(angle), jnp.sin(angle))


        attn_out, kept = attend(index, raw, cosine, sine)
        pick = halves(attn_out)
        branch = layer_sum(lambda side, pick=pick: nn_dot(pick(side)[0], out_weight), grad_m)
        second_in = hidden + RESIDUAL * branch
        scale_two = lax.rsqrt(jnp.mean(second_in * second_in, axis=1, keepdims=True) + EPS)
        normed_two = second_in * scale_two
        h_two = layer_gather((normed_two * gain_two[None, :]).astype(BF))
        both = nn_dot(h_two, ff_weight)
        gate = both[:, :ff_wide]
        up_val = both[:, ff_wide:]
        sigma = jax.nn.sigmoid(gate)
        silu = gate * sigma
        act = (silu * up_val).astype(BF)


        down_local = tn_dot(act, grad_m).astype(BF).reshape(n_tok, ff_tall, width)
        grad_act = nt_dot(after(grad_m, down_local), down_w)
        grad_both = jnp.concatenate(
            [
                (grad_act * up_val * (sigma * (1.0 + gate * (1.0 - sigma)))).astype(BF),
                (grad_act * silu).astype(BF),
            ],
            axis=1,
        )
        def spread_rows(grad):
            columns = grad.shape[1]
            grad = grad.astype(BF).reshape(n_grp, n_tok, width // (n_grp * n_tok), columns)
            return grad.transpose(1, 0, 2, 3).reshape(n_tok, width // n_tok, columns)

        def sum_rows(grad):
            grad = lax.psum_scatter(grad, "tok", scatter_dimension=0, tiled=True)
            return grad.reshape(ranks, width // (ranks * n_tok), grad.shape[2])

        def to_owners(grad):
            return lax.all_to_all(grad, LAYER, 0, 0, tiled=True)

        pick = halves(grad_both)
        parts = layer_send(pair_sum(lambda side, pick=pick: nt_dot(pick(side)[0], ff_weight)))
        ff_local = spread_rows(tn_dot(h_two, after(grad_both, parts[0])))
        grad_h2 = layer_add(parts, ff_local)
        down_rows = lax.psum_scatter(down_local, "tok", scatter_dimension=0, tiled=True)
        down_rows = down_rows[0, :ff_piece]
        ff_rows = sum_rows(ff_local)
        gain_two_sum = jnp.sum(grad_h2 * normed_two, axis=0)
        pulled = grad_h2 * gain_two[None, :]
        grad_second = (
            grad_out
            + scale_two * pulled
            - scale_two**3 * second_in * jnp.mean(pulled * second_in, axis=1, keepdims=True)
        )
        grad_z_here = (RESIDUAL * grad_second).astype(BF)
        grad_z = layer_gather(grad_z_here)
        pick = halves(after(act, grad_z_here))
        feed_sums = pair_sum(lambda side, pick=pick: nn_dot(pick(side)[0], down_w))
        grad_attn = nt_dot(grad_z, out_weight).astype(BF)
        feed_parts = layer_send(feed_sums, grad_z)
        out_full = tn_dot(attn_out, grad_z)
        shared = out_full[own_span : own_span + HEAD_DIM]
        swapped = send(
            jnp.where(even, shared[half_head:], shared[:half_head]).astype(BF), sibling
        ).astype(F32)
        kept_half = jnp.where(even, shared[:half_head], shared[half_head:]) + swapped
        out_full = jnp.where(
            even,
            jnp.concatenate([out_full[:own_span], kept_half], axis=0),
            jnp.concatenate([kept_half, out_full[:own_span]], axis=0),
        )
        out_full = out_full.astype(BF).reshape(n_tok, -1, width)
        output_grad = lax.psum_scatter(out_full, "tok", scatter_dimension=0, tiled=True)

        grad_attn = after(grad_attn, out_full, down_rows)
        grads = attend_back(0, 3, index, kept, grad_attn, cosine, sine, qkv_weight.shape[1])
        grads = after(grads, ff_rows)
        qkv_local = spread_rows(tn_dot(h_one, grads))
        qkv_rows = sum_rows(qkv_local)
        got = to_owners(after(ff_rows, grads))
        down_grad = send(
            after(down_rows, grads),
            lambda g, t, f: (t, (n_grp * f + g) // n_fs, (n_grp * f + g) % n_fs),
        )
        pick = halves(after(grads, qkv_local, got, output_grad, down_grad))
        parts = layer_send(pair_sum(lambda side, pick=pick: nt_dot(pick(side)[0], qkv_weight)))
        feed = layer_add(feed_parts, parts[0])
        layer_output = (second_in + RESIDUAL * feed).astype(BF)
        got = after(got, layer_output).reshape(n_grp, n_fs, -1, 2, n_tok, ff_tall)
        gate_grad, up_grad = (
            got[:, :, :, which, :, :ff_piece]
            .transpose(2, 3, 1, 0, 4)
            .reshape(-1, ff_width)
            .astype(F32)
            for which in range(2)
        )
        grad_h1 = layer_add(parts, (gate_grad, up_grad))
        gain_one_sum = jnp.sum(grad_h1 * normed_one, axis=0)
        pulled = grad_h1 * gain_one[None, :]
        input_grad = (
            grad_second
            + scale_one * pulled
            - scale_one**3 * hidden * jnp.mean(pulled * hidden, axis=1, keepdims=True)
        )
        input_grad = after(input_grad.astype(BF), qkv_rows)
        layer_output, input_grad = shuffle_out(layer_output, input_grad)
        input_grad = input_grad.astype(F32)
        output_grad = send(
            output_grad[0], lambda g, t, f: (g, (n_tok * f + t) // n_fs, (n_tok * f + t) % n_fs)
        ).astype(F32)
        got = to_owners(qkv_rows).astype(F32)
        own_rows = got.shape[1]
        got = got.reshape(n_grp, n_fs, own_rows, got.shape[2])

        def projection_grad(which):
            def own(side):
                return [
                    got[:, side, :, SLAB * pair + PAIR * which : SLAB * pair + PAIR * (which + 1)]
                    for pair in range(2)
                ]

            at = 2 * SLAB + HEAD_DIM * which
            shared = got[:, 0, :, at : at + HEAD_DIM] + got[:, 1, :, at : at + HEAD_DIM]
            whole = jnp.concatenate(own(0) + [shared] + own(1), axis=2)
            return whole.transpose(1, 0, 2).reshape(own_rows, width)

        gains = jnp.stack([gain_one_sum, gain_two_sum], axis=1).reshape(
            n_grp * n_tok * n_fs, -1
        )
        gains = jnp.sum(lax.all_to_all(gains, ALL, 0, 0, tiled=True), axis=0).reshape(-1, 2)
        return (
            layer_output,
            input_grad,
            projection_grad(0),
            projection_grad(1),
            projection_grad(2),
            output_grad,
            gate_grad,
            up_grad,
            down_grad.astype(F32),
            gains[:, 0],
            gains[:, 1],
        )

    return local


def spread(block, axis, source):
    block = jnp.where(lax.axis_index(axis) == source, block, jnp.zeros_like(block))
    return lax.psum(block, axis)


def rope_tables(positions, head_size):
    half = head_size // 2
    freq = 10000.0 ** (-(jnp.arange(half, dtype=jnp.float32) * 2.0) / head_size)
    angle = positions.astype(jnp.float32)[:, None] * freq[None, :]
    return (jnp.cos(angle)[:, None, :], jnp.sin(angle)[:, None, :])


def rotate(field, cosine, sine):
    half = field.shape[-1] // 2
    first = field[..., :half]
    second = field[..., half:]
    return jnp.concatenate(
        [first * cosine - second * sine, second * cosine + first * sine], axis=-1
    )


def unrotate(grad, cosine, sine):
    half = grad.shape[-1] // 2
    first = grad[..., :half]
    second = grad[..., half:]
    return jnp.concatenate(
        [first * cosine + second * sine, second * cosine - first * sine], axis=-1
    )


def row_norm(values):
    return values * lax.rsqrt(jnp.mean(values * values, axis=-1, keepdims=True) + EPS)


def swish_product(gate, up_val):
    return jax.nn.silu(gate) * up_val


def contract_rows(left, right):
    return lax.dot_general(
        left, right, (((0,), (0,)), ((), ())), preferred_element_type=jnp.float32
    )


def contract_cols(left, right):
    return lax.dot_general(
        left, right, (((1,), (1,)), ((), ())), preferred_element_type=jnp.float32
    )


def weight_sums(left, right):
    return lax.psum_scatter(
        contract_rows(left, right), ("grp", "tok", "fs"), scatter_dimension=0, tiled=True
    )


def spread_local(
    hidden_in,
    cotangent,
    block_start,
    query_weight,
    key_weight,
    value_weight,
    output_weight,
    gate_weight,
    up_weight,
    down_weight,
    first_gain,
    second_gain,
):
    local_rows, width = hidden_in.shape
    ff_width = gate_weight.shape[1]
    head_size = HEAD_DIM
    heads = width // head_size
    group_width = GROUP_HEADS * head_size
    group_count = heads // GROUP_HEADS
    scale = 1.0 / math.sqrt(head_size)
    device = lax.axis_index(("tok", "fs"))
    holders = -(-PROMPT // local_rows)
    prompt_rows = holders * local_rows
    starts = block_start[0]
    offsets = jnp.arange(BLOCK, dtype=jnp.int32)
    local_starts = lax.dynamic_slice_in_dim(
        starts, device * (local_rows // BLOCK), local_rows // BLOCK
    )
    my_pos = (local_starts[:, None] + offsets[None, :]).reshape(local_rows)
    prompt_pos = (starts[: prompt_rows // BLOCK][:, None] + offsets[None, :]).reshape(prompt_rows)
    my_row = device * local_rows + jnp.arange(local_rows, dtype=jnp.int32)
    my_seg = jnp.where(my_row < PROMPT, 0, 1 + (my_row - PROMPT) // CONT)
    prompt_row = jnp.arange(prompt_rows, dtype=jnp.int32)
    prompt_seen = (prompt_row[None, :] < PROMPT) & (prompt_pos[None, :] <= my_pos[:, None])
    local_seen = (
        (my_seg[None, :] == my_seg[:, None])
        & (my_seg[None, :] > 0)
        & (my_pos[None, :] <= my_pos[:, None])
    )
    visible = jnp.concatenate([prompt_seen, local_seen], axis=1)
    cosine, sine = rope_tables(my_pos, head_size)
    hidden = hidden_in.astype(jnp.float32)
    normed_one, pull_one = jax.vjp(row_norm, hidden)
    zero_rows = jnp.zeros((local_rows, width), jnp.float32)
    pieces = (
        lax.all_gather(query_weight, ("tok", "fs"), axis=0, tiled=True),
        lax.all_gather(key_weight, ("tok", "fs"), axis=0, tiled=True),
        lax.all_gather(value_weight, ("tok", "fs"), axis=0, tiled=True),
        lax.all_gather(first_gain, ("tok", "fs"), axis=0, tiled=True),
    )
    normed = normed_one
    scaled = (normed * pieces[3].astype(jnp.float32)[None, :]).astype(jnp.bfloat16)
    kept = scaled
    query_acc = jnp.dot(scaled, pieces[0], preferred_element_type=jnp.float32)
    key_acc = jnp.dot(scaled, pieces[1], preferred_element_type=jnp.float32)
    value_acc = jnp.dot(scaled, pieces[2], preferred_element_type=jnp.float32)
    kept_one = kept
    queries = (
        rotate(query_acc.reshape(local_rows, heads, head_size), cosine, sine)
        .astype(jnp.bfloat16)
        .reshape(local_rows, width)
    )
    keys = (
        rotate(key_acc.reshape(local_rows, heads, head_size), cosine, sine)
        .astype(jnp.bfloat16)
        .reshape(local_rows, width)
    )
    values = value_acc.astype(jnp.bfloat16)
    paired = jnp.stack([keys, values])
    received = []
    for root in range(holders):
        received.append(spread(paired, ("tok", "fs"), root))
    gathered = jnp.concatenate(received, axis=1)
    all_keys = jnp.concatenate([gathered[0], keys], axis=0)
    all_values = jnp.concatenate([gathered[1], values], axis=0)
    total_keys = all_keys.shape[0]

    def head_slice(array, index):
        return lax.dynamic_slice_in_dim(array, index * group_width, group_width, 1).reshape(
            array.shape[0], GROUP_HEADS, head_size
        )

    def scores_of(index):
        raw = (
            jnp.einsum(
                "qhd,khd->hqk",
                head_slice(queries, index),
                head_slice(all_keys, index),
                preferred_element_type=jnp.float32,
            )
            * scale
        )
        return jnp.where(visible[None], raw, NEGATIVE)

    def attend_group(index, carry):
        mixed, peaks, totals = carry
        scores = scores_of(index)
        peak = jnp.max(scores, axis=-1, keepdims=True)
        expo = jnp.exp(scores - peak)
        total = jnp.sum(expo, axis=-1, keepdims=True)
        probs = (expo / total).astype(jnp.bfloat16)
        block_out = jnp.einsum(
            "hqk,khd->qhd", probs, head_slice(all_values, index), preferred_element_type=jnp.float32
        ).reshape(local_rows, group_width)
        mixed = lax.dynamic_update_slice_in_dim(mixed, block_out, index * group_width, 1)
        peaks = lax.dynamic_update_slice_in_dim(peaks, peak[None, :, :, 0], index, 0)
        totals = lax.dynamic_update_slice_in_dim(totals, total[None, :, :, 0], index, 0)
        return (mixed, peaks, totals)

    stats_zero = jnp.zeros((group_count, GROUP_HEADS, local_rows), jnp.float32)
    mixed, peaks, totals = lax.fori_loop(
        0, group_count, attend_group, (zero_rows, stats_zero, stats_zero)
    )
    attention_out = mixed.astype(jnp.bfloat16)
    branch = jnp.dot(
        attention_out,
        lax.all_gather(output_weight, ("tok", "fs"), axis=0, tiled=True),
        preferred_element_type=jnp.float32,
    )
    second_in = hidden + RESIDUAL * branch
    normed_two, pull_two = jax.vjp(row_norm, second_in)
    retained = ()
    pieces = (
        lax.all_gather(gate_weight, ("tok", "fs"), axis=0, tiled=True),
        lax.all_gather(up_weight, ("tok", "fs"), axis=0, tiled=True),
        lax.all_gather(second_gain, ("tok", "fs"), axis=0, tiled=True),
    )
    start = jnp.int32(0)
    stored = retained
    normed = normed_two
    scaled = (normed * pieces[2].astype(jnp.float32)[None, :]).astype(jnp.bfloat16)
    kept = scaled
    stored = tuple(
        (
            lax.dynamic_update_slice_in_dim(buffer, piece, start, 0)
            for buffer, piece in zip(stored, pieces)
        )
    )
    gate_acc, up_acc, kept_two, stored = (
        jnp.dot(scaled, pieces[0], preferred_element_type=jnp.float32),
        jnp.dot(scaled, pieces[1], preferred_element_type=jnp.float32),
        kept,
        stored,
    )
    swish, pull_swish = jax.vjp(swish_product, gate_acc, up_acc)
    act = swish.astype(jnp.bfloat16)
    down_store = ()
    piece = lax.all_gather(down_weight, ("tok", "fs"), axis=0, tiled=True)
    start = jnp.int32(0)
    stored_down = down_store
    total_acc = jnp.dot(act, piece, preferred_element_type=jnp.float32)
    stored_down = tuple(
        (lax.dynamic_update_slice_in_dim(buffer, piece, start, 0) for buffer in stored_down)
    )
    feed, stored_down = (total_acc, stored_down)
    layer_output = (second_in + RESIDUAL * feed).astype(jnp.bfloat16)
    grad_out = cotangent.astype(jnp.float32)
    grad_m = (RESIDUAL * grad_out).astype(jnp.bfloat16)
    grad_act = contract_cols(grad_m, lax.all_gather(down_weight, ("tok", "fs"), axis=0, tiled=True))
    down_grad = weight_sums(act, grad_m)
    grad_gate_f, grad_up_f = pull_swish(grad_act)
    grad_gate = grad_gate_f.astype(jnp.bfloat16)
    grad_up = grad_up_f.astype(jnp.bfloat16)
    pieces = (
        lax.all_gather(gate_weight, ("tok", "fs"), axis=0, tiled=True),
        lax.all_gather(up_weight, ("tok", "fs"), axis=0, tiled=True),
        lax.all_gather(second_gain, ("tok", "fs"), axis=0, tiled=True),
    )
    section = contract_cols(grad_gate, pieces[0]) + contract_cols(grad_up, pieces[1])
    normed = normed_two
    grad_normed = section * pieces[2].astype(jnp.float32)[None, :]
    gain_sum = jnp.sum(section * normed, axis=0)
    grad_n2 = grad_normed
    gain_two = gain_sum
    both_grads = jnp.concatenate([grad_gate, grad_up], axis=1)
    mixer_grad = weight_sums(kept_two, both_grads)
    grad_second = grad_out + pull_two(grad_n2)[0]
    grad_z = (RESIDUAL * grad_second).astype(jnp.bfloat16)
    output_full = contract_rows(attention_out, grad_z)
    grad_attn = contract_cols(
        grad_z, lax.all_gather(output_weight, ("tok", "fs"), axis=0, tiled=True)
    ).astype(jnp.bfloat16)

    def attend_back(index, carry):
        grad_q, grad_k, grad_v = carry
        query_g = head_slice(queries, index)
        key_g = head_slice(all_keys, index)
        value_g = head_slice(all_values, index)
        outer_g = head_slice(grad_attn, index)
        scores = scores_of(index)
        peak = lax.dynamic_index_in_dim(peaks, index, 0, keepdims=False)[:, :, None]
        total = lax.dynamic_index_in_dim(totals, index, 0, keepdims=False)[:, :, None]
        probs = jnp.exp(scores - peak) / total
        grad_probs = jnp.einsum(
            "qhd,khd->hqk", outer_g, value_g, preferred_element_type=jnp.float32
        )
        grad_scores = (
            probs * (grad_probs - jnp.sum(grad_probs * probs, axis=-1, keepdims=True))
        ).astype(jnp.bfloat16)
        query_part = (
            jnp.einsum("hqk,khd->qhd", grad_scores, key_g, preferred_element_type=jnp.float32)
            * scale
        )
        key_part = (
            jnp.einsum("hqk,qhd->khd", grad_scores, query_g, preferred_element_type=jnp.float32)
            * scale
        )
        value_part = jnp.einsum(
            "hqk,qhd->khd", probs.astype(jnp.bfloat16), outer_g, preferred_element_type=jnp.float32
        )
        grad_q = lax.dynamic_update_slice_in_dim(
            grad_q, query_part.reshape(local_rows, group_width), index * group_width, 1
        )
        grad_k = lax.dynamic_update_slice_in_dim(
            grad_k, key_part.reshape(total_keys, group_width), index * group_width, 1
        )
        grad_v = lax.dynamic_update_slice_in_dim(
            grad_v, value_part.reshape(total_keys, group_width), index * group_width, 1
        )
        return (grad_q, grad_k, grad_v)

    zero_keys = jnp.zeros((total_keys, width), jnp.float32)
    grad_q, grad_k, grad_v = lax.fori_loop(
        0, group_count, attend_back, (zero_rows, zero_keys, zero_keys)
    )
    share_k, share_v = (
        lax.psum_scatter(
            grad_k[:prompt_rows].astype(jnp.bfloat16),
            ("tok", "fs"),
            scatter_dimension=1,
            tiled=True,
        ).astype(jnp.float32),
        lax.psum_scatter(
            grad_v[:prompt_rows].astype(jnp.bfloat16),
            ("tok", "fs"),
            scatter_dimension=1,
            tiled=True,
        ).astype(jnp.float32),
    )
    prompt_dk, prompt_dv = (
        lax.all_gather(share_k.astype(jnp.bfloat16), ("tok", "fs"), axis=1, tiled=True).astype(
            share_k.dtype
        ),
        lax.all_gather(share_v.astype(jnp.bfloat16), ("tok", "fs"), axis=1, tiled=True).astype(
            share_v.dtype
        ),
    )
    holder = jnp.minimum(device, holders - 1)
    owned = device < holders
    mine_k = (
        jnp.where(
            owned, lax.dynamic_slice_in_dim(prompt_dk, holder * local_rows, local_rows, 0), 0.0
        )
        + grad_k[prompt_rows:]
    )
    mine_v = (
        jnp.where(
            owned, lax.dynamic_slice_in_dim(prompt_dv, holder * local_rows, local_rows, 0), 0.0
        )
        + grad_v[prompt_rows:]
    )
    grad_qraw = (
        unrotate(grad_q.reshape(local_rows, heads, head_size), cosine, sine)
        .reshape(local_rows, width)
        .astype(jnp.bfloat16)
    )
    grad_kraw = (
        unrotate(mine_k.reshape(local_rows, heads, head_size), cosine, sine)
        .reshape(local_rows, width)
        .astype(jnp.bfloat16)
    )
    grad_vraw = mine_v.astype(jnp.bfloat16)
    pieces = (
        lax.all_gather(query_weight, ("tok", "fs"), axis=0, tiled=True),
        lax.all_gather(key_weight, ("tok", "fs"), axis=0, tiled=True),
        lax.all_gather(value_weight, ("tok", "fs"), axis=0, tiled=True),
        lax.all_gather(first_gain, ("tok", "fs"), axis=0, tiled=True),
    )
    section = (
        contract_cols(grad_qraw, pieces[0])
        + contract_cols(grad_kraw, pieces[1])
        + contract_cols(grad_vraw, pieces[2])
    )
    normed = normed_one
    grad_normed = section * pieces[3].astype(jnp.float32)[None, :]
    gain_sum = jnp.sum(section * normed, axis=0)
    three_grads = jnp.concatenate([grad_qraw, grad_kraw, grad_vraw], axis=1)
    attention_grad = weight_sums(kept_one, three_grads)
    input_grad = grad_second + pull_one(grad_normed)[0]
    output_grad, first_gain_grad, second_gain_grad = (
        lax.psum_scatter(output_full, ("grp", "tok", "fs"), scatter_dimension=0, tiled=True),
        lax.psum_scatter(gain_sum, ("grp", "tok", "fs"), scatter_dimension=0, tiled=True),
        lax.psum_scatter(gain_two, ("grp", "tok", "fs"), scatter_dimension=0, tiled=True),
    )
    return (
        layer_output,
        input_grad,
        attention_grad[:, :width],
        attention_grad[:, width : 2 * width],
        attention_grad[:, 2 * width :],
        output_grad,
        mixer_grad[:, :ff_width],
        mixer_grad[:, ff_width:],
        down_grad,
        first_gain_grad,
        second_gain_grad,
    )


def solution(mesh):
    layered = mesh.shape["grp"] == mesh.shape["tok"] == 4 and mesh.shape["fs"] == 2
    return jax.shard_map(
        make_layered(mesh) if layered else spread_local,
        mesh=mesh,
        in_specs=(
            P(("grp", "tok", "fs"), None),
            P(("grp", "tok", "fs"), None),
            P("grp", None),
            P(("tok", "fs"), None),
            P(("tok", "fs"), None),
            P(("tok", "fs"), None),
            P(("tok", "fs"), None),
            P(("tok", "fs"), None),
            P(("tok", "fs"), None),
            P(("tok", "fs"), None),
            P(("tok", "fs")),
            P(("tok", "fs")),
        ),
        out_specs=(
            P(("grp", "tok", "fs"), None),
            P(("grp", "tok", "fs"), None),
            P(("grp", "tok", "fs"), None),
            P(("grp", "tok", "fs"), None),
            P(("grp", "tok", "fs"), None),
            P(("grp", "tok", "fs"), None),
            P(("grp", "tok", "fs"), None),
            P(("grp", "tok", "fs"), None),
            P(("grp", "tok", "fs"), None),
            P(("grp", "tok", "fs")),
            P(("grp", "tok", "fs")),
        ),
        check_vma=False,
    )
```

```python
import functools
import math

import jax
import jax.numpy as jnp
from jax import lax
from jax.experimental import pallas as pl
from jax.experimental.pallas import tpu as pltpu
from jax.sharding import PartitionSpec as P

HEAD_DIM = 64
BLOCK = 128
PROMPT = 1024
CONT = 256


EPS = 1e-05
RESIDUAL = 1.4 / math.sqrt(40.0)
NEGATIVE = -1e30
GROUP_HEADS = 4

ALL = ("grp", "tok", "fs")
LAYER = ("grp", "fs")
PIECE = 64
TILE = 256
PAIR = 2 * HEAD_DIM
SLAB = 3 * PAIR
BF = jnp.bfloat16
F32 = jnp.float32


def turn(field):
    lane = lax.broadcasted_iota(jnp.int32, field.shape, 1)
    return jnp.where(
        lane % HEAD_DIM < HEAD_DIM // 2,
        pltpu.roll(field, PAIR - HEAD_DIM // 2, 1),
        pltpu.roll(field, HEAD_DIM // 2, 1),
    )


def table_row(piece):
    prompt_pieces = PROMPT // PIECE
    cont_pieces = CONT // PIECE
    return jnp.where(
        piece < prompt_pieces,
        piece,
        prompt_pieces + lax.rem(jnp.maximum(piece - prompt_pieces, 0), cont_pieces),
    )


def head_tiles(pair, index_ref, total, run_tile):
    side = index_ref[total // PIECE]
    own = pair < 2
    for tile in range(PROMPT // TILE):
        mine = side == (0 if tile % 4 in (0, 3) else 1)

        @pl.when(own)
        def _(tile=tile):
            run_tile(tile * TILE, tile * TILE, (0, 1))

        @pl.when(jnp.logical_and(jnp.logical_not(own), mine))
        def _(tile=tile):
            run_tile(tile * TILE, tile * TILE, (0,))

    later = (total - PROMPT) // TILE

    def body(step, carry):
        mine = (step * 2 >= later).astype(jnp.int32) == side
        start = pl.multiple_of(PROMPT + step * TILE, TILE)

        @pl.when(own)
        def _():
            run_tile(start, PROMPT, (0, 1))

        @pl.when(jnp.logical_and(jnp.logical_not(own), mine))
        def _():
            run_tile(start, PROMPT, (0,))

        return carry

    lax.fori_loop(0, later, body, 0)


def lanes_of(head, shape):
    lane = lax.broadcasted_iota(jnp.int32, shape, 1)
    return lane < HEAD_DIM if head == 0 else lane >= HEAD_DIM


def nt_dot(left, right):
    return lax.dot_general(left, right, (((1,), (1,)), ((), ())), preferred_element_type=F32)


def tn_dot(left, right):
    return lax.dot_general(left, right, (((0,), (0,)), ((), ())), preferred_element_type=F32)


def nn_dot(left, right):
    return lax.dot_general(left, right, (((1,), (0,)), ((), ())), preferred_element_type=F32)


def attend_kernel(index_ref, raw_ref, cos_ref, sin_ref, out_ref, kept_ref, mixed):
    total = out_ref.shape[0]
    pieces = total // PIECE
    pair = pl.program_id(0)

    def rope(field, row):
        cosine = cos_ref[pl.ds(row, PIECE), :]
        sine = sin_ref[pl.ds(row, PIECE), :]
        return field * cosine + turn(field) * sine

    @pl.when(pair < 2)
    def _():
        def body(piece, carry):
            source = pl.multiple_of(index_ref[piece], PIECE)
            row = pl.multiple_of(table_row(piece) * PIECE, PIECE)
            target = pl.ds(pl.multiple_of(piece * PIECE, PIECE), PIECE)
            query = rope(raw_ref[pl.ds(source, PIECE), 0:PAIR], row)
            key = rope(raw_ref[pl.ds(source, PIECE), PAIR : 2 * PAIR], row)
            value = raw_ref[pl.ds(source, PIECE), 2 * PAIR : 3 * PAIR]
            kept_ref[0, target, 0:PAIR] = query.astype(BF)
            kept_ref[0, target, PAIR : 2 * PAIR] = key.astype(BF)
            kept_ref[0, target, 2 * PAIR : 3 * PAIR] = value.astype(BF)
            return carry

        lax.fori_loop(0, pieces, body, 0)

    @pl.when(pair == 2)
    def _():
        def body(piece, carry):
            source = pl.multiple_of(index_ref[piece], PIECE)
            row = pl.multiple_of(table_row(piece) * PIECE, PIECE)
            target = pl.ds(pl.multiple_of(piece * PIECE, PIECE), PIECE)
            both = rope(raw_ref[pl.ds(source, PIECE), 0:PAIR], row)
            value = raw_ref[pl.ds(source, PIECE), PAIR : 2 * PAIR]
            low = lanes_of(0, both.shape)
            kept_ref[0, target, 0:PAIR] = jnp.where(low, both, 0.0).astype(BF)
            kept_ref[0, target, PAIR : 2 * PAIR] = jnp.where(
                low, pltpu.roll(both, HEAD_DIM, 1), 0.0
            ).astype(BF)
            kept_ref[0, target, 2 * PAIR : 3 * PAIR] = jnp.where(low, value, 0.0).astype(BF)
            return carry

        lax.fori_loop(0, pieces, body, 0)

    mixed[...] = jnp.zeros_like(mixed)
    scale = 1.0 / math.sqrt(HEAD_DIM)

    def run_tile(start, prefix, heads):
        rows = pl.ds(start, TILE)
        query = kept_ref[0, rows, 0:PAIR].astype(F32) * scale
        masks = [lanes_of(head, query.shape) for head in heads]
        queries = [jnp.where(mask, query, 0.0).astype(BF) for mask in masks]
        seen = lax.broadcasted_iota(jnp.int32, (TILE, TILE), 1) <= lax.broadcasted_iota(
            jnp.int32, (TILE, TILE), 0
        )
        keys = [kept_ref[0, rows, PAIR : 2 * PAIR]]
        values = [kept_ref[0, rows, 2 * PAIR : 3 * PAIR]]
        if prefix:
            keys.append(kept_ref[0, 0:prefix, PAIR : 2 * PAIR])
            values.append(kept_ref[0, 0:prefix, 2 * PAIR : 3 * PAIR])
        scores = [[nt_dot(query, key) for key in keys] for query in queries]
        total_out = mixed[rows, :]
        for mask, parts in zip(masks, scores):
            parts[0] = jnp.where(seen, parts[0], NEGATIVE)
            peak = functools.reduce(
                jnp.maximum, [jnp.max(part, axis=1, keepdims=True) for part in parts]
            )
            parts = [jnp.exp(part - peak) for part in parts]
            count = sum(jnp.sum(part, axis=1, keepdims=True) for part in parts)
            out = sum(nn_dot(part.astype(BF), value) for part, value in zip(parts, values))
            total_out = jnp.where(mask, out / count, total_out)
        mixed[rows, :] = total_out

    head_tiles(pair, index_ref, total, run_tile)

    def back(piece, carry):
        source = pl.multiple_of(index_ref[piece], PIECE)
        target = pl.ds(pl.multiple_of(piece * PIECE, PIECE), PIECE)
        out_ref[pl.ds(source, PIECE), :] = mixed[target, :].astype(BF)
        return carry

    lax.fori_loop(0, pieces, back, 0)


def attend(index, raw, cosine, sine):
    total = raw.shape[0]
    return pl.pallas_call(
        attend_kernel,
        grid_spec=pltpu.PrefetchScalarGridSpec(
            num_scalar_prefetch=1,
            grid=(3,),
            in_specs=[
                pl.BlockSpec((total, SLAB), lambda j, index: (0, j)),
                pl.BlockSpec(cosine.shape, lambda j, index: (0, 0)),
                pl.BlockSpec(sine.shape, lambda j, index: (0, 0)),
            ],
            out_specs=[
                pl.BlockSpec((total, PAIR), lambda j, index: (0, j)),
                pl.BlockSpec((1, total, SLAB), lambda j, index: (j, 0, 0)),
            ],
            scratch_shapes=[pltpu.VMEM((total, PAIR), F32)],
        ),
        out_shape=[
            jax.ShapeDtypeStruct((total, 3 * PAIR), BF),
            jax.ShapeDtypeStruct((3, total, SLAB), BF),
        ],
        compiler_params=pltpu.CompilerParams(vmem_limit_bytes=40 << 20),
        cost_estimate=pl.CostEstimate(
            flops=36 * 10**9, bytes_accessed=1 << 20, transcendentals=0
        ),
        name="attend",
    )(index, raw, cosine, sine)


def attend_back_kernel(
    first, index_ref, kept_ref, outer_ref, cos_ref, sin_ref, grad_ref, outer, grad_q, grad_k, grad_v
):
    total = outer.shape[0]
    pieces = total // PIECE
    pair = pl.program_id(0) + first

    def sort(piece, carry):
        source = pl.multiple_of(index_ref[piece], PIECE)
        target = pl.ds(pl.multiple_of(piece * PIECE, PIECE), PIECE)
        outer[target, :] = outer_ref[pl.ds(source, PIECE), :]
        return carry

    lax.fori_loop(0, pieces, sort, 0)
    grad_q[...] = jnp.zeros_like(grad_q)
    grad_k[...] = jnp.zeros_like(grad_k)
    grad_v[...] = jnp.zeros_like(grad_v)
    scale = 1.0 / math.sqrt(HEAD_DIM)

    def run_tile(start, prefix, heads):
        rows = pl.ds(start, TILE)
        query = kept_ref[0, rows, 0:PAIR].astype(F32) * scale
        away = outer[rows, :].astype(F32)
        masks = [lanes_of(head, query.shape) for head in heads]
        queries = [jnp.where(mask, query, 0.0).astype(BF) for mask in masks]
        aways = [jnp.where(mask, away, 0.0).astype(BF) for mask in masks]
        seen = lax.broadcasted_iota(jnp.int32, (TILE, TILE), 0) <= lax.broadcasted_iota(
            jnp.int32, (TILE, TILE), 1
        )
        spans = [rows] + ([pl.ds(0, prefix)] if prefix else [])
        keys = [kept_ref[0, span, PAIR : 2 * PAIR] for span in spans]
        values = [kept_ref[0, span, 2 * PAIR : 3 * PAIR] for span in spans]
        scores = [[nt_dot(key, query) for key in keys] for query in queries]
        pulls = [[nt_dot(value, away) for value in values] for away in aways]
        probs, slopes = [], []
        for parts, pull in zip(scores, pulls):
            parts[0] = jnp.where(seen, parts[0], NEGATIVE)
            peak = functools.reduce(
                jnp.maximum, [jnp.max(part, axis=0, keepdims=True) for part in parts]
            )
            parts = [jnp.exp(part - peak) for part in parts]
            inverse = 1.0 / sum(jnp.sum(part, axis=0, keepdims=True) for part in parts)
            parts = [part * inverse for part in parts]
            delta = sum(jnp.sum(p * q, axis=0, keepdims=True) for p, q in zip(parts, pull))
            probs.append([part.astype(BF) for part in parts])
            slopes.append([(p * (q - delta)).astype(BF) for p, q in zip(parts, pull)])
        for i, span in enumerate(spans):
            grad_v[span, :] += sum(nn_dot(prob[i], away) for prob, away in zip(probs, aways))
            grad_k[span, :] += sum(nn_dot(slope[i], query) for slope, query in zip(slopes, queries))
        part_q = grad_q[rows, :]
        for mask, slope in zip(masks, slopes):
            part = sum(tn_dot(piece, key) for piece, key in zip(slope, keys))
            part_q = jnp.where(mask, part * scale, part_q)
        grad_q[rows, :] = part_q

    head_tiles(pair, index_ref, total, run_tile)

    def unrope(field, row):
        cosine = cos_ref[pl.ds(row, PIECE), :]
        sine = sin_ref[pl.ds(row, PIECE), :]
        return field * cosine - turn(field) * sine

    @pl.when(pair < 2)
    def _():
        def back(piece, carry):
            source = pl.ds(pl.multiple_of(index_ref[piece], PIECE), PIECE)
            row = pl.multiple_of(table_row(piece) * PIECE, PIECE)
            here = pl.ds(pl.multiple_of(piece * PIECE, PIECE), PIECE)
            grad_ref[source, 0:PAIR] = unrope(grad_q[here, :], row).astype(BF)
            grad_ref[source, PAIR : 2 * PAIR] = unrope(grad_k[here, :], row).astype(BF)
            grad_ref[source, 2 * PAIR : 3 * PAIR] = grad_v[here, :].astype(BF)
            return carry

        lax.fori_loop(0, pieces, back, 0)

    @pl.when(pair == 2)
    def _():
        def back(piece, carry):
            source = pl.ds(pl.multiple_of(index_ref[piece], PIECE), PIECE)
            row = pl.multiple_of(table_row(piece) * PIECE, PIECE)
            here = pl.ds(pl.multiple_of(piece * PIECE, PIECE), PIECE)
            low = lanes_of(0, (PIECE, PAIR))
            both = jnp.where(low, grad_q[here, :], pltpu.roll(grad_k[here, :], HEAD_DIM, 1))
            grad_ref[source, 0:PAIR] = unrope(both, row).astype(BF)
            grad_ref[source, PAIR : 2 * PAIR] = grad_v[here, :].astype(BF)
            grad_ref[source, 2 * PAIR : 3 * PAIR] = jnp.zeros((PIECE, PAIR), BF)
            return carry

        lax.fori_loop(0, pieces, back, 0)


def attend_back(first, count, index, kept, outer, cosine, sine, columns):
    total = outer.shape[0]
    return pl.pallas_call(
        functools.partial(attend_back_kernel, first),
        grid_spec=pltpu.PrefetchScalarGridSpec(
            num_scalar_prefetch=1,
            grid=(count,),
            in_specs=[
                pl.BlockSpec((1, total, SLAB), lambda j, index: (j + first, 0, 0)),
                pl.BlockSpec((total, PAIR), lambda j, index: (0, j + first)),
                pl.BlockSpec(cosine.shape, lambda j, index: (0, 0)),
                pl.BlockSpec(sine.shape, lambda j, index: (0, 0)),
            ],
            out_specs=pl.BlockSpec((total, SLAB), lambda j, index: (0, j)),
            scratch_shapes=[
                pltpu.VMEM((total, PAIR), BF),
                pltpu.VMEM((total, PAIR), F32),
                pltpu.VMEM((total, PAIR), F32),
                pltpu.VMEM((total, PAIR), F32),
            ],
        ),
        out_shape=jax.ShapeDtypeStruct((total, columns), BF),
        compiler_params=pltpu.CompilerParams(vmem_limit_bytes=48 << 20),
        cost_estimate=pl.CostEstimate(
            flops=0, bytes_accessed=1 << 20, transcendentals=0
        ),
        name="attend_back",
    )(index, kept, outer, cosine, sine)


def after(array, *earlier):
    leaves = [array] + jax.tree.leaves(earlier)
    place = pl.BlockSpec(memory_space=pl.ANY)
    return pl.pallas_call(
        lambda *refs: None,
        in_specs=[place] * len(leaves),
        out_specs=place,
        out_shape=jax.ShapeDtypeStruct(array.shape, array.dtype),
        input_output_aliases={0: 0},
        name="after",
    )(*leaves)


def make_layered(mesh):
    n_grp, n_tok, n_fs = (mesh.shape[axis] for axis in ALL)

    def device(grp, tok, fs):
        return (grp * n_tok + tok) * n_fs + fs

    def permutation(move):
        return [
            (device(g, t, f), device(*move(g, t, f)))
            for g in range(n_grp)
            for t in range(n_tok)
            for f in range(n_fs)
        ]

    def send(array, move):
        return lax.ppermute(array, ALL, permutation(move))

    def cross(step):
        return lambda g, t, f: (g ^ step, t, f)

    def sibling(g, t, f):
        return (g, t, 1 - f)

    def local(
        hidden_in,
        cotangent,
        block_start,
        query_weight,
        key_weight,
        value_weight,
        output_weight,
        gate_weight,
        up_weight,
        down_weight,
        first_gain,
        second_gain,
    ):
        rows, width = hidden_in.shape
        ff_width = gate_weight.shape[1]
        g, t, f = (lax.axis_index(axis) for axis in ALL)
        even = f == 0
        ranks = n_grp * n_fs
        total = rows * ranks
        quarter = rows // n_grp


        def spread_in(array):
            return lax.all_to_all(array.reshape(n_grp, quarter, width), "grp", 0, 0, tiled=True)

        def shuffle_in(parts):
            return lax.all_to_all(parts, "tok", 0, 0, tiled=True).reshape(rows, width)

        def shuffle_out(arrays, beside):
            parts = [array.reshape(n_tok, quarter, width) for array in arrays]
            results = [jnp.zeros_like(part) for part in parts]
            for turn_by in range(n_grp):
                away = g ^ t ^ turn_by
                pieces = [lax.dynamic_index_in_dim(part, away, 0, keepdims=True) for part in parts]
                piece = send(
                    jnp.concatenate(pieces, axis=1),
                    lambda g, t, f, turn_by=turn_by: (t, g ^ t ^ turn_by, f),
                )
                piece = after(piece, beside)
                for i, result in enumerate(results):
                    results[i] = lax.dynamic_update_slice_in_dim(
                        result, piece[:, i * quarter : (i + 1) * quarter], away, 0
                    )
            return [result.reshape(rows, width) for result in results]


        def layer_pieces(array):
            half = array.shape[0] // 2
            by_x = send(array, cross(1))
            by_y = send(array, cross(2))
            return array, by_x, by_y, send(by_x[:half], cross(2)), send(by_y[half:], cross(1))

        def layer_join(array, by_x, by_y, *by_xy):
            mine = [array, by_x, by_y, jnp.concatenate(by_xy, axis=0)]
            return jnp.concatenate(mine + [send(part, sibling) for part in mine], axis=0)

        def layer_gather(array):
            return layer_join(*layer_pieces(array))

        def pair_sum(rows_of):
            away = rows_of(1).astype(BF).reshape(n_grp, rows, -1)
            away = {step: send(away[step], sibling) for step in (3, 1, 2, 0)}
            here = rows_of(0).reshape(n_grp, rows, -1)
            parts = [(here[step] + away[step].astype(F32)).astype(BF) for step in (3, 1, 2)]
            return here[0], away[0], parts

        def layer_send(sums, *earlier):
            here, away, parts = sums
            if earlier:
                parts = [after(part, *earlier) for part in parts]
            return here, away, [send(part, cross(step)) for part, step in zip(parts, (3, 1, 2))]

        def layer_add(parts, beside=None):
            here, away, got = parts
            if beside is not None:
                got = [after(part, beside) for part in got]
            return here + away.astype(F32) + sum(part.astype(F32) for part in got)

        def layer_sum(rows_of, beside=None):
            return layer_add(layer_send(pair_sum(rows_of)), beside)

        def halves(*arrays):
            half = arrays[0].shape[0] // 2
            return lambda which: [array[which * half : (which + 1) * half] for array in arrays]

        extra = 8
        gains_here = jnp.concatenate([first_gain, second_gain])
        span = gains_here.shape[0]
        gains_here = jnp.pad(gains_here[None, :], ((0, extra - 1), (0, width - span)))
        hidden_parts = spread_in(hidden_in)
        cotangent_parts = spread_in(after(cotangent, hidden_parts))
        arrived = lax.all_to_all(
            jnp.concatenate(
                [hidden_parts, jnp.broadcast_to(gains_here[None], (n_tok, extra, width))], axis=1
            ),
            "tok",
            0,
            0,
            tiled=True,
        )
        gains_mine = arrived[:, quarter, :span]
        gains_other = send(gains_mine, sibling)
        gains_all = jnp.stack(
            [jnp.where(even, gains_mine, gains_other), jnp.where(even, gains_other, gains_mine)],
            axis=1,
        ).astype(F32).reshape(n_tok * n_fs, 2, -1)
        gain_one = gains_all[:, 0].reshape(width)
        gain_two = gains_all[:, 1].reshape(width)
        starts = send(block_start, lambda g, t, f: (t, g, f))[0]
        xs = arrived[:, :quarter].reshape(rows, width)
        cotangent_here = shuffle_in(after(cotangent_parts, xs))


        head_span = width // n_grp
        own_span = 4 * HEAD_DIM

        def rank_columns(side):
            picked = [
                lax.dynamic_slice_in_dim(weight, g * head_span, head_span, 1)
                for weight in (query_weight, key_weight, value_weight)
            ]
            first = side * (own_span + HEAD_DIM)
            spans = [(first, PAIR), (first + PAIR, PAIR), (own_span, HEAD_DIM)]
            columns = [weight[:, at : at + size] for at, size in spans for weight in picked]
            wide = sum(part.shape[1] for part in columns)
            columns.append(jnp.zeros((query_weight.shape[0], -wide % PAIR), BF))
            return jnp.concatenate(columns, axis=1)

        def pair_rows(zero_block, one_block):
            mine = jnp.where(even, zero_block, one_block)
            other = send(jnp.where(even, one_block, zero_block), sibling)
            return jnp.concatenate(
                [jnp.where(even, mine, other), jnp.where(even, other, mine)], axis=0
            )

        def gather_rows(array, *earlier):
            array = after(array, *earlier)
            return array, lax.all_gather(array, "tok", axis=0, tiled=True)

        turn_one, qkv_weight = gather_rows(
            pair_rows(rank_columns(0), rank_columns(1)), xs
        )
        ff_piece = ff_width // (ranks * n_tok)
        ff_tall = -(-ff_piece // 64) * 64
        ff_wide = ff_tall * n_tok

        def ff_columns(side):
            parts = [
                lax.dynamic_slice_in_dim(
                    weight, (step * n_fs + side) * n_grp * ff_piece + g * ff_piece, ff_piece, 1
                )
                for weight in (gate_weight, up_weight)
                for step in range(n_tok)
            ]
            zeros = jnp.zeros((gate_weight.shape[0], ff_tall - ff_piece), BF)
            return jnp.concatenate([item for part in parts for item in (part, zeros)], axis=1)

        ff_inputs = (
            pair_rows(ff_columns(0), ff_columns(1)),
            jnp.pad(
                lax.dynamic_slice_in_dim(down_weight, g * ff_piece, ff_piece, 0),
                ((0, ff_tall - ff_piece), (0, 0)),
            ),
        )

        hidden = after(xs, *ff_inputs).astype(F32)
        scale_one = lax.rsqrt(jnp.mean(hidden * hidden, axis=1, keepdims=True) + EPS)
        normed_one = hidden * scale_one
        h_one = layer_gather((normed_one * gain_one[None, :]).astype(BF))
        out_rows = output_weight.shape[0] // n_grp
        turn_two, out_weight = gather_rows(
            lax.dynamic_slice_in_dim(output_weight, g * out_rows, out_rows, 0), turn_one, h_one
        )
        grad_out = cotangent_here.astype(F32)
        grad_m_pieces = layer_pieces(after((RESIDUAL * grad_out).astype(BF), h_one))
        grad_m = layer_join(*grad_m_pieces)
        raw = nn_dot(after(h_one, *grad_m_pieces[1:3]), qkv_weight)
        out_weight = lax.all_to_all(after(out_weight, raw), "grp", 0, 0, tiled=True)
        half_head = HEAD_DIM // 2
        swapped = send(
            jnp.where(even, out_weight[own_span:], out_weight[:half_head]), sibling
        )
        out_weight = jnp.concatenate(
            [
                jnp.where(even, out_weight[:own_span], out_weight[half_head:]),
                jnp.where(even, out_weight[own_span:], swapped),
                jnp.where(even, swapped, out_weight[:half_head]),
                jnp.zeros((HEAD_DIM, width), BF),
            ],
            axis=0,
        )

        _, ff_weight = gather_rows(ff_inputs[0], turn_two)
        _, down_w = gather_rows(ff_inputs[1], ff_inputs[0], turn_two)


        number = jnp.arange(total // BLOCK, dtype=jnp.int32)
        prompt_blocks = PROMPT // BLOCK
        cont_blocks = CONT // BLOCK
        place = jnp.where(
            number < prompt_blocks,
            starts // BLOCK,
            prompt_blocks
            + (number - prompt_blocks) // cont_blocks * cont_blocks
            + (starts - PROMPT) // BLOCK,
        )
        order = jnp.sum(
            jnp.where(place[None, :] == number[:, None], number[None, :], 0), axis=1
        )
        pieces = (
            order[:, None] * (BLOCK // PIECE) + jnp.arange(BLOCK // PIECE, dtype=jnp.int32)
        ).reshape(-1)
        from_t = pieces // ranks
        from_f = pieces // n_grp % n_fs
        from_g = pieces % n_grp
        index = jnp.concatenate(
            [
                (((from_f ^ f) * n_grp + (from_g ^ g)) * n_tok + from_t) * PIECE,
                f[None].astype(jnp.int32),
            ]
        ).astype(jnp.int32)
        lane = jnp.arange(PAIR, dtype=jnp.int32)
        half_head_lane = lane % (HEAD_DIM // 2)
        freq = 10000.0 ** (-(half_head_lane.astype(F32) * 2.0) / HEAD_DIM)
        angle = jnp.arange(PROMPT + CONT, dtype=F32)[:, None] * freq[None, :]
        cosine = jnp.cos(angle)
        sine = jnp.where(lane[None, :] % HEAD_DIM < HEAD_DIM // 2, -jnp.sin(angle), jnp.sin(angle))


        attn_out, kept = attend(index, raw, cosine, sine)
        pick = halves(attn_out)
        branch = layer_sum(lambda side, pick=pick: nn_dot(pick(side)[0], out_weight), grad_m)
        second_in = hidden + RESIDUAL * branch
        scale_two = lax.rsqrt(jnp.mean(second_in * second_in, axis=1, keepdims=True) + EPS)
        normed_two = second_in * scale_two
        h_two = layer_gather((normed_two * gain_two[None, :]).astype(BF))
        both = nn_dot(h_two, ff_weight)
        gate = both[:, :ff_wide]
        up_val = both[:, ff_wide:]
        sigma = jax.nn.sigmoid(gate)
        silu = gate * sigma
        act = (silu * up_val).astype(BF)


        down_local = tn_dot(act, grad_m).astype(BF).reshape(n_tok, ff_tall, width)
        grad_act = nt_dot(after(grad_m, down_local), down_w)
        grad_both = jnp.concatenate(
            [
                (grad_act * up_val * (sigma * (1.0 + gate * (1.0 - sigma)))).astype(BF),
                (grad_act * silu).astype(BF),
            ],
            axis=1,
        )
        def spread_rows(grad):
            columns = grad.shape[1]
            grad = grad.astype(BF).reshape(n_grp, n_tok, width // (n_grp * n_tok), columns)
            return grad.transpose(1, 0, 2, 3).reshape(n_tok, width // n_tok, columns)

        def sum_rows(grad):
            grad = lax.psum_scatter(grad, "tok", scatter_dimension=0, tiled=True)
            return grad.reshape(ranks, width // (ranks * n_tok), grad.shape[2])

        def to_owners(grad):
            return lax.all_to_all(grad, LAYER, 0, 0, tiled=True)

        pick = halves(grad_both)
        parts = layer_send(pair_sum(lambda side, pick=pick: nt_dot(pick(side)[0], ff_weight)))
        ff_local = spread_rows(tn_dot(h_two, after(grad_both, parts[0])))
        grad_h2 = layer_add(parts, ff_local)
        ff_rows = sum_rows(ff_local)
        gain_two_sum = jnp.sum(grad_h2 * normed_two, axis=0)
        pulled = grad_h2 * gain_two[None, :]
        grad_second = (
            grad_out
            + scale_two * pulled
            - scale_two**3 * second_in * jnp.mean(pulled * second_in, axis=1, keepdims=True)
        )
        grad_z_here = (RESIDUAL * grad_second).astype(BF)
        down_rows = lax.psum_scatter(down_local, "tok", scatter_dimension=0, tiled=True)
        down_rows = down_rows[0, :ff_piece]
        grad_z = layer_gather(grad_z_here)
        pick = halves(after(act, grad_z_here))
        feed_sums = pair_sum(lambda side, pick=pick: nn_dot(pick(side)[0], down_w))
        grad_attn = nt_dot(grad_z, out_weight).astype(BF)
        feed_parts = layer_send(feed_sums, grad_z)
        out_full = tn_dot(attn_out, grad_z)
        shared = out_full[own_span : own_span + HEAD_DIM]
        swapped = send(
            jnp.where(even, shared[half_head:], shared[:half_head]).astype(BF), sibling
        ).astype(F32)
        kept_half = jnp.where(even, shared[:half_head], shared[half_head:]) + swapped
        out_full = jnp.where(
            even,
            jnp.concatenate([out_full[:own_span], kept_half], axis=0),
            jnp.concatenate([kept_half, out_full[:own_span]], axis=0),
        )
        out_full = out_full.astype(BF).reshape(n_tok, -1, width)
        output_grad = lax.psum_scatter(out_full, "tok", scatter_dimension=0, tiled=True)

        grad_attn = after(grad_attn, out_full, down_rows, feed_parts[0])
        grads = attend_back(0, 3, index, kept, grad_attn, cosine, sine, qkv_weight.shape[1])
        grads = after(grads, ff_rows, *feed_parts[2])
        qkv_local = spread_rows(tn_dot(h_one, grads))
        qkv_rows = sum_rows(qkv_local)
        got = to_owners(after(ff_rows, grads))
        down_grad = send(
            after(down_rows, qkv_rows),
            lambda g, t, f: (t, (n_grp * f + g) // n_fs, (n_grp * f + g) % n_fs),
        )
        pick = halves(after(grads, qkv_local, output_grad, got))
        parts = layer_send(pair_sum(lambda side, pick=pick: nt_dot(pick(side)[0], qkv_weight)))
        feed = layer_add(feed_parts, parts[2][1])
        layer_output = (second_in + RESIDUAL * feed).astype(BF)
        got = after(got, layer_output).reshape(n_grp, n_fs, -1, 2, n_tok, ff_tall)
        gate_grad, up_grad = (
            got[:, :, :, which, :, :ff_piece]
            .transpose(2, 3, 1, 0, 4)
            .reshape(-1, ff_width)
            .astype(F32)
            for which in range(2)
        )
        grad_h1 = layer_add(parts, (gate_grad, up_grad))
        gain_one_sum = jnp.sum(grad_h1 * normed_one, axis=0)
        pulled = grad_h1 * gain_one[None, :]
        input_grad = (
            grad_second
            + scale_one * pulled
            - scale_one**3 * hidden * jnp.mean(pulled * hidden, axis=1, keepdims=True)
        )
        input_grad = after(input_grad.astype(BF), qkv_rows)
        output_grad = send(
            output_grad[0], lambda g, t, f: (g, (n_tok * f + t) // n_fs, (n_tok * f + t) % n_fs)
        ).astype(F32)
        got = to_owners(qkv_rows)
        own_rows = got.shape[1]
        here = got.astype(F32).reshape(n_grp, n_fs, own_rows, got.shape[2])

        def projection_grad(which):
            def own(side):
                return [
                    here[:, side, :, SLAB * pair + PAIR * which : SLAB * pair + PAIR * (which + 1)]
                    for pair in range(2)
                ]

            at = 2 * SLAB + HEAD_DIM * which
            shared = here[:, 0, :, at : at + HEAD_DIM] + here[:, 1, :, at : at + HEAD_DIM]
            whole = jnp.concatenate(own(0) + [shared] + own(1), axis=2)
            return whole.transpose(1, 0, 2).reshape(own_rows, width)

        qkv_grads = [projection_grad(which) for which in range(3)]
        layer_output, input_grad = shuffle_out((layer_output, input_grad), qkv_grads)
        input_grad = input_grad.astype(F32)
        gains = jnp.stack([gain_one_sum, gain_two_sum], axis=1).reshape(
            n_grp * n_tok * n_fs, -1
        )
        gains = after(gains, got)
        gains = jnp.sum(lax.all_to_all(gains, ALL, 0, 0, tiled=True), axis=0).reshape(-1, 2)
        return (
            layer_output,
            input_grad,
            *qkv_grads,
            output_grad,
            gate_grad,
            up_grad,
            down_grad.astype(F32),
            gains[:, 0],
            gains[:, 1],
        )

    return local


def spread(block, axis, source):
    block = jnp.where(lax.axis_index(axis) == source, block, jnp.zeros_like(block))
    return lax.psum(block, axis)


def rope_tables(positions, head_size):
    half = head_size // 2
    freq = 10000.0 ** (-(jnp.arange(half, dtype=jnp.float32) * 2.0) / head_size)
    angle = positions.astype(jnp.float32)[:, None] * freq[None, :]
    return (jnp.cos(angle)[:, None, :], jnp.sin(angle)[:, None, :])


def rotate(field, cosine, sine):
    half = field.shape[-1] // 2
    first = field[..., :half]
    second = field[..., half:]
    return jnp.concatenate(
        [first * cosine - second * sine, second * cosine + first * sine], axis=-1
    )


def unrotate(grad, cosine, sine):
    half = grad.shape[-1] // 2
    first = grad[..., :half]
    second = grad[..., half:]
    return jnp.concatenate(
        [first * cosine + second * sine, second * cosine - first * sine], axis=-1
    )


def row_norm(values):
    return values * lax.rsqrt(jnp.mean(values * values, axis=-1, keepdims=True) + EPS)


def swish_product(gate, up_val):
    return jax.nn.silu(gate) * up_val


def contract_rows(left, right):
    return lax.dot_general(
        left, right, (((0,), (0,)), ((), ())), preferred_element_type=jnp.float32
    )


def contract_cols(left, right):
    return lax.dot_general(
        left, right, (((1,), (1,)), ((), ())), preferred_element_type=jnp.float32
    )


def weight_sums(left, right):
    return lax.psum_scatter(
        contract_rows(left, right), ("grp", "tok", "fs"), scatter_dimension=0, tiled=True
    )


def spread_local(
    hidden_in,
    cotangent,
    block_start,
    query_weight,
    key_weight,
    value_weight,
    output_weight,
    gate_weight,
    up_weight,
    down_weight,
    first_gain,
    second_gain,
):
    local_rows, width = hidden_in.shape
    ff_width = gate_weight.shape[1]
    head_size = HEAD_DIM
    heads = width // head_size
    group_width = GROUP_HEADS * head_size
    group_count = heads // GROUP_HEADS
    scale = 1.0 / math.sqrt(head_size)
    device = lax.axis_index(("tok", "fs"))
    holders = -(-PROMPT // local_rows)
    prompt_rows = holders * local_rows
    starts = block_start[0]
    offsets = jnp.arange(BLOCK, dtype=jnp.int32)
    local_starts = lax.dynamic_slice_in_dim(
        starts, device * (local_rows // BLOCK), local_rows // BLOCK
    )
    my_pos = (local_starts[:, None] + offsets[None, :]).reshape(local_rows)
    prompt_pos = (starts[: prompt_rows // BLOCK][:, None] + offsets[None, :]).reshape(prompt_rows)
    my_row = device * local_rows + jnp.arange(local_rows, dtype=jnp.int32)
    my_seg = jnp.where(my_row < PROMPT, 0, 1 + (my_row - PROMPT) // CONT)
    prompt_row = jnp.arange(prompt_rows, dtype=jnp.int32)
    prompt_seen = (prompt_row[None, :] < PROMPT) & (prompt_pos[None, :] <= my_pos[:, None])
    local_seen = (
        (my_seg[None, :] == my_seg[:, None])
        & (my_seg[None, :] > 0)
        & (my_pos[None, :] <= my_pos[:, None])
    )
    visible = jnp.concatenate([prompt_seen, local_seen], axis=1)
    cosine, sine = rope_tables(my_pos, head_size)
    hidden = hidden_in.astype(jnp.float32)
    normed_one, pull_one = jax.vjp(row_norm, hidden)
    zero_rows = jnp.zeros((local_rows, width), jnp.float32)
    pieces = (
        lax.all_gather(query_weight, ("tok", "fs"), axis=0, tiled=True),
        lax.all_gather(key_weight, ("tok", "fs"), axis=0, tiled=True),
        lax.all_gather(value_weight, ("tok", "fs"), axis=0, tiled=True),
        lax.all_gather(first_gain, ("tok", "fs"), axis=0, tiled=True),
    )
    normed = normed_one
    scaled = (normed * pieces[3].astype(jnp.float32)[None, :]).astype(jnp.bfloat16)
    kept = scaled
    query_acc = jnp.dot(scaled, pieces[0], preferred_element_type=jnp.float32)
    key_acc = jnp.dot(scaled, pieces[1], preferred_element_type=jnp.float32)
    value_acc = jnp.dot(scaled, pieces[2], preferred_element_type=jnp.float32)
    kept_one = kept
    queries = (
        rotate(query_acc.reshape(local_rows, heads, head_size), cosine, sine)
        .astype(jnp.bfloat16)
        .reshape(local_rows, width)
    )
    keys = (
        rotate(key_acc.reshape(local_rows, heads, head_size), cosine, sine)
        .astype(jnp.bfloat16)
        .reshape(local_rows, width)
    )
    values = value_acc.astype(jnp.bfloat16)
    paired = jnp.stack([keys, values])
    received = []
    for root in range(holders):
        received.append(spread(paired, ("tok", "fs"), root))
    gathered = jnp.concatenate(received, axis=1)
    all_keys = jnp.concatenate([gathered[0], keys], axis=0)
    all_values = jnp.concatenate([gathered[1], values], axis=0)
    total_keys = all_keys.shape[0]

    def head_slice(array, index):
        return lax.dynamic_slice_in_dim(array, index * group_width, group_width, 1).reshape(
            array.shape[0], GROUP_HEADS, head_size
        )

    def scores_of(index):
        raw = (
            jnp.einsum(
                "qhd,khd->hqk",
                head_slice(queries, index),
                head_slice(all_keys, index),
                preferred_element_type=jnp.float32,
            )
            * scale
        )
        return jnp.where(visible[None], raw, NEGATIVE)

    def attend_group(index, carry):
        mixed, peaks, totals = carry
        scores = scores_of(index)
        peak = jnp.max(scores, axis=-1, keepdims=True)
        expo = jnp.exp(scores - peak)
        total = jnp.sum(expo, axis=-1, keepdims=True)
        probs = (expo / total).astype(jnp.bfloat16)
        block_out = jnp.einsum(
            "hqk,khd->qhd", probs, head_slice(all_values, index), preferred_element_type=jnp.float32
        ).reshape(local_rows, group_width)
        mixed = lax.dynamic_update_slice_in_dim(mixed, block_out, index * group_width, 1)
        peaks = lax.dynamic_update_slice_in_dim(peaks, peak[None, :, :, 0], index, 0)
        totals = lax.dynamic_update_slice_in_dim(totals, total[None, :, :, 0], index, 0)
        return (mixed, peaks, totals)

    stats_zero = jnp.zeros((group_count, GROUP_HEADS, local_rows), jnp.float32)
    mixed, peaks, totals = lax.fori_loop(
        0, group_count, attend_group, (zero_rows, stats_zero, stats_zero)
    )
    attention_out = mixed.astype(jnp.bfloat16)
    branch = jnp.dot(
        attention_out,
        lax.all_gather(output_weight, ("tok", "fs"), axis=0, tiled=True),
        preferred_element_type=jnp.float32,
    )
    second_in = hidden + RESIDUAL * branch
    normed_two, pull_two = jax.vjp(row_norm, second_in)
    retained = ()
    pieces = (
        lax.all_gather(gate_weight, ("tok", "fs"), axis=0, tiled=True),
        lax.all_gather(up_weight, ("tok", "fs"), axis=0, tiled=True),
        lax.all_gather(second_gain, ("tok", "fs"), axis=0, tiled=True),
    )
    start = jnp.int32(0)
    stored = retained
    normed = normed_two
    scaled = (normed * pieces[2].astype(jnp.float32)[None, :]).astype(jnp.bfloat16)
    kept = scaled
    stored = tuple(
        (
            lax.dynamic_update_slice_in_dim(buffer, piece, start, 0)
            for buffer, piece in zip(stored, pieces)
        )
    )
    gate_acc, up_acc, kept_two, stored = (
        jnp.dot(scaled, pieces[0], preferred_element_type=jnp.float32),
        jnp.dot(scaled, pieces[1], preferred_element_type=jnp.float32),
        kept,
        stored,
    )
    swish, pull_swish = jax.vjp(swish_product, gate_acc, up_acc)
    act = swish.astype(jnp.bfloat16)
    down_store = ()
    piece = lax.all_gather(down_weight, ("tok", "fs"), axis=0, tiled=True)
    start = jnp.int32(0)
    stored_down = down_store
    total_acc = jnp.dot(act, piece, preferred_element_type=jnp.float32)
    stored_down = tuple(
        (lax.dynamic_update_slice_in_dim(buffer, piece, start, 0) for buffer in stored_down)
    )
    feed, stored_down = (total_acc, stored_down)
    layer_output = (second_in + RESIDUAL * feed).astype(jnp.bfloat16)
    grad_out = cotangent.astype(jnp.float32)
    grad_m = (RESIDUAL * grad_out).astype(jnp.bfloat16)
    grad_act = contract_cols(grad_m, lax.all_gather(down_weight, ("tok", "fs"), axis=0, tiled=True))
    down_grad = weight_sums(act, grad_m)
    grad_gate_f, grad_up_f = pull_swish(grad_act)
    grad_gate = grad_gate_f.astype(jnp.bfloat16)
    grad_up = grad_up_f.astype(jnp.bfloat16)
    pieces = (
        lax.all_gather(gate_weight, ("tok", "fs"), axis=0, tiled=True),
        lax.all_gather(up_weight, ("tok", "fs"), axis=0, tiled=True),
        lax.all_gather(second_gain, ("tok", "fs"), axis=0, tiled=True),
    )
    section = contract_cols(grad_gate, pieces[0]) + contract_cols(grad_up, pieces[1])
    normed = normed_two
    grad_normed = section * pieces[2].astype(jnp.float32)[None, :]
    gain_sum = jnp.sum(section * normed, axis=0)
    grad_n2 = grad_normed
    gain_two = gain_sum
    both_grads = jnp.concatenate([grad_gate, grad_up], axis=1)
    mixer_grad = weight_sums(kept_two, both_grads)
    grad_second = grad_out + pull_two(grad_n2)[0]
    grad_z = (RESIDUAL * grad_second).astype(jnp.bfloat16)
    output_full = contract_rows(attention_out, grad_z)
    grad_attn = contract_cols(
        grad_z, lax.all_gather(output_weight, ("tok", "fs"), axis=0, tiled=True)
    ).astype(jnp.bfloat16)

    def attend_back(index, carry):
        grad_q, grad_k, grad_v = carry
        query_g = head_slice(queries, index)
        key_g = head_slice(all_keys, index)
        value_g = head_slice(all_values, index)
        outer_g = head_slice(grad_attn, index)
        scores = scores_of(index)
        peak = lax.dynamic_index_in_dim(peaks, index, 0, keepdims=False)[:, :, None]
        total = lax.dynamic_index_in_dim(totals, index, 0, keepdims=False)[:, :, None]
        probs = jnp.exp(scores - peak) / total
        grad_probs = jnp.einsum(
            "qhd,khd->hqk", outer_g, value_g, preferred_element_type=jnp.float32
        )
        grad_scores = (
            probs * (grad_probs - jnp.sum(grad_probs * probs, axis=-1, keepdims=True))
        ).astype(jnp.bfloat16)
        query_part = (
            jnp.einsum("hqk,khd->qhd", grad_scores, key_g, preferred_element_type=jnp.float32)
            * scale
        )
        key_part = (
            jnp.einsum("hqk,qhd->khd", grad_scores, query_g, preferred_element_type=jnp.float32)
            * scale
        )
        value_part = jnp.einsum(
            "hqk,qhd->khd", probs.astype(jnp.bfloat16), outer_g, preferred_element_type=jnp.float32
        )
        grad_q = lax.dynamic_update_slice_in_dim(
            grad_q, query_part.reshape(local_rows, group_width), index * group_width, 1
        )
        grad_k = lax.dynamic_update_slice_in_dim(
            grad_k, key_part.reshape(total_keys, group_width), index * group_width, 1
        )
        grad_v = lax.dynamic_update_slice_in_dim(
            grad_v, value_part.reshape(total_keys, group_width), index * group_width, 1
        )
        return (grad_q, grad_k, grad_v)

    zero_keys = jnp.zeros((total_keys, width), jnp.float32)
    grad_q, grad_k, grad_v = lax.fori_loop(
        0, group_count, attend_back, (zero_rows, zero_keys, zero_keys)
    )
    share_k, share_v = (
        lax.psum_scatter(
            grad_k[:prompt_rows].astype(jnp.bfloat16),
            ("tok", "fs"),
            scatter_dimension=1,
            tiled=True,
        ).astype(jnp.float32),
        lax.psum_scatter(
            grad_v[:prompt_rows].astype(jnp.bfloat16),
            ("tok", "fs"),
            scatter_dimension=1,
            tiled=True,
        ).astype(jnp.float32),
    )
    prompt_dk, prompt_dv = (
        lax.all_gather(share_k.astype(jnp.bfloat16), ("tok", "fs"), axis=1, tiled=True).astype(
            share_k.dtype
        ),
        lax.all_gather(share_v.astype(jnp.bfloat16), ("tok", "fs"), axis=1, tiled=True).astype(
            share_v.dtype
        ),
    )
    holder = jnp.minimum(device, holders - 1)
    owned = device < holders
    mine_k = (
        jnp.where(
            owned, lax.dynamic_slice_in_dim(prompt_dk, holder * local_rows, local_rows, 0), 0.0
        )
        + grad_k[prompt_rows:]
    )
    mine_v = (
        jnp.where(
            owned, lax.dynamic_slice_in_dim(prompt_dv, holder * local_rows, local_rows, 0), 0.0
        )
        + grad_v[prompt_rows:]
    )
    grad_qraw = (
        unrotate(grad_q.reshape(local_rows, heads, head_size), cosine, sine)
        .reshape(local_rows, width)
        .astype(jnp.bfloat16)
    )
    grad_kraw = (
        unrotate(mine_k.reshape(local_rows, heads, head_size), cosine, sine)
        .reshape(local_rows, width)
        .astype(jnp.bfloat16)
    )
    grad_vraw = mine_v.astype(jnp.bfloat16)
    pieces = (
        lax.all_gather(query_weight, ("tok", "fs"), axis=0, tiled=True),
        lax.all_gather(key_weight, ("tok", "fs"), axis=0, tiled=True),
        lax.all_gather(value_weight, ("tok", "fs"), axis=0, tiled=True),
        lax.all_gather(first_gain, ("tok", "fs"), axis=0, tiled=True),
    )
    section = (
        contract_cols(grad_qraw, pieces[0])
        + contract_cols(grad_kraw, pieces[1])
        + contract_cols(grad_vraw, pieces[2])
    )
    normed = normed_one
    grad_normed = section * pieces[3].astype(jnp.float32)[None, :]
    gain_sum = jnp.sum(section * normed, axis=0)
    three_grads = jnp.concatenate([grad_qraw, grad_kraw, grad_vraw], axis=1)
    attention_grad = weight_sums(kept_one, three_grads)
    input_grad = grad_second + pull_one(grad_normed)[0]
    output_grad, first_gain_grad, second_gain_grad = (
        lax.psum_scatter(output_full, ("grp", "tok", "fs"), scatter_dimension=0, tiled=True),
        lax.psum_scatter(gain_sum, ("grp", "tok", "fs"), scatter_dimension=0, tiled=True),
        lax.psum_scatter(gain_two, ("grp", "tok", "fs"), scatter_dimension=0, tiled=True),
    )
    return (
        layer_output,
        input_grad,
        attention_grad[:, :width],
        attention_grad[:, width : 2 * width],
        attention_grad[:, 2 * width :],
        output_grad,
        mixer_grad[:, :ff_width],
        mixer_grad[:, ff_width:],
        down_grad,
        first_gain_grad,
        second_gain_grad,
    )


def solution(mesh):
    layered = mesh.shape["grp"] == mesh.shape["tok"] == 4 and mesh.shape["fs"] == 2
    return jax.shard_map(
        make_layered(mesh) if layered else spread_local,
        mesh=mesh,
        in_specs=(
            P(("grp", "tok", "fs"), None),
            P(("grp", "tok", "fs"), None),
            P("grp", None),
            P(("tok", "fs"), None),
            P(("tok", "fs"), None),
            P(("tok", "fs"), None),
            P(("tok", "fs"), None),
            P(("tok", "fs"), None),
            P(("tok", "fs"), None),
            P(("tok", "fs"), None),
            P(("tok", "fs")),
            P(("tok", "fs")),
        ),
        out_specs=(
            P(("grp", "tok", "fs"), None),
            P(("grp", "tok", "fs"), None),
            P(("grp", "tok", "fs"), None),
            P(("grp", "tok", "fs"), None),
            P(("grp", "tok", "fs"), None),
            P(("grp", "tok", "fs"), None),
            P(("grp", "tok", "fs"), None),
            P(("grp", "tok", "fs"), None),
            P(("grp", "tok", "fs"), None),
            P(("grp", "tok", "fs")),
            P(("grp", "tok", "fs")),
        ),
        check_vma=False,
    )
```

```python
import functools
import math

import jax
import jax.numpy as jnp
from jax import lax
from jax.experimental import pallas as pl
from jax.experimental.pallas import tpu as pltpu
from jax.sharding import PartitionSpec as P

HEAD_DIM = 64
BLOCK = 128
PROMPT = 1024
CONT = 256


EPS = 1e-05
RESIDUAL = 1.4 / math.sqrt(40.0)
NEGATIVE = -1e30
GROUP_HEADS = 4

ALL = ("grp", "tok", "fs")
LAYER = ("grp", "fs")
PIECE = 64
TILE = 256
PAIR = 2 * HEAD_DIM
SLAB = 3 * PAIR
BF = jnp.bfloat16
F32 = jnp.float32


def turn(field):
    lane = lax.broadcasted_iota(jnp.int32, field.shape, 1)
    return jnp.where(
        lane % HEAD_DIM < HEAD_DIM // 2,
        pltpu.roll(field, PAIR - HEAD_DIM // 2, 1),
        pltpu.roll(field, HEAD_DIM // 2, 1),
    )


def table_row(piece):
    prompt_pieces = PROMPT // PIECE
    cont_pieces = CONT // PIECE
    return jnp.where(
        piece < prompt_pieces,
        piece,
        prompt_pieces + lax.rem(jnp.maximum(piece - prompt_pieces, 0), cont_pieces),
    )


def head_tiles(pair, index_ref, total, run_tile):
    side = index_ref[total // PIECE]
    own = pair < 2
    for tile in range(PROMPT // TILE):
        mine = side == (0 if tile % 4 in (0, 3) else 1)

        @pl.when(own)
        def _(tile=tile):
            run_tile(tile * TILE, tile * TILE, (0, 1))

        @pl.when(jnp.logical_and(jnp.logical_not(own), mine))
        def _(tile=tile):
            run_tile(tile * TILE, tile * TILE, (0,))

    later = (total - PROMPT) // TILE

    def body(step, carry):
        mine = (step * 2 >= later).astype(jnp.int32) == side
        start = pl.multiple_of(PROMPT + step * TILE, TILE)

        @pl.when(own)
        def _():
            run_tile(start, PROMPT, (0, 1))

        @pl.when(jnp.logical_and(jnp.logical_not(own), mine))
        def _():
            run_tile(start, PROMPT, (0,))

        return carry

    lax.fori_loop(0, later, body, 0)


def lanes_of(head, shape):
    lane = lax.broadcasted_iota(jnp.int32, shape, 1)
    return lane < HEAD_DIM if head == 0 else lane >= HEAD_DIM


def nt_dot(left, right):
    return lax.dot_general(left, right, (((1,), (1,)), ((), ())), preferred_element_type=F32)


def tn_dot(left, right):
    return lax.dot_general(left, right, (((0,), (0,)), ((), ())), preferred_element_type=F32)


def nn_dot(left, right):
    return lax.dot_general(left, right, (((1,), (0,)), ((), ())), preferred_element_type=F32)


def attend_kernel(index_ref, raw_ref, cos_ref, sin_ref, out_ref, kept_ref, mixed):
    total = out_ref.shape[0]
    pieces = total // PIECE
    pair = pl.program_id(0)

    def rope(field, row):
        cosine = cos_ref[pl.ds(row, PIECE), :]
        sine = sin_ref[pl.ds(row, PIECE), :]
        return field * cosine + turn(field) * sine

    @pl.when(pair < 2)
    def _():
        def body(piece, carry):
            source = pl.multiple_of(index_ref[piece], PIECE)
            row = pl.multiple_of(table_row(piece) * PIECE, PIECE)
            target = pl.ds(pl.multiple_of(piece * PIECE, PIECE), PIECE)
            query = rope(raw_ref[pl.ds(source, PIECE), 0:PAIR], row)
            key = rope(raw_ref[pl.ds(source, PIECE), PAIR : 2 * PAIR], row)
            value = raw_ref[pl.ds(source, PIECE), 2 * PAIR : 3 * PAIR]
            kept_ref[0, target, 0:PAIR] = query.astype(BF)
            kept_ref[0, target, PAIR : 2 * PAIR] = key.astype(BF)
            kept_ref[0, target, 2 * PAIR : 3 * PAIR] = value.astype(BF)
            return carry

        lax.fori_loop(0, pieces, body, 0)

    @pl.when(pair == 2)
    def _():
        def body(piece, carry):
            source = pl.multiple_of(index_ref[piece], PIECE)
            row = pl.multiple_of(table_row(piece) * PIECE, PIECE)
            target = pl.ds(pl.multiple_of(piece * PIECE, PIECE), PIECE)
            both = rope(raw_ref[pl.ds(source, PIECE), 0:PAIR], row)
            value = raw_ref[pl.ds(source, PIECE), PAIR : 2 * PAIR]
            low = lanes_of(0, both.shape)
            kept_ref[0, target, 0:PAIR] = jnp.where(low, both, 0.0).astype(BF)
            kept_ref[0, target, PAIR : 2 * PAIR] = jnp.where(
                low, pltpu.roll(both, HEAD_DIM, 1), 0.0
            ).astype(BF)
            kept_ref[0, target, 2 * PAIR : 3 * PAIR] = jnp.where(low, value, 0.0).astype(BF)
            return carry

        lax.fori_loop(0, pieces, body, 0)

    mixed[...] = jnp.zeros_like(mixed)
    scale = 1.0 / math.sqrt(HEAD_DIM)

    def run_tile(start, prefix, heads):
        rows = pl.ds(start, TILE)
        query = kept_ref[0, rows, 0:PAIR].astype(F32) * scale
        masks = [lanes_of(head, query.shape) for head in heads]
        queries = [jnp.where(mask, query, 0.0).astype(BF) for mask in masks]
        seen = lax.broadcasted_iota(jnp.int32, (TILE, TILE), 1) <= lax.broadcasted_iota(
            jnp.int32, (TILE, TILE), 0
        )
        keys = [kept_ref[0, rows, PAIR : 2 * PAIR]]
        values = [kept_ref[0, rows, 2 * PAIR : 3 * PAIR]]
        if prefix:
            keys.append(kept_ref[0, 0:prefix, PAIR : 2 * PAIR])
            values.append(kept_ref[0, 0:prefix, 2 * PAIR : 3 * PAIR])
        scores = [[nt_dot(query, key) for key in keys] for query in queries]
        total_out = mixed[rows, :]
        for mask, parts in zip(masks, scores):
            parts[0] = jnp.where(seen, parts[0], NEGATIVE)
            peak = functools.reduce(
                jnp.maximum, [jnp.max(part, axis=1, keepdims=True) for part in parts]
            )
            parts = [jnp.exp(part - peak) for part in parts]
            count = sum(jnp.sum(part, axis=1, keepdims=True) for part in parts)
            out = sum(nn_dot(part.astype(BF), value) for part, value in zip(parts, values))
            total_out = jnp.where(mask, out / count, total_out)
        mixed[rows, :] = total_out

    head_tiles(pair, index_ref, total, run_tile)

    def back(piece, carry):
        source = pl.multiple_of(index_ref[piece], PIECE)
        target = pl.ds(pl.multiple_of(piece * PIECE, PIECE), PIECE)
        out_ref[pl.ds(source, PIECE), :] = mixed[target, :].astype(BF)
        return carry

    lax.fori_loop(0, pieces, back, 0)


def attend(index, raw, cosine, sine):
    total = raw.shape[0]
    return pl.pallas_call(
        attend_kernel,
        grid_spec=pltpu.PrefetchScalarGridSpec(
            num_scalar_prefetch=1,
            grid=(3,),
            in_specs=[
                pl.BlockSpec((total, SLAB), lambda j, index: (0, j)),
                pl.BlockSpec(cosine.shape, lambda j, index: (0, 0)),
                pl.BlockSpec(sine.shape, lambda j, index: (0, 0)),
            ],
            out_specs=[
                pl.BlockSpec((total, PAIR), lambda j, index: (0, j)),
                pl.BlockSpec((1, total, SLAB), lambda j, index: (j, 0, 0)),
            ],
            scratch_shapes=[pltpu.VMEM((total, PAIR), F32)],
        ),
        out_shape=[
            jax.ShapeDtypeStruct((total, 3 * PAIR), BF),
            jax.ShapeDtypeStruct((3, total, SLAB), BF),
        ],
        compiler_params=pltpu.CompilerParams(vmem_limit_bytes=40 << 20),
        cost_estimate=pl.CostEstimate(
            flops=36 * 10**9, bytes_accessed=1 << 20, transcendentals=0
        ),
        name="attend",
    )(index, raw, cosine, sine)


def attend_back_kernel(
    first, index_ref, kept_ref, outer_ref, cos_ref, sin_ref, grad_ref, outer, grad_q, grad_k, grad_v
):
    total = outer.shape[0]
    pieces = total // PIECE
    pair = pl.program_id(0) + first

    def sort(piece, carry):
        source = pl.multiple_of(index_ref[piece], PIECE)
        target = pl.ds(pl.multiple_of(piece * PIECE, PIECE), PIECE)
        outer[target, :] = outer_ref[pl.ds(source, PIECE), :]
        return carry

    lax.fori_loop(0, pieces, sort, 0)
    grad_q[...] = jnp.zeros_like(grad_q)
    grad_k[...] = jnp.zeros_like(grad_k)
    grad_v[...] = jnp.zeros_like(grad_v)
    scale = 1.0 / math.sqrt(HEAD_DIM)

    def run_tile(start, prefix, heads):
        rows = pl.ds(start, TILE)
        query = kept_ref[0, rows, 0:PAIR].astype(F32) * scale
        away = outer[rows, :].astype(F32)
        masks = [lanes_of(head, query.shape) for head in heads]
        queries = [jnp.where(mask, query, 0.0).astype(BF) for mask in masks]
        aways = [jnp.where(mask, away, 0.0).astype(BF) for mask in masks]
        seen = lax.broadcasted_iota(jnp.int32, (TILE, TILE), 0) <= lax.broadcasted_iota(
            jnp.int32, (TILE, TILE), 1
        )
        spans = [rows] + ([pl.ds(0, prefix)] if prefix else [])
        keys = [kept_ref[0, span, PAIR : 2 * PAIR] for span in spans]
        values = [kept_ref[0, span, 2 * PAIR : 3 * PAIR] for span in spans]
        scores = [[nt_dot(key, query) for key in keys] for query in queries]
        pulls = [[nt_dot(value, away) for value in values] for away in aways]
        probs, slopes = [], []
        for parts, pull in zip(scores, pulls):
            parts[0] = jnp.where(seen, parts[0], NEGATIVE)
            peak = functools.reduce(
                jnp.maximum, [jnp.max(part, axis=0, keepdims=True) for part in parts]
            )
            parts = [jnp.exp(part - peak) for part in parts]
            inverse = 1.0 / sum(jnp.sum(part, axis=0, keepdims=True) for part in parts)
            parts = [part * inverse for part in parts]
            delta = sum(jnp.sum(p * q, axis=0, keepdims=True) for p, q in zip(parts, pull))
            probs.append([part.astype(BF) for part in parts])
            slopes.append([(p * (q - delta)).astype(BF) for p, q in zip(parts, pull)])
        for i, span in enumerate(spans):
            grad_v[span, :] += sum(nn_dot(prob[i], away) for prob, away in zip(probs, aways))
            grad_k[span, :] += sum(nn_dot(slope[i], query) for slope, query in zip(slopes, queries))
        part_q = grad_q[rows, :]
        for mask, slope in zip(masks, slopes):
            part = sum(tn_dot(piece, key) for piece, key in zip(slope, keys))
            part_q = jnp.where(mask, part * scale, part_q)
        grad_q[rows, :] = part_q

    head_tiles(pair, index_ref, total, run_tile)

    def unrope(field, row):
        cosine = cos_ref[pl.ds(row, PIECE), :]
        sine = sin_ref[pl.ds(row, PIECE), :]
        return field * cosine - turn(field) * sine

    @pl.when(pair < 2)
    def _():
        def back(piece, carry):
            source = pl.ds(pl.multiple_of(index_ref[piece], PIECE), PIECE)
            row = pl.multiple_of(table_row(piece) * PIECE, PIECE)
            here = pl.ds(pl.multiple_of(piece * PIECE, PIECE), PIECE)
            grad_ref[source, 0:PAIR] = unrope(grad_q[here, :], row).astype(BF)
            grad_ref[source, PAIR : 2 * PAIR] = unrope(grad_k[here, :], row).astype(BF)
            grad_ref[source, 2 * PAIR : 3 * PAIR] = grad_v[here, :].astype(BF)
            return carry

        lax.fori_loop(0, pieces, back, 0)

    @pl.when(pair == 2)
    def _():
        def back(piece, carry):
            source = pl.ds(pl.multiple_of(index_ref[piece], PIECE), PIECE)
            row = pl.multiple_of(table_row(piece) * PIECE, PIECE)
            here = pl.ds(pl.multiple_of(piece * PIECE, PIECE), PIECE)
            low = lanes_of(0, (PIECE, PAIR))
            both = jnp.where(low, grad_q[here, :], pltpu.roll(grad_k[here, :], HEAD_DIM, 1))
            grad_ref[source, 0:PAIR] = unrope(both, row).astype(BF)
            grad_ref[source, PAIR : 2 * PAIR] = grad_v[here, :].astype(BF)
            grad_ref[source, 2 * PAIR : 3 * PAIR] = jnp.zeros((PIECE, PAIR), BF)
            return carry

        lax.fori_loop(0, pieces, back, 0)


def attend_back(first, count, index, kept, outer, cosine, sine, columns):
    total = outer.shape[0]
    return pl.pallas_call(
        functools.partial(attend_back_kernel, first),
        grid_spec=pltpu.PrefetchScalarGridSpec(
            num_scalar_prefetch=1,
            grid=(count,),
            in_specs=[
                pl.BlockSpec((1, total, SLAB), lambda j, index: (j + first, 0, 0)),
                pl.BlockSpec((total, PAIR), lambda j, index: (0, j + first)),
                pl.BlockSpec(cosine.shape, lambda j, index: (0, 0)),
                pl.BlockSpec(sine.shape, lambda j, index: (0, 0)),
            ],
            out_specs=pl.BlockSpec((total, SLAB), lambda j, index: (0, j)),
            scratch_shapes=[
                pltpu.VMEM((total, PAIR), BF),
                pltpu.VMEM((total, PAIR), F32),
                pltpu.VMEM((total, PAIR), F32),
                pltpu.VMEM((total, PAIR), F32),
            ],
        ),
        out_shape=jax.ShapeDtypeStruct((total, columns), BF),
        compiler_params=pltpu.CompilerParams(vmem_limit_bytes=48 << 20),
        cost_estimate=pl.CostEstimate(
            flops=0, bytes_accessed=1 << 20, transcendentals=0
        ),
        name="attend_back",
    )(index, kept, outer, cosine, sine)


def after(array, *earlier):
    leaves = [array] + jax.tree.leaves(earlier)
    place = pl.BlockSpec(memory_space=pl.ANY)
    return pl.pallas_call(
        lambda *refs: None,
        in_specs=[place] * len(leaves),
        out_specs=place,
        out_shape=jax.ShapeDtypeStruct(array.shape, array.dtype),
        input_output_aliases={0: 0},
        name="after",
    )(*leaves)


def make_layered(mesh):
    n_grp, n_tok, n_fs = (mesh.shape[axis] for axis in ALL)

    def device(grp, tok, fs):
        return (grp * n_tok + tok) * n_fs + fs

    def permutation(move):
        return [
            (device(g, t, f), device(*move(g, t, f)))
            for g in range(n_grp)
            for t in range(n_tok)
            for f in range(n_fs)
        ]

    def send(array, move):
        return lax.ppermute(array, ALL, permutation(move))

    def cross(step):
        return lambda g, t, f: (g ^ step, t, f)

    def sibling(g, t, f):
        return (g, t, 1 - f)

    def local(
        hidden_in,
        cotangent,
        block_start,
        query_weight,
        key_weight,
        value_weight,
        output_weight,
        gate_weight,
        up_weight,
        down_weight,
        first_gain,
        second_gain,
    ):
        rows, width = hidden_in.shape
        ff_width = gate_weight.shape[1]
        g, t, f = (lax.axis_index(axis) for axis in ALL)
        even = f == 0
        ranks = n_grp * n_fs
        total = rows * ranks
        quarter = rows // n_grp


        def spread_in(array):
            return lax.all_to_all(array.reshape(n_grp, quarter, width), "grp", 0, 0, tiled=True)

        def shuffle_in(parts):
            return lax.all_to_all(parts, "tok", 0, 0, tiled=True).reshape(rows, width)

        def shuffle_out(arrays, beside):
            parts = [array.reshape(n_tok, quarter, width) for array in arrays]
            results = [jnp.zeros_like(part) for part in parts]
            for turn_by in range(n_grp):
                away = g ^ t ^ turn_by
                pieces = [lax.dynamic_index_in_dim(part, away, 0, keepdims=True) for part in parts]
                piece = send(
                    jnp.concatenate(pieces, axis=1),
                    lambda g, t, f, turn_by=turn_by: (t, g ^ t ^ turn_by, f),
                )
                piece = after(piece, beside)
                for i, result in enumerate(results):
                    results[i] = lax.dynamic_update_slice_in_dim(
                        result, piece[:, i * quarter : (i + 1) * quarter], away, 0
                    )
            return [result.reshape(rows, width) for result in results]


        def layer_pieces(array):
            half = array.shape[0] // 2
            by_x = send(array, cross(1))
            by_y = send(array, cross(2))
            return array, by_x, by_y, send(by_x[:half], cross(2)), send(by_y[half:], cross(1))

        def layer_join(array, by_x, by_y, *by_xy):
            mine = [array, by_x, by_y, jnp.concatenate(by_xy, axis=0)]
            return jnp.concatenate(mine + [send(part, sibling) for part in mine], axis=0)

        def layer_gather(array):
            return layer_join(*layer_pieces(array))

        def pair_sum(rows_of):
            away = rows_of(1).astype(BF).reshape(n_grp, rows, -1)
            away = {step: send(away[step], sibling) for step in (3, 1, 2, 0)}
            here = rows_of(0).reshape(n_grp, rows, -1)
            parts = [(here[step] + away[step].astype(F32)).astype(BF) for step in (3, 1, 2)]
            return here[0], away[0], parts

        def layer_send(sums, *earlier):
            here, away, parts = sums
            if earlier:
                parts = [after(part, *earlier) for part in parts]
            return here, away, [send(part, cross(step)) for part, step in zip(parts, (3, 1, 2))]

        def layer_add(parts, beside=None):
            here, away, got = parts
            if beside is not None:
                got = [after(part, beside) for part in got]
            return here + away.astype(F32) + sum(part.astype(F32) for part in got)

        def layer_sum(rows_of, beside=None):
            return layer_add(layer_send(pair_sum(rows_of)), beside)

        def halves(*arrays):
            half = arrays[0].shape[0] // 2
            return lambda which: [array[which * half : (which + 1) * half] for array in arrays]

        extra = 8
        gains_here = jnp.concatenate([first_gain, second_gain])
        span = gains_here.shape[0]
        gains_here = jnp.pad(gains_here[None, :], ((0, extra - 1), (0, width - span)))
        hidden_parts = spread_in(hidden_in)
        cotangent_parts = spread_in(after(cotangent, hidden_parts))
        arrived = lax.all_to_all(
            jnp.concatenate(
                [hidden_parts, jnp.broadcast_to(gains_here[None], (n_tok, extra, width))], axis=1
            ),
            "tok",
            0,
            0,
            tiled=True,
        )
        gains_mine = arrived[:, quarter, :span]
        gains_other = send(gains_mine, sibling)
        gains_all = jnp.stack(
            [jnp.where(even, gains_mine, gains_other), jnp.where(even, gains_other, gains_mine)],
            axis=1,
        ).astype(F32).reshape(n_tok * n_fs, 2, -1)
        gain_one = gains_all[:, 0].reshape(width)
        gain_two = gains_all[:, 1].reshape(width)
        starts = send(block_start, lambda g, t, f: (t, g, f))[0]
        xs = arrived[:, :quarter].reshape(rows, width)
        cotangent_here = shuffle_in(after(cotangent_parts, xs))


        head_span = width // n_grp
        own_span = 4 * HEAD_DIM

        def rank_columns(side):
            picked = [
                lax.dynamic_slice_in_dim(weight, g * head_span, head_span, 1)
                for weight in (query_weight, key_weight, value_weight)
            ]
            first = side * (own_span + HEAD_DIM)
            spans = [(first, PAIR), (first + PAIR, PAIR), (own_span, HEAD_DIM)]
            columns = [weight[:, at : at + size] for at, size in spans for weight in picked]
            wide = sum(part.shape[1] for part in columns)
            columns.append(jnp.zeros((query_weight.shape[0], -wide % PAIR), BF))
            return jnp.concatenate(columns, axis=1)

        def pair_rows(zero_block, one_block):
            mine = jnp.where(even, zero_block, one_block)
            other = send(jnp.where(even, one_block, zero_block), sibling)
            return jnp.concatenate(
                [jnp.where(even, mine, other), jnp.where(even, other, mine)], axis=0
            )

        def gather_rows(array, *earlier):
            array = after(array, *earlier)
            return array, lax.all_gather(array, "tok", axis=0, tiled=True)

        turn_one, qkv_weight = gather_rows(
            pair_rows(rank_columns(0), rank_columns(1)), xs
        )
        ff_piece = ff_width // (ranks * n_tok)
        ff_tall = -(-ff_piece // 64) * 64
        ff_wide = ff_tall * n_tok

        def ff_columns(side):
            parts = [
                lax.dynamic_slice_in_dim(
                    weight, (step * n_fs + side) * n_grp * ff_piece + g * ff_piece, ff_piece, 1
                )
                for weight in (gate_weight, up_weight)
                for step in range(n_tok)
            ]
            zeros = jnp.zeros((gate_weight.shape[0], ff_tall - ff_piece), BF)
            return jnp.concatenate([item for part in parts for item in (part, zeros)], axis=1)

        ff_inputs = (
            pair_rows(ff_columns(0), ff_columns(1)),
            jnp.pad(
                lax.dynamic_slice_in_dim(down_weight, g * ff_piece, ff_piece, 0),
                ((0, ff_tall - ff_piece), (0, 0)),
            ),
        )

        hidden = after(xs, *ff_inputs).astype(F32)
        scale_one = lax.rsqrt(jnp.mean(hidden * hidden, axis=1, keepdims=True) + EPS)
        normed_one = hidden * scale_one
        h_one = layer_gather((normed_one * gain_one[None, :]).astype(BF))
        out_rows = output_weight.shape[0] // n_grp
        turn_two, out_weight = gather_rows(
            lax.dynamic_slice_in_dim(output_weight, g * out_rows, out_rows, 0), turn_one, h_one
        )
        grad_out = cotangent_here.astype(F32)
        grad_m_pieces = layer_pieces(after((RESIDUAL * grad_out).astype(BF), h_one))
        grad_m = layer_join(*grad_m_pieces)
        raw = nn_dot(after(h_one, *grad_m_pieces[1:3]), qkv_weight)
        out_weight = lax.all_to_all(after(out_weight, raw), "grp", 0, 0, tiled=True)
        half_head = HEAD_DIM // 2
        swapped = send(
            jnp.where(even, out_weight[own_span:], out_weight[:half_head]), sibling
        )
        out_weight = jnp.concatenate(
            [
                jnp.where(even, out_weight[:own_span], out_weight[half_head:]),
                jnp.where(even, out_weight[own_span:], swapped),
                jnp.where(even, swapped, out_weight[:half_head]),
                jnp.zeros((HEAD_DIM, width), BF),
            ],
            axis=0,
        )

        _, ff_weight = gather_rows(ff_inputs[0], turn_two)
        _, down_w = gather_rows(ff_inputs[1], ff_inputs[0], turn_two)


        number = jnp.arange(total // BLOCK, dtype=jnp.int32)
        prompt_blocks = PROMPT // BLOCK
        cont_blocks = CONT // BLOCK
        place = jnp.where(
            number < prompt_blocks,
            starts // BLOCK,
            prompt_blocks
            + (number - prompt_blocks) // cont_blocks * cont_blocks
            + (starts - PROMPT) // BLOCK,
        )
        order = jnp.sum(
            jnp.where(place[None, :] == number[:, None], number[None, :], 0), axis=1
        )
        pieces = (
            order[:, None] * (BLOCK // PIECE) + jnp.arange(BLOCK // PIECE, dtype=jnp.int32)
        ).reshape(-1)
        from_t = pieces // ranks
        from_f = pieces // n_grp % n_fs
        from_g = pieces % n_grp
        index = jnp.concatenate(
            [
                (((from_f ^ f) * n_grp + (from_g ^ g)) * n_tok + from_t) * PIECE,
                f[None].astype(jnp.int32),
            ]
        ).astype(jnp.int32)
        lane = jnp.arange(PAIR, dtype=jnp.int32)
        half_head_lane = lane % (HEAD_DIM // 2)
        freq = 10000.0 ** (-(half_head_lane.astype(F32) * 2.0) / HEAD_DIM)
        angle = jnp.arange(PROMPT + CONT, dtype=F32)[:, None] * freq[None, :]
        cosine = jnp.cos(angle)
        sine = jnp.where(lane[None, :] % HEAD_DIM < HEAD_DIM // 2, -jnp.sin(angle), jnp.sin(angle))


        attn_out, kept = attend(index, raw, cosine, sine)
        pick = halves(attn_out)
        branch = layer_sum(lambda side, pick=pick: nn_dot(pick(side)[0], out_weight), grad_m)
        second_in = hidden + RESIDUAL * branch
        scale_two = lax.rsqrt(jnp.mean(second_in * second_in, axis=1, keepdims=True) + EPS)
        normed_two = second_in * scale_two
        h_two = layer_gather((normed_two * gain_two[None, :]).astype(BF))
        both = nn_dot(h_two, ff_weight)
        gate = both[:, :ff_wide]
        up_val = both[:, ff_wide:]
        sigma = jax.nn.sigmoid(gate)
        silu = gate * sigma
        act = (silu * up_val).astype(BF)


        down_local = tn_dot(act, grad_m).astype(BF).reshape(n_tok, ff_tall, width)
        grad_act = nt_dot(after(grad_m, down_local), down_w)
        grad_gate = (grad_act * up_val * (sigma * (1.0 + gate * (1.0 - sigma)))).astype(BF)
        grad_up = (grad_act * silu).astype(BF)

        def spread_rows(grad):
            columns = grad.shape[1]
            grad = grad.astype(BF).reshape(n_grp, n_tok, width // (n_grp * n_tok), columns)
            return grad.transpose(1, 0, 2, 3).reshape(n_tok, width // n_tok, columns)

        def sum_rows(grad):
            grad = lax.psum_scatter(grad, "tok", scatter_dimension=0, tiled=True)
            return grad.reshape(ranks, width // (ranks * n_tok), grad.shape[2])

        def to_owners(grad, weight, spare):
            weight = weight.reshape(n_grp, n_tok, width // (n_grp * n_tok), grad.shape[2])
            weight = lax.dynamic_index_in_dim(weight, t, 1, keepdims=False).reshape(grad.shape)
            total = jnp.sum(grad.astype(F32) * weight.astype(F32), axis=2, keepdims=True)
            high = total.astype(BF)
            low = (total - high.astype(F32)).astype(BF)
            column = lax.broadcasted_iota(jnp.int32, grad.shape, 2)
            grad = jnp.where(column == spare, high, jnp.where(column == spare + 1, low, grad))
            return lax.all_to_all(grad, LAYER, 0, 0, tiled=True)

        def gain_of(got, spare):
            return jnp.sum(got[..., spare : spare + 2].astype(F32), axis=(0, 2))

        pick = halves(grad_gate, grad_up)
        parts = layer_send(
            pair_sum(
                lambda side, pick=pick: nt_dot(pick(side)[0], ff_weight[:, :ff_wide])
                + nt_dot(pick(side)[1], ff_weight[:, ff_wide:])
            )
        )
        ff_local = spread_rows(
            tn_dot(
                h_two,
                jnp.concatenate([after(grad_gate, parts[0]), after(grad_up, parts[0])], axis=1),
            )
        )
        grad_h2 = layer_add(parts, ff_local)
        ff_rows = sum_rows(ff_local)
        pulled = grad_h2 * gain_two[None, :]
        grad_second = (
            grad_out
            + scale_two * pulled
            - scale_two**3 * second_in * jnp.mean(pulled * second_in, axis=1, keepdims=True)
        )
        grad_z_here = (RESIDUAL * grad_second).astype(BF)
        down_rows = lax.psum_scatter(down_local, "tok", scatter_dimension=0, tiled=True)
        down_rows = down_rows[0, :ff_piece]
        grad_z = layer_gather(grad_z_here)
        pick = halves(after(act, grad_z_here))
        feed_sums = pair_sum(lambda side, pick=pick: nn_dot(pick(side)[0], down_w))
        grad_attn = nt_dot(grad_z, out_weight).astype(BF)
        feed_parts = layer_send(feed_sums, grad_z)
        out_full = tn_dot(attn_out, grad_z)
        shared = out_full[own_span : own_span + HEAD_DIM]
        swapped = send(
            jnp.where(even, shared[half_head:], shared[:half_head]).astype(BF), sibling
        ).astype(F32)
        kept_half = jnp.where(even, shared[:half_head], shared[half_head:]) + swapped
        out_full = jnp.where(
            even,
            jnp.concatenate([out_full[:own_span], kept_half], axis=0),
            jnp.concatenate([kept_half, out_full[:own_span]], axis=0),
        )
        out_full = out_full.astype(BF).reshape(n_tok, -1, width)
        output_grad = lax.psum_scatter(out_full, "tok", scatter_dimension=0, tiled=True)

        grad_attn = after(grad_attn, out_full, down_rows, feed_parts[0])
        grads = attend_back(0, 3, index, kept, grad_attn, cosine, sine, qkv_weight.shape[1])
        grads = after(grads, ff_rows, *feed_parts[2])
        qkv_local = spread_rows(tn_dot(h_one, grads))
        qkv_rows = sum_rows(qkv_local)
        ff_got = to_owners(after(ff_rows, grads), ff_weight, ff_piece)
        pick = halves(after(grads, qkv_local, output_grad, ff_got))
        parts = layer_send(pair_sum(lambda side, pick=pick: nt_dot(pick(side)[0], qkv_weight)))
        feed = layer_add(feed_parts, parts[2][1])
        layer_output = (second_in + RESIDUAL * feed).astype(BF)
        grad_h1 = layer_add(parts)
        pulled = grad_h1 * gain_one[None, :]
        input_grad = (
            grad_second
            + scale_one * pulled
            - scale_one**3 * hidden * jnp.mean(pulled * hidden, axis=1, keepdims=True)
        )
        input_grad = input_grad.astype(BF)
        input_grad = after(input_grad, qkv_rows)
        used = 5 * 3 * HEAD_DIM
        got = to_owners(qkv_rows, qkv_weight, used)
        down_grad = send(
            after(down_rows, got),
            lambda g, t, f: (t, (n_grp * f + g) // n_fs, (n_grp * f + g) % n_fs),
        )
        output_grad = send(
            after(output_grad[0], got),
            lambda g, t, f: (g, (n_tok * f + t) // n_fs, (n_tok * f + t) % n_fs),
        )
        gain_one_grad = gain_of(got, used)
        ff_got = after(ff_got, got)
        gain_two_grad = gain_of(ff_got, ff_piece)
        wide = ff_got.reshape(n_grp, n_fs, -1, 2, n_tok, ff_tall)
        gate_grad, up_grad = (
            wide[:, :, :, which, :, :ff_piece]
            .transpose(2, 3, 1, 0, 4)
            .reshape(-1, ff_width)
            .astype(F32)
            for which in range(2)
        )
        own_rows = got.shape[1]
        here = got.astype(F32).reshape(n_grp, n_fs, own_rows, got.shape[2])

        def projection_grad(which):
            def own(side):
                return [
                    here[:, side, :, SLAB * pair + PAIR * which : SLAB * pair + PAIR * (which + 1)]
                    for pair in range(2)
                ]

            at = 2 * SLAB + HEAD_DIM * which
            shared = here[:, 0, :, at : at + HEAD_DIM] + here[:, 1, :, at : at + HEAD_DIM]
            whole = jnp.concatenate(own(0) + [shared] + own(1), axis=2)
            return whole.transpose(1, 0, 2).reshape(own_rows, width)

        qkv_grads = [projection_grad(which) for which in range(3)]
        layer_output, input_grad = shuffle_out((layer_output, input_grad), (qkv_grads, gate_grad, up_grad))
        input_grad = input_grad.astype(F32)
        mine = ((g * n_tok + t) * n_fs + f) * own_rows
        gain_one_grad = gain_one_grad / lax.dynamic_slice_in_dim(gain_one, mine, own_rows)
        gain_two_grad = gain_two_grad / lax.dynamic_slice_in_dim(gain_two, mine, own_rows)
        return (
            layer_output,
            input_grad,
            *qkv_grads,
            output_grad.astype(F32),
            gate_grad,
            up_grad,
            down_grad.astype(F32),
            gain_one_grad,
            gain_two_grad,
        )

    return local


def spread(block, axis, source):
    block = jnp.where(lax.axis_index(axis) == source, block, jnp.zeros_like(block))
    return lax.psum(block, axis)


def rope_tables(positions, head_size):
    half = head_size // 2
    freq = 10000.0 ** (-(jnp.arange(half, dtype=jnp.float32) * 2.0) / head_size)
    angle = positions.astype(jnp.float32)[:, None] * freq[None, :]
    return (jnp.cos(angle)[:, None, :], jnp.sin(angle)[:, None, :])


def rotate(field, cosine, sine):
    half = field.shape[-1] // 2
    first = field[..., :half]
    second = field[..., half:]
    return jnp.concatenate(
        [first * cosine - second * sine, second * cosine + first * sine], axis=-1
    )


def unrotate(grad, cosine, sine):
    half = grad.shape[-1] // 2
    first = grad[..., :half]
    second = grad[..., half:]
    return jnp.concatenate(
        [first * cosine + second * sine, second * cosine - first * sine], axis=-1
    )


def row_norm(values):
    return values * lax.rsqrt(jnp.mean(values * values, axis=-1, keepdims=True) + EPS)


def swish_product(gate, up_val):
    return jax.nn.silu(gate) * up_val


def contract_rows(left, right):
    return lax.dot_general(
        left, right, (((0,), (0,)), ((), ())), preferred_element_type=jnp.float32
    )


def contract_cols(left, right):
    return lax.dot_general(
        left, right, (((1,), (1,)), ((), ())), preferred_element_type=jnp.float32
    )


def weight_sums(left, right):
    return lax.psum_scatter(
        contract_rows(left, right), ("grp", "tok", "fs"), scatter_dimension=0, tiled=True
    )


def spread_local(
    hidden_in,
    cotangent,
    block_start,
    query_weight,
    key_weight,
    value_weight,
    output_weight,
    gate_weight,
    up_weight,
    down_weight,
    first_gain,
    second_gain,
):
    local_rows, width = hidden_in.shape
    ff_width = gate_weight.shape[1]
    head_size = HEAD_DIM
    heads = width // head_size
    group_width = GROUP_HEADS * head_size
    group_count = heads // GROUP_HEADS
    scale = 1.0 / math.sqrt(head_size)
    device = lax.axis_index(("tok", "fs"))
    holders = -(-PROMPT // local_rows)
    prompt_rows = holders * local_rows
    starts = block_start[0]
    offsets = jnp.arange(BLOCK, dtype=jnp.int32)
    local_starts = lax.dynamic_slice_in_dim(
        starts, device * (local_rows // BLOCK), local_rows // BLOCK
    )
    my_pos = (local_starts[:, None] + offsets[None, :]).reshape(local_rows)
    prompt_pos = (starts[: prompt_rows // BLOCK][:, None] + offsets[None, :]).reshape(prompt_rows)
    my_row = device * local_rows + jnp.arange(local_rows, dtype=jnp.int32)
    my_seg = jnp.where(my_row < PROMPT, 0, 1 + (my_row - PROMPT) // CONT)
    prompt_row = jnp.arange(prompt_rows, dtype=jnp.int32)
    prompt_seen = (prompt_row[None, :] < PROMPT) & (prompt_pos[None, :] <= my_pos[:, None])
    local_seen = (
        (my_seg[None, :] == my_seg[:, None])
        & (my_seg[None, :] > 0)
        & (my_pos[None, :] <= my_pos[:, None])
    )
    visible = jnp.concatenate([prompt_seen, local_seen], axis=1)
    cosine, sine = rope_tables(my_pos, head_size)
    hidden = hidden_in.astype(jnp.float32)
    normed_one, pull_one = jax.vjp(row_norm, hidden)
    zero_rows = jnp.zeros((local_rows, width), jnp.float32)
    pieces = (
        lax.all_gather(query_weight, ("tok", "fs"), axis=0, tiled=True),
        lax.all_gather(key_weight, ("tok", "fs"), axis=0, tiled=True),
        lax.all_gather(value_weight, ("tok", "fs"), axis=0, tiled=True),
        lax.all_gather(first_gain, ("tok", "fs"), axis=0, tiled=True),
    )
    normed = normed_one
    scaled = (normed * pieces[3].astype(jnp.float32)[None, :]).astype(jnp.bfloat16)
    kept = scaled
    query_acc = jnp.dot(scaled, pieces[0], preferred_element_type=jnp.float32)
    key_acc = jnp.dot(scaled, pieces[1], preferred_element_type=jnp.float32)
    value_acc = jnp.dot(scaled, pieces[2], preferred_element_type=jnp.float32)
    kept_one = kept
    queries = (
        rotate(query_acc.reshape(local_rows, heads, head_size), cosine, sine)
        .astype(jnp.bfloat16)
        .reshape(local_rows, width)
    )
    keys = (
        rotate(key_acc.reshape(local_rows, heads, head_size), cosine, sine)
        .astype(jnp.bfloat16)
        .reshape(local_rows, width)
    )
    values = value_acc.astype(jnp.bfloat16)
    paired = jnp.stack([keys, values])
    received = []
    for root in range(holders):
        received.append(spread(paired, ("tok", "fs"), root))
    gathered = jnp.concatenate(received, axis=1)
    all_keys = jnp.concatenate([gathered[0], keys], axis=0)
    all_values = jnp.concatenate([gathered[1], values], axis=0)
    total_keys = all_keys.shape[0]

    def head_slice(array, index):
        return lax.dynamic_slice_in_dim(array, index * group_width, group_width, 1).reshape(
            array.shape[0], GROUP_HEADS, head_size
        )

    def scores_of(index):
        raw = (
            jnp.einsum(
                "qhd,khd->hqk",
                head_slice(queries, index),
                head_slice(all_keys, index),
                preferred_element_type=jnp.float32,
            )
            * scale
        )
        return jnp.where(visible[None], raw, NEGATIVE)

    def attend_group(index, carry):
        mixed, peaks, totals = carry
        scores = scores_of(index)
        peak = jnp.max(scores, axis=-1, keepdims=True)
        expo = jnp.exp(scores - peak)
        total = jnp.sum(expo, axis=-1, keepdims=True)
        probs = (expo / total).astype(jnp.bfloat16)
        block_out = jnp.einsum(
            "hqk,khd->qhd", probs, head_slice(all_values, index), preferred_element_type=jnp.float32
        ).reshape(local_rows, group_width)
        mixed = lax.dynamic_update_slice_in_dim(mixed, block_out, index * group_width, 1)
        peaks = lax.dynamic_update_slice_in_dim(peaks, peak[None, :, :, 0], index, 0)
        totals = lax.dynamic_update_slice_in_dim(totals, total[None, :, :, 0], index, 0)
        return (mixed, peaks, totals)

    stats_zero = jnp.zeros((group_count, GROUP_HEADS, local_rows), jnp.float32)
    mixed, peaks, totals = lax.fori_loop(
        0, group_count, attend_group, (zero_rows, stats_zero, stats_zero)
    )
    attention_out = mixed.astype(jnp.bfloat16)
    branch = jnp.dot(
        attention_out,
        lax.all_gather(output_weight, ("tok", "fs"), axis=0, tiled=True),
        preferred_element_type=jnp.float32,
    )
    second_in = hidden + RESIDUAL * branch
    normed_two, pull_two = jax.vjp(row_norm, second_in)
    retained = ()
    pieces = (
        lax.all_gather(gate_weight, ("tok", "fs"), axis=0, tiled=True),
        lax.all_gather(up_weight, ("tok", "fs"), axis=0, tiled=True),
        lax.all_gather(second_gain, ("tok", "fs"), axis=0, tiled=True),
    )
    start = jnp.int32(0)
    stored = retained
    normed = normed_two
    scaled = (normed * pieces[2].astype(jnp.float32)[None, :]).astype(jnp.bfloat16)
    kept = scaled
    stored = tuple(
        (
            lax.dynamic_update_slice_in_dim(buffer, piece, start, 0)
            for buffer, piece in zip(stored, pieces)
        )
    )
    gate_acc, up_acc, kept_two, stored = (
        jnp.dot(scaled, pieces[0], preferred_element_type=jnp.float32),
        jnp.dot(scaled, pieces[1], preferred_element_type=jnp.float32),
        kept,
        stored,
    )
    swish, pull_swish = jax.vjp(swish_product, gate_acc, up_acc)
    act = swish.astype(jnp.bfloat16)
    down_store = ()
    piece = lax.all_gather(down_weight, ("tok", "fs"), axis=0, tiled=True)
    start = jnp.int32(0)
    stored_down = down_store
    total_acc = jnp.dot(act, piece, preferred_element_type=jnp.float32)
    stored_down = tuple(
        (lax.dynamic_update_slice_in_dim(buffer, piece, start, 0) for buffer in stored_down)
    )
    feed, stored_down = (total_acc, stored_down)
    layer_output = (second_in + RESIDUAL * feed).astype(jnp.bfloat16)
    grad_out = cotangent.astype(jnp.float32)
    grad_m = (RESIDUAL * grad_out).astype(jnp.bfloat16)
    grad_act = contract_cols(grad_m, lax.all_gather(down_weight, ("tok", "fs"), axis=0, tiled=True))
    down_grad = weight_sums(act, grad_m)
    grad_gate_f, grad_up_f = pull_swish(grad_act)
    grad_gate = grad_gate_f.astype(jnp.bfloat16)
    grad_up = grad_up_f.astype(jnp.bfloat16)
    pieces = (
        lax.all_gather(gate_weight, ("tok", "fs"), axis=0, tiled=True),
        lax.all_gather(up_weight, ("tok", "fs"), axis=0, tiled=True),
        lax.all_gather(second_gain, ("tok", "fs"), axis=0, tiled=True),
    )
    section = contract_cols(grad_gate, pieces[0]) + contract_cols(grad_up, pieces[1])
    normed = normed_two
    grad_normed = section * pieces[2].astype(jnp.float32)[None, :]
    gain_sum = jnp.sum(section * normed, axis=0)
    grad_n2 = grad_normed
    gain_two = gain_sum
    both_grads = jnp.concatenate([grad_gate, grad_up], axis=1)
    mixer_grad = weight_sums(kept_two, both_grads)
    grad_second = grad_out + pull_two(grad_n2)[0]
    grad_z = (RESIDUAL * grad_second).astype(jnp.bfloat16)
    output_full = contract_rows(attention_out, grad_z)
    grad_attn = contract_cols(
        grad_z, lax.all_gather(output_weight, ("tok", "fs"), axis=0, tiled=True)
    ).astype(jnp.bfloat16)

    def attend_back(index, carry):
        grad_q, grad_k, grad_v = carry
        query_g = head_slice(queries, index)
        key_g = head_slice(all_keys, index)
        value_g = head_slice(all_values, index)
        outer_g = head_slice(grad_attn, index)
        scores = scores_of(index)
        peak = lax.dynamic_index_in_dim(peaks, index, 0, keepdims=False)[:, :, None]
        total = lax.dynamic_index_in_dim(totals, index, 0, keepdims=False)[:, :, None]
        probs = jnp.exp(scores - peak) / total
        grad_probs = jnp.einsum(
            "qhd,khd->hqk", outer_g, value_g, preferred_element_type=jnp.float32
        )
        grad_scores = (
            probs * (grad_probs - jnp.sum(grad_probs * probs, axis=-1, keepdims=True))
        ).astype(jnp.bfloat16)
        query_part = (
            jnp.einsum("hqk,khd->qhd", grad_scores, key_g, preferred_element_type=jnp.float32)
            * scale
        )
        key_part = (
            jnp.einsum("hqk,qhd->khd", grad_scores, query_g, preferred_element_type=jnp.float32)
            * scale
        )
        value_part = jnp.einsum(
            "hqk,qhd->khd", probs.astype(jnp.bfloat16), outer_g, preferred_element_type=jnp.float32
        )
        grad_q = lax.dynamic_update_slice_in_dim(
            grad_q, query_part.reshape(local_rows, group_width), index * group_width, 1
        )
        grad_k = lax.dynamic_update_slice_in_dim(
            grad_k, key_part.reshape(total_keys, group_width), index * group_width, 1
        )
        grad_v = lax.dynamic_update_slice_in_dim(
            grad_v, value_part.reshape(total_keys, group_width), index * group_width, 1
        )
        return (grad_q, grad_k, grad_v)

    zero_keys = jnp.zeros((total_keys, width), jnp.float32)
    grad_q, grad_k, grad_v = lax.fori_loop(
        0, group_count, attend_back, (zero_rows, zero_keys, zero_keys)
    )
    share_k, share_v = (
        lax.psum_scatter(
            grad_k[:prompt_rows].astype(jnp.bfloat16),
            ("tok", "fs"),
            scatter_dimension=1,
            tiled=True,
        ).astype(jnp.float32),
        lax.psum_scatter(
            grad_v[:prompt_rows].astype(jnp.bfloat16),
            ("tok", "fs"),
            scatter_dimension=1,
            tiled=True,
        ).astype(jnp.float32),
    )
    prompt_dk, prompt_dv = (
        lax.all_gather(share_k.astype(jnp.bfloat16), ("tok", "fs"), axis=1, tiled=True).astype(
            share_k.dtype
        ),
        lax.all_gather(share_v.astype(jnp.bfloat16), ("tok", "fs"), axis=1, tiled=True).astype(
            share_v.dtype
        ),
    )
    holder = jnp.minimum(device, holders - 1)
    owned = device < holders
    mine_k = (
        jnp.where(
            owned, lax.dynamic_slice_in_dim(prompt_dk, holder * local_rows, local_rows, 0), 0.0
        )
        + grad_k[prompt_rows:]
    )
    mine_v = (
        jnp.where(
            owned, lax.dynamic_slice_in_dim(prompt_dv, holder * local_rows, local_rows, 0), 0.0
        )
        + grad_v[prompt_rows:]
    )
    grad_qraw = (
        unrotate(grad_q.reshape(local_rows, heads, head_size), cosine, sine)
        .reshape(local_rows, width)
        .astype(jnp.bfloat16)
    )
    grad_kraw = (
        unrotate(mine_k.reshape(local_rows, heads, head_size), cosine, sine)
        .reshape(local_rows, width)
        .astype(jnp.bfloat16)
    )
    grad_vraw = mine_v.astype(jnp.bfloat16)
    pieces = (
        lax.all_gather(query_weight, ("tok", "fs"), axis=0, tiled=True),
        lax.all_gather(key_weight, ("tok", "fs"), axis=0, tiled=True),
        lax.all_gather(value_weight, ("tok", "fs"), axis=0, tiled=True),
        lax.all_gather(first_gain, ("tok", "fs"), axis=0, tiled=True),
    )
    section = (
        contract_cols(grad_qraw, pieces[0])
        + contract_cols(grad_kraw, pieces[1])
        + contract_cols(grad_vraw, pieces[2])
    )
    normed = normed_one
    grad_normed = section * pieces[3].astype(jnp.float32)[None, :]
    gain_sum = jnp.sum(section * normed, axis=0)
    three_grads = jnp.concatenate([grad_qraw, grad_kraw, grad_vraw], axis=1)
    attention_grad = weight_sums(kept_one, three_grads)
    input_grad = grad_second + pull_one(grad_normed)[0]
    output_grad, first_gain_grad, second_gain_grad = (
        lax.psum_scatter(output_full, ("grp", "tok", "fs"), scatter_dimension=0, tiled=True),
        lax.psum_scatter(gain_sum, ("grp", "tok", "fs"), scatter_dimension=0, tiled=True),
        lax.psum_scatter(gain_two, ("grp", "tok", "fs"), scatter_dimension=0, tiled=True),
    )
    return (
        layer_output,
        input_grad,
        attention_grad[:, :width],
        attention_grad[:, width : 2 * width],
        attention_grad[:, 2 * width :],
        output_grad,
        mixer_grad[:, :ff_width],
        mixer_grad[:, ff_width:],
        down_grad,
        first_gain_grad,
        second_gain_grad,
    )


def solution(mesh):
    layered = mesh.shape["grp"] == mesh.shape["tok"] == 4 and mesh.shape["fs"] == 2
    return jax.shard_map(
        make_layered(mesh) if layered else spread_local,
        mesh=mesh,
        in_specs=(
            P(("grp", "tok", "fs"), None),
            P(("grp", "tok", "fs"), None),
            P("grp", None),
            P(("tok", "fs"), None),
            P(("tok", "fs"), None),
            P(("tok", "fs"), None),
            P(("tok", "fs"), None),
            P(("tok", "fs"), None),
            P(("tok", "fs"), None),
            P(("tok", "fs"), None),
            P(("tok", "fs")),
            P(("tok", "fs")),
        ),
        out_specs=(
            P(("grp", "tok", "fs"), None),
            P(("grp", "tok", "fs"), None),
            P(("grp", "tok", "fs"), None),
            P(("grp", "tok", "fs"), None),
            P(("grp", "tok", "fs"), None),
            P(("grp", "tok", "fs"), None),
            P(("grp", "tok", "fs"), None),
            P(("grp", "tok", "fs"), None),
            P(("grp", "tok", "fs"), None),
            P(("grp", "tok", "fs")),
            P(("grp", "tok", "fs")),
        ),
        check_vma=False,
    )
```

```python
import functools
import math

import jax
import jax.numpy as jnp
from jax import lax
from jax.experimental import pallas as pl
from jax.experimental.pallas import tpu as pltpu
from jax.sharding import PartitionSpec as P

HEAD_DIM = 64
BLOCK = 128
PROMPT = 1024
CONT = 256


EPS = 1e-05
RESIDUAL = 1.4 / math.sqrt(40.0)
NEGATIVE = -1e30
GROUP_HEADS = 4

ALL = ("grp", "tok", "fs")
LAYER = ("grp", "fs")
PIECE = 64
TILE = 256
PAIR = 2 * HEAD_DIM
SLAB = 3 * PAIR
BF = jnp.bfloat16
F32 = jnp.float32


def turn(field):
    lane = lax.broadcasted_iota(jnp.int32, field.shape, 1)
    return jnp.where(
        lane % HEAD_DIM < HEAD_DIM // 2,
        pltpu.roll(field, PAIR - HEAD_DIM // 2, 1),
        pltpu.roll(field, HEAD_DIM // 2, 1),
    )


def table_row(piece):
    prompt_pieces = PROMPT // PIECE
    cont_pieces = CONT // PIECE
    return jnp.where(
        piece < prompt_pieces,
        piece,
        prompt_pieces + lax.rem(jnp.maximum(piece - prompt_pieces, 0), cont_pieces),
    )


def head_tiles(pair, index_ref, total, run_tile):
    side = index_ref[total // PIECE]
    own = pair < 2
    for tile in range(PROMPT // TILE):
        mine = side == (0 if tile % 4 in (0, 3) else 1)

        @pl.when(own)
        def _(tile=tile):
            run_tile(tile * TILE, tile * TILE, (0, 1))

        @pl.when(jnp.logical_and(jnp.logical_not(own), mine))
        def _(tile=tile):
            run_tile(tile * TILE, tile * TILE, (0,))

    later = (total - PROMPT) // TILE

    def body(step, carry):
        mine = (step * 2 >= later).astype(jnp.int32) == side
        start = pl.multiple_of(PROMPT + step * TILE, TILE)

        @pl.when(own)
        def _():
            run_tile(start, PROMPT, (0, 1))

        @pl.when(jnp.logical_and(jnp.logical_not(own), mine))
        def _():
            run_tile(start, PROMPT, (0,))

        return carry

    lax.fori_loop(0, later, body, 0)


def lanes_of(head, shape):
    lane = lax.broadcasted_iota(jnp.int32, shape, 1)
    return lane < HEAD_DIM if head == 0 else lane >= HEAD_DIM


def nt_dot(left, right):
    return lax.dot_general(left, right, (((1,), (1,)), ((), ())), preferred_element_type=F32)


def tn_dot(left, right):
    return lax.dot_general(left, right, (((0,), (0,)), ((), ())), preferred_element_type=F32)


def nn_dot(left, right):
    return lax.dot_general(left, right, (((1,), (0,)), ((), ())), preferred_element_type=F32)


def attend_kernel(index_ref, raw_ref, cos_ref, sin_ref, out_ref, kept_ref, mixed):
    total = out_ref.shape[0]
    pieces = total // PIECE
    pair = pl.program_id(0)

    def rope(field, row):
        cosine = cos_ref[pl.ds(row, PIECE), :]
        sine = sin_ref[pl.ds(row, PIECE), :]
        return field * cosine + turn(field) * sine

    @pl.when(pair < 2)
    def _():
        def body(piece, carry):
            source = pl.multiple_of(index_ref[piece], PIECE)
            row = pl.multiple_of(table_row(piece) * PIECE, PIECE)
            target = pl.ds(pl.multiple_of(piece * PIECE, PIECE), PIECE)
            query = rope(raw_ref[pl.ds(source, PIECE), 0:PAIR], row)
            key = rope(raw_ref[pl.ds(source, PIECE), PAIR : 2 * PAIR], row)
            value = raw_ref[pl.ds(source, PIECE), 2 * PAIR : 3 * PAIR]
            kept_ref[0, target, 0:PAIR] = query.astype(BF)
            kept_ref[0, target, PAIR : 2 * PAIR] = key.astype(BF)
            kept_ref[0, target, 2 * PAIR : 3 * PAIR] = value.astype(BF)
            return carry

        lax.fori_loop(0, pieces, body, 0)

    @pl.when(pair == 2)
    def _():
        def body(piece, carry):
            source = pl.multiple_of(index_ref[piece], PIECE)
            row = pl.multiple_of(table_row(piece) * PIECE, PIECE)
            target = pl.ds(pl.multiple_of(piece * PIECE, PIECE), PIECE)
            both = rope(raw_ref[pl.ds(source, PIECE), 0:PAIR], row)
            value = raw_ref[pl.ds(source, PIECE), PAIR : 2 * PAIR]
            low = lanes_of(0, both.shape)
            kept_ref[0, target, 0:PAIR] = jnp.where(low, both, 0.0).astype(BF)
            kept_ref[0, target, PAIR : 2 * PAIR] = jnp.where(
                low, pltpu.roll(both, HEAD_DIM, 1), 0.0
            ).astype(BF)
            kept_ref[0, target, 2 * PAIR : 3 * PAIR] = jnp.where(low, value, 0.0).astype(BF)
            return carry

        lax.fori_loop(0, pieces, body, 0)

    mixed[...] = jnp.zeros_like(mixed)
    scale = 1.0 / math.sqrt(HEAD_DIM)

    def run_tile(start, prefix, heads):
        rows = pl.ds(start, TILE)
        query = kept_ref[0, rows, 0:PAIR].astype(F32) * scale
        masks = [lanes_of(head, query.shape) for head in heads]
        queries = [jnp.where(mask, query, 0.0).astype(BF) for mask in masks]
        seen = lax.broadcasted_iota(jnp.int32, (TILE, TILE), 1) <= lax.broadcasted_iota(
            jnp.int32, (TILE, TILE), 0
        )
        keys = [kept_ref[0, rows, PAIR : 2 * PAIR]]
        values = [kept_ref[0, rows, 2 * PAIR : 3 * PAIR]]
        if prefix:
            keys.append(kept_ref[0, 0:prefix, PAIR : 2 * PAIR])
            values.append(kept_ref[0, 0:prefix, 2 * PAIR : 3 * PAIR])
        scores = [[nt_dot(query, key) for key in keys] for query in queries]
        total_out = mixed[rows, :]
        for mask, parts in zip(masks, scores):
            parts[0] = jnp.where(seen, parts[0], NEGATIVE)
            peak = functools.reduce(
                jnp.maximum, [jnp.max(part, axis=1, keepdims=True) for part in parts]
            )
            parts = [jnp.exp(part - peak) for part in parts]
            count = sum(jnp.sum(part, axis=1, keepdims=True) for part in parts)
            out = sum(nn_dot(part.astype(BF), value) for part, value in zip(parts, values))
            total_out = jnp.where(mask, out / count, total_out)
        mixed[rows, :] = total_out

    head_tiles(pair, index_ref, total, run_tile)

    def back(piece, carry):
        source = pl.multiple_of(index_ref[piece], PIECE)
        target = pl.ds(pl.multiple_of(piece * PIECE, PIECE), PIECE)
        out_ref[pl.ds(source, PIECE), :] = mixed[target, :].astype(BF)
        return carry

    lax.fori_loop(0, pieces, back, 0)


def attend(index, raw, cosine, sine):
    total = raw.shape[0]
    return pl.pallas_call(
        attend_kernel,
        grid_spec=pltpu.PrefetchScalarGridSpec(
            num_scalar_prefetch=1,
            grid=(3,),
            in_specs=[
                pl.BlockSpec((total, SLAB), lambda j, index: (0, j)),
                pl.BlockSpec(cosine.shape, lambda j, index: (0, 0)),
                pl.BlockSpec(sine.shape, lambda j, index: (0, 0)),
            ],
            out_specs=[
                pl.BlockSpec((total, PAIR), lambda j, index: (0, j)),
                pl.BlockSpec((1, total, SLAB), lambda j, index: (j, 0, 0)),
            ],
            scratch_shapes=[pltpu.VMEM((total, PAIR), F32)],
        ),
        out_shape=[
            jax.ShapeDtypeStruct((total, 3 * PAIR), BF),
            jax.ShapeDtypeStruct((3, total, SLAB), BF),
        ],
        compiler_params=pltpu.CompilerParams(vmem_limit_bytes=40 << 20),
        cost_estimate=pl.CostEstimate(
            flops=36 * 10**9, bytes_accessed=1 << 20, transcendentals=0
        ),
        name="attend",
    )(index, raw, cosine, sine)


def attend_back_kernel(
    first, index_ref, kept_ref, outer_ref, cos_ref, sin_ref, grad_ref, outer, grad_q, grad_k, grad_v
):
    total = outer.shape[0]
    pieces = total // PIECE
    pair = pl.program_id(0) + first

    def sort(piece, carry):
        source = pl.multiple_of(index_ref[piece], PIECE)
        target = pl.ds(pl.multiple_of(piece * PIECE, PIECE), PIECE)
        outer[target, :] = outer_ref[pl.ds(source, PIECE), :]
        return carry

    lax.fori_loop(0, pieces, sort, 0)
    grad_q[...] = jnp.zeros_like(grad_q)
    grad_k[...] = jnp.zeros_like(grad_k)
    grad_v[...] = jnp.zeros_like(grad_v)
    scale = 1.0 / math.sqrt(HEAD_DIM)

    def run_tile(start, prefix, heads):
        rows = pl.ds(start, TILE)
        query = kept_ref[0, rows, 0:PAIR].astype(F32) * scale
        away = outer[rows, :].astype(F32)
        masks = [lanes_of(head, query.shape) for head in heads]
        queries = [jnp.where(mask, query, 0.0).astype(BF) for mask in masks]
        aways = [jnp.where(mask, away, 0.0).astype(BF) for mask in masks]
        seen = lax.broadcasted_iota(jnp.int32, (TILE, TILE), 0) <= lax.broadcasted_iota(
            jnp.int32, (TILE, TILE), 1
        )
        spans = [rows] + ([pl.ds(0, prefix)] if prefix else [])
        keys = [kept_ref[0, span, PAIR : 2 * PAIR] for span in spans]
        values = [kept_ref[0, span, 2 * PAIR : 3 * PAIR] for span in spans]
        scores = [[nt_dot(key, query) for key in keys] for query in queries]
        pulls = [[nt_dot(value, away) for value in values] for away in aways]
        probs, slopes = [], []
        for parts, pull in zip(scores, pulls):
            parts[0] = jnp.where(seen, parts[0], NEGATIVE)
            peak = functools.reduce(
                jnp.maximum, [jnp.max(part, axis=0, keepdims=True) for part in parts]
            )
            parts = [jnp.exp(part - peak) for part in parts]
            inverse = 1.0 / sum(jnp.sum(part, axis=0, keepdims=True) for part in parts)
            parts = [part * inverse for part in parts]
            delta = sum(jnp.sum(p * q, axis=0, keepdims=True) for p, q in zip(parts, pull))
            probs.append([part.astype(BF) for part in parts])
            slopes.append([(p * (q - delta)).astype(BF) for p, q in zip(parts, pull)])
        for i, span in enumerate(spans):
            grad_v[span, :] += sum(nn_dot(prob[i], away) for prob, away in zip(probs, aways))
            grad_k[span, :] += sum(nn_dot(slope[i], query) for slope, query in zip(slopes, queries))
        part_q = grad_q[rows, :]
        for mask, slope in zip(masks, slopes):
            part = sum(tn_dot(piece, key) for piece, key in zip(slope, keys))
            part_q = jnp.where(mask, part * scale, part_q)
        grad_q[rows, :] = part_q

    head_tiles(pair, index_ref, total, run_tile)

    def unrope(field, row):
        cosine = cos_ref[pl.ds(row, PIECE), :]
        sine = sin_ref[pl.ds(row, PIECE), :]
        return field * cosine - turn(field) * sine

    @pl.when(pair < 2)
    def _():
        def back(piece, carry):
            source = pl.ds(pl.multiple_of(index_ref[piece], PIECE), PIECE)
            row = pl.multiple_of(table_row(piece) * PIECE, PIECE)
            here = pl.ds(pl.multiple_of(piece * PIECE, PIECE), PIECE)
            grad_ref[source, 0:PAIR] = unrope(grad_q[here, :], row).astype(BF)
            grad_ref[source, PAIR : 2 * PAIR] = unrope(grad_k[here, :], row).astype(BF)
            grad_ref[source, 2 * PAIR : 3 * PAIR] = grad_v[here, :].astype(BF)
            return carry

        lax.fori_loop(0, pieces, back, 0)

    @pl.when(pair == 2)
    def _():
        def back(piece, carry):
            source = pl.ds(pl.multiple_of(index_ref[piece], PIECE), PIECE)
            row = pl.multiple_of(table_row(piece) * PIECE, PIECE)
            here = pl.ds(pl.multiple_of(piece * PIECE, PIECE), PIECE)
            low = lanes_of(0, (PIECE, PAIR))
            both = jnp.where(low, grad_q[here, :], pltpu.roll(grad_k[here, :], HEAD_DIM, 1))
            grad_ref[source, 0:PAIR] = unrope(both, row).astype(BF)
            grad_ref[source, PAIR : 2 * PAIR] = grad_v[here, :].astype(BF)
            grad_ref[source, 2 * PAIR : 3 * PAIR] = jnp.zeros((PIECE, PAIR), BF)
            return carry

        lax.fori_loop(0, pieces, back, 0)


def attend_back(first, count, index, kept, outer, cosine, sine, columns):
    total = outer.shape[0]
    return pl.pallas_call(
        functools.partial(attend_back_kernel, first),
        grid_spec=pltpu.PrefetchScalarGridSpec(
            num_scalar_prefetch=1,
            grid=(count,),
            in_specs=[
                pl.BlockSpec((1, total, SLAB), lambda j, index: (j + first, 0, 0)),
                pl.BlockSpec((total, PAIR), lambda j, index: (0, j + first)),
                pl.BlockSpec(cosine.shape, lambda j, index: (0, 0)),
                pl.BlockSpec(sine.shape, lambda j, index: (0, 0)),
            ],
            out_specs=pl.BlockSpec((total, SLAB), lambda j, index: (0, j)),
            scratch_shapes=[
                pltpu.VMEM((total, PAIR), BF),
                pltpu.VMEM((total, PAIR), F32),
                pltpu.VMEM((total, PAIR), F32),
                pltpu.VMEM((total, PAIR), F32),
            ],
        ),
        out_shape=jax.ShapeDtypeStruct((total, columns), BF),
        compiler_params=pltpu.CompilerParams(vmem_limit_bytes=48 << 20),
        cost_estimate=pl.CostEstimate(
            flops=0, bytes_accessed=1 << 20, transcendentals=0
        ),
        name="attend_back",
    )(index, kept, outer, cosine, sine)


def after(array, *earlier):
    leaves = [array] + jax.tree.leaves(earlier)
    place = pl.BlockSpec(memory_space=pl.ANY)
    return pl.pallas_call(
        lambda *refs: None,
        in_specs=[place] * len(leaves),
        out_specs=place,
        out_shape=jax.ShapeDtypeStruct(array.shape, array.dtype),
        input_output_aliases={0: 0},
        name="after",
    )(*leaves)


def make_layered(mesh):
    n_grp, n_tok, n_fs = (mesh.shape[axis] for axis in ALL)

    def device(grp, tok, fs):
        return (grp * n_tok + tok) * n_fs + fs

    def permutation(move):
        return [
            (device(g, t, f), device(*move(g, t, f)))
            for g in range(n_grp)
            for t in range(n_tok)
            for f in range(n_fs)
        ]

    def send(array, move):
        return lax.ppermute(array, ALL, permutation(move))

    def cross(step):
        return lambda g, t, f: (g ^ step, t, f)

    def sibling(g, t, f):
        return (g, t, 1 - f)

    def local(
        hidden_in,
        cotangent,
        block_start,
        query_weight,
        key_weight,
        value_weight,
        output_weight,
        gate_weight,
        up_weight,
        down_weight,
        first_gain,
        second_gain,
    ):
        rows, width = hidden_in.shape
        ff_width = gate_weight.shape[1]
        g, t, f = (lax.axis_index(axis) for axis in ALL)
        even = f == 0
        ranks = n_grp * n_fs
        total = rows * ranks
        quarter = rows // n_grp


        def spread_in(array):
            return lax.all_to_all(array.reshape(n_grp, quarter, width), "grp", 0, 0, tiled=True)

        def shuffle_in(parts):
            return lax.all_to_all(parts, "tok", 0, 0, tiled=True).reshape(rows, width)

        def shuffle_out(arrays, beside):
            parts = [array.reshape(n_tok, quarter, width) for array in arrays]
            pieces = []
            for turn_by in range(n_grp):
                away = g ^ t ^ turn_by
                piece = [lax.dynamic_index_in_dim(part, away, 0, keepdims=True) for part in parts]
                piece = send(
                    jnp.concatenate(piece, axis=1),
                    lambda g, t, f, turn_by=turn_by: (t, g ^ t ^ turn_by, f),
                )
                pieces.append(after(piece, beside))

            def arrived_from(place):
                chosen = pieces[place]
                for step in range(1, n_grp):
                    chosen = jnp.where(g ^ t == step, pieces[place ^ step], chosen)
                return chosen

            found = jnp.concatenate([arrived_from(place) for place in range(n_grp)], axis=0)
            results = [
                found[:, i * quarter : (i + 1) * quarter] for i in range(len(arrays))
            ]
            return [result.reshape(rows, width) for result in results]


        def layer_pieces(array):
            half = array.shape[0] // 2
            by_x = send(array, cross(1))
            by_y = send(array, cross(2))
            return array, by_x, by_y, send(by_x[:half], cross(2)), send(by_y[half:], cross(1))

        def layer_join(array, by_x, by_y, *by_xy):
            mine = [array, by_x, by_y, jnp.concatenate(by_xy, axis=0)]
            return jnp.concatenate(mine + [send(part, sibling) for part in mine], axis=0)

        def layer_gather(array):
            return layer_join(*layer_pieces(array))

        def pair_sum(rows_of):
            away = rows_of(1).astype(BF).reshape(n_grp, rows, -1)
            away = {step: send(away[step], sibling) for step in (3, 1, 2, 0)}
            here = rows_of(0).reshape(n_grp, rows, -1)
            parts = [(here[step] + away[step].astype(F32)).astype(BF) for step in (3, 1, 2)]
            return here[0], away[0], parts

        def layer_send(sums, *earlier):
            here, away, parts = sums
            if earlier:
                parts = [after(part, *earlier) for part in parts]
            return here, away, [send(part, cross(step)) for part, step in zip(parts, (3, 1, 2))]

        def layer_add(parts, beside=None):
            here, away, got = parts
            if beside is not None:
                got = [after(part, beside) for part in got]
            return here + away.astype(F32) + sum(part.astype(F32) for part in got)

        def layer_sum(rows_of, beside=None):
            return layer_add(layer_send(pair_sum(rows_of)), beside)

        def halves(*arrays):
            half = arrays[0].shape[0] // 2
            return lambda which: [array[which * half : (which + 1) * half] for array in arrays]

        extra = 8
        gains_here = jnp.concatenate([first_gain, second_gain])
        span = gains_here.shape[0]
        gains_here = jnp.pad(gains_here[None, :], ((0, extra - 1), (0, width - span)))
        hidden_parts = spread_in(hidden_in)
        cotangent_parts = spread_in(after(cotangent, hidden_parts))
        arrived = lax.all_to_all(
            jnp.concatenate(
                [hidden_parts, jnp.broadcast_to(gains_here[None], (n_tok, extra, width))], axis=1
            ),
            "tok",
            0,
            0,
            tiled=True,
        )
        gains_mine = arrived[:, quarter, :span]
        gains_other = send(gains_mine, sibling)
        gains_all = jnp.stack(
            [jnp.where(even, gains_mine, gains_other), jnp.where(even, gains_other, gains_mine)],
            axis=1,
        ).astype(F32).reshape(n_tok * n_fs, 2, -1)
        gain_one = gains_all[:, 0].reshape(width)
        gain_two = gains_all[:, 1].reshape(width)
        starts = send(block_start, lambda g, t, f: (t, g, f))[0]
        xs = arrived[:, :quarter].reshape(rows, width)
        cotangent_here = shuffle_in(after(cotangent_parts, xs))


        head_span = width // n_grp
        own_span = 4 * HEAD_DIM

        def rank_columns(side):
            picked = [
                lax.dynamic_slice_in_dim(weight, g * head_span, head_span, 1)
                for weight in (query_weight, key_weight, value_weight)
            ]
            first = side * (own_span + HEAD_DIM)
            spans = [(first, PAIR), (first + PAIR, PAIR), (own_span, HEAD_DIM)]
            columns = [weight[:, at : at + size] for at, size in spans for weight in picked]
            wide = sum(part.shape[1] for part in columns)
            columns.append(jnp.zeros((query_weight.shape[0], -wide % PAIR), BF))
            return jnp.concatenate(columns, axis=1)

        def pair_rows(zero_block, one_block):
            mine = jnp.where(even, zero_block, one_block)
            other = send(jnp.where(even, one_block, zero_block), sibling)
            return jnp.concatenate(
                [jnp.where(even, mine, other), jnp.where(even, other, mine)], axis=0
            )

        def gather_rows(array, *earlier):
            array = after(array, *earlier)
            return array, lax.all_gather(array, "tok", axis=0, tiled=True)

        turn_one, qkv_weight = gather_rows(
            pair_rows(rank_columns(0), rank_columns(1)), xs
        )
        ff_piece = ff_width // (ranks * n_tok)
        ff_tall = -(-ff_piece // 64) * 64
        ff_wide = ff_tall * n_tok

        def ff_columns(side):
            parts = [
                lax.dynamic_slice_in_dim(
                    weight, (step * n_fs + side) * n_grp * ff_piece + g * ff_piece, ff_piece, 1
                )
                for weight in (gate_weight, up_weight)
                for step in range(n_tok)
            ]
            zeros = jnp.zeros((gate_weight.shape[0], ff_tall - ff_piece), BF)
            return jnp.concatenate([item for part in parts for item in (part, zeros)], axis=1)

        ff_inputs = (
            pair_rows(ff_columns(0), ff_columns(1)),
            jnp.pad(
                lax.dynamic_slice_in_dim(down_weight, g * ff_piece, ff_piece, 0),
                ((0, ff_tall - ff_piece), (0, 0)),
            ),
        )

        hidden = after(xs, *ff_inputs).astype(F32)
        scale_one = lax.rsqrt(jnp.mean(hidden * hidden, axis=1, keepdims=True) + EPS)
        normed_one = hidden * scale_one
        h_one = layer_gather((normed_one * gain_one[None, :]).astype(BF))
        out_rows = output_weight.shape[0] // n_grp
        turn_two, out_weight = gather_rows(
            lax.dynamic_slice_in_dim(output_weight, g * out_rows, out_rows, 0), turn_one, h_one
        )
        grad_out = cotangent_here.astype(F32)
        grad_m_pieces = layer_pieces(after((RESIDUAL * grad_out).astype(BF), h_one))
        grad_m = layer_join(*grad_m_pieces)
        raw = nn_dot(after(h_one, *grad_m_pieces[1:3]), qkv_weight)
        out_weight = lax.all_to_all(after(out_weight, raw), "grp", 0, 0, tiled=True)
        half_head = HEAD_DIM // 2
        swapped = send(
            jnp.where(even, out_weight[own_span:], out_weight[:half_head]), sibling
        )
        out_weight = jnp.concatenate(
            [
                jnp.where(even, out_weight[:own_span], out_weight[half_head:]),
                jnp.where(even, out_weight[own_span:], swapped),
                jnp.where(even, swapped, out_weight[:half_head]),
                jnp.zeros((HEAD_DIM, width), BF),
            ],
            axis=0,
        )

        _, ff_weight = gather_rows(ff_inputs[0], turn_two)
        _, down_w = gather_rows(ff_inputs[1], ff_inputs[0], turn_two)


        number = jnp.arange(total // BLOCK, dtype=jnp.int32)
        prompt_blocks = PROMPT // BLOCK
        cont_blocks = CONT // BLOCK
        place = jnp.where(
            number < prompt_blocks,
            starts // BLOCK,
            prompt_blocks
            + (number - prompt_blocks) // cont_blocks * cont_blocks
            + (starts - PROMPT) // BLOCK,
        )
        order = jnp.sum(
            jnp.where(place[None, :] == number[:, None], number[None, :], 0), axis=1
        )
        pieces = (
            order[:, None] * (BLOCK // PIECE) + jnp.arange(BLOCK // PIECE, dtype=jnp.int32)
        ).reshape(-1)
        from_t = pieces // ranks
        from_f = pieces // n_grp % n_fs
        from_g = pieces % n_grp
        index = jnp.concatenate(
            [
                (((from_f ^ f) * n_grp + (from_g ^ g)) * n_tok + from_t) * PIECE,
                f[None].astype(jnp.int32),
            ]
        ).astype(jnp.int32)
        lane = jnp.arange(PAIR, dtype=jnp.int32)
        half_head_lane = lane % (HEAD_DIM // 2)
        freq = 10000.0 ** (-(half_head_lane.astype(F32) * 2.0) / HEAD_DIM)
        angle = jnp.arange(PROMPT + CONT, dtype=F32)[:, None] * freq[None, :]
        cosine = jnp.cos(angle)
        sine = jnp.where(lane[None, :] % HEAD_DIM < HEAD_DIM // 2, -jnp.sin(angle), jnp.sin(angle))


        attn_out, kept = attend(index, raw, cosine, sine)
        pick = halves(attn_out)
        branch = layer_sum(lambda side, pick=pick: nn_dot(pick(side)[0], out_weight), grad_m)
        second_in = hidden + RESIDUAL * branch
        scale_two = lax.rsqrt(jnp.mean(second_in * second_in, axis=1, keepdims=True) + EPS)
        normed_two = second_in * scale_two
        h_two = layer_gather((normed_two * gain_two[None, :]).astype(BF))
        both = nn_dot(h_two, ff_weight)
        gate = both[:, :ff_wide]
        up_val = both[:, ff_wide:]
        sigma = jax.nn.sigmoid(gate)
        silu = gate * sigma
        act = (silu * up_val).astype(BF)


        down_local = tn_dot(act, grad_m).astype(BF).reshape(n_tok, ff_tall, width)
        grad_act = nt_dot(after(grad_m, down_local), down_w)
        grad_gate = (grad_act * up_val * (sigma * (1.0 + gate * (1.0 - sigma)))).astype(BF)
        grad_up = (grad_act * silu).astype(BF)

        def spread_rows(grad):
            columns = grad.shape[1]
            grad = grad.astype(BF).reshape(n_grp, n_tok, width // (n_grp * n_tok), columns)
            return grad.transpose(1, 0, 2, 3).reshape(n_tok, width // n_tok, columns)

        def sum_rows(grad):
            grad = lax.psum_scatter(grad, "tok", scatter_dimension=0, tiled=True)
            return grad.reshape(ranks, width // (ranks * n_tok), grad.shape[2])

        def to_owners(grad, weight, spare):
            weight = weight.reshape(n_grp, n_tok, width // (n_grp * n_tok), grad.shape[2])
            weight = lax.dynamic_index_in_dim(weight, t, 1, keepdims=False).reshape(grad.shape)
            total = jnp.sum(grad.astype(F32) * weight.astype(F32), axis=2, keepdims=True)
            high = total.astype(BF)
            low = (total - high.astype(F32)).astype(BF)
            column = lax.broadcasted_iota(jnp.int32, grad.shape, 2)
            grad = jnp.where(column == spare, high, jnp.where(column == spare + 1, low, grad))
            return lax.all_to_all(grad, LAYER, 0, 0, tiled=True)

        def gain_of(got, spare):
            return jnp.sum(got[..., spare : spare + 2].astype(F32), axis=(0, 2))

        pick = halves(grad_gate, grad_up)
        parts = layer_send(
            pair_sum(
                lambda side, pick=pick: nt_dot(pick(side)[0], ff_weight[:, :ff_wide])
                + nt_dot(pick(side)[1], ff_weight[:, ff_wide:])
            )
        )
        ff_local = spread_rows(
            tn_dot(
                h_two,
                jnp.concatenate([after(grad_gate, parts[0]), after(grad_up, parts[0])], axis=1),
            )
        )
        grad_h2 = layer_add(parts, ff_local)
        ff_rows = sum_rows(ff_local)
        pulled = grad_h2 * gain_two[None, :]
        grad_second = (
            grad_out
            + scale_two * pulled
            - scale_two**3 * second_in * jnp.mean(pulled * second_in, axis=1, keepdims=True)
        )
        grad_z_here = (RESIDUAL * grad_second).astype(BF)
        down_rows = lax.psum_scatter(down_local, "tok", scatter_dimension=0, tiled=True)
        down_rows = down_rows[0, :ff_piece]
        grad_z = layer_gather(grad_z_here)
        pick = halves(after(act, grad_z_here))
        feed_sums = pair_sum(lambda side, pick=pick: nn_dot(pick(side)[0], down_w))
        grad_attn = nt_dot(grad_z, out_weight).astype(BF)
        feed_parts = layer_send(feed_sums, grad_z)
        out_full = tn_dot(attn_out, grad_z)
        shared = out_full[own_span : own_span + HEAD_DIM]
        swapped = send(
            jnp.where(even, shared[half_head:], shared[:half_head]).astype(BF), sibling
        ).astype(F32)
        kept_half = jnp.where(even, shared[:half_head], shared[half_head:]) + swapped
        out_full = jnp.where(
            even,
            jnp.concatenate([out_full[:own_span], kept_half], axis=0),
            jnp.concatenate([kept_half, out_full[:own_span]], axis=0),
        )
        out_full = out_full.astype(BF).reshape(n_tok, -1, width)
        output_grad = lax.psum_scatter(out_full, "tok", scatter_dimension=0, tiled=True)

        grad_attn = after(grad_attn, out_full, down_rows, feed_parts[0])
        grads = attend_back(0, 3, index, kept, grad_attn, cosine, sine, qkv_weight.shape[1])
        grads = after(grads, ff_rows, *feed_parts[2])
        qkv_local = spread_rows(tn_dot(h_one, grads))
        qkv_rows = sum_rows(qkv_local)
        ff_got = to_owners(after(ff_rows, grads), ff_weight, ff_piece)
        pick = halves(after(grads, qkv_local, output_grad, ff_got))
        parts = layer_send(pair_sum(lambda side, pick=pick: nt_dot(pick(side)[0], qkv_weight)))
        feed = layer_add(feed_parts, parts[2][1])
        layer_output = (second_in + RESIDUAL * feed).astype(BF)
        grad_h1 = layer_add(parts)
        pulled = grad_h1 * gain_one[None, :]
        input_grad = (
            grad_second
            + scale_one * pulled
            - scale_one**3 * hidden * jnp.mean(pulled * hidden, axis=1, keepdims=True)
        )
        input_grad = input_grad.astype(BF)
        input_grad = after(input_grad, qkv_rows)
        used = 5 * 3 * HEAD_DIM
        got = to_owners(qkv_rows, qkv_weight, used)
        down_grad = send(
            after(down_rows, got),
            lambda g, t, f: (t, (n_grp * f + g) // n_fs, (n_grp * f + g) % n_fs),
        )
        output_grad = send(
            after(output_grad[0], got),
            lambda g, t, f: (g, (n_tok * f + t) // n_fs, (n_tok * f + t) % n_fs),
        )
        gain_one_grad = gain_of(got, used)
        ff_got = after(ff_got, got)
        gain_two_grad = gain_of(ff_got, ff_piece)
        wide = ff_got.reshape(n_grp, n_fs, -1, 2, n_tok, ff_tall)
        gate_grad, up_grad = (
            wide[:, :, :, which, :, :ff_piece]
            .transpose(2, 3, 1, 0, 4)
            .reshape(-1, ff_width)
            .astype(F32)
            for which in range(2)
        )
        own_rows = got.shape[1]
        here = got.astype(F32).reshape(n_grp, n_fs, own_rows, got.shape[2])

        def projection_grad(which):
            def own(side):
                return [
                    here[:, side, :, SLAB * pair + PAIR * which : SLAB * pair + PAIR * (which + 1)]
                    for pair in range(2)
                ]

            at = 2 * SLAB + HEAD_DIM * which
            shared = here[:, 0, :, at : at + HEAD_DIM] + here[:, 1, :, at : at + HEAD_DIM]
            whole = jnp.concatenate(own(0) + [shared] + own(1), axis=2)
            return whole.transpose(1, 0, 2).reshape(own_rows, width)

        qkv_grads = [projection_grad(which) for which in range(3)]
        layer_output, input_grad = shuffle_out((layer_output, input_grad), (qkv_grads, gate_grad, up_grad))
        input_grad = input_grad.astype(F32)
        mine = ((g * n_tok + t) * n_fs + f) * own_rows
        gain_one_grad = gain_one_grad / lax.dynamic_slice_in_dim(gain_one, mine, own_rows)
        gain_two_grad = gain_two_grad / lax.dynamic_slice_in_dim(gain_two, mine, own_rows)
        return (
            layer_output,
            input_grad,
            *qkv_grads,
            output_grad.astype(F32),
            gate_grad,
            up_grad,
            down_grad.astype(F32),
            gain_one_grad,
            gain_two_grad,
        )

    return local


def spread(block, axis, source):
    block = jnp.where(lax.axis_index(axis) == source, block, jnp.zeros_like(block))
    return lax.psum(block, axis)


def rope_tables(positions, head_size):
    half = head_size // 2
    freq = 10000.0 ** (-(jnp.arange(half, dtype=jnp.float32) * 2.0) / head_size)
    angle = positions.astype(jnp.float32)[:, None] * freq[None, :]
    return (jnp.cos(angle)[:, None, :], jnp.sin(angle)[:, None, :])


def rotate(field, cosine, sine):
    half = field.shape[-1] // 2
    first = field[..., :half]
    second = field[..., half:]
    return jnp.concatenate(
        [first * cosine - second * sine, second * cosine + first * sine], axis=-1
    )


def unrotate(grad, cosine, sine):
    half = grad.shape[-1] // 2
    first = grad[..., :half]
    second = grad[..., half:]
    return jnp.concatenate(
        [first * cosine + second * sine, second * cosine - first * sine], axis=-1
    )


def row_norm(values):
    return values * lax.rsqrt(jnp.mean(values * values, axis=-1, keepdims=True) + EPS)


def swish_product(gate, up_val):
    return jax.nn.silu(gate) * up_val


def contract_rows(left, right):
    return lax.dot_general(
        left, right, (((0,), (0,)), ((), ())), preferred_element_type=jnp.float32
    )


def contract_cols(left, right):
    return lax.dot_general(
        left, right, (((1,), (1,)), ((), ())), preferred_element_type=jnp.float32
    )


def weight_sums(left, right):
    return lax.psum_scatter(
        contract_rows(left, right), ("grp", "tok", "fs"), scatter_dimension=0, tiled=True
    )


def spread_local(
    hidden_in,
    cotangent,
    block_start,
    query_weight,
    key_weight,
    value_weight,
    output_weight,
    gate_weight,
    up_weight,
    down_weight,
    first_gain,
    second_gain,
):
    local_rows, width = hidden_in.shape
    ff_width = gate_weight.shape[1]
    head_size = HEAD_DIM
    heads = width // head_size
    group_width = GROUP_HEADS * head_size
    group_count = heads // GROUP_HEADS
    scale = 1.0 / math.sqrt(head_size)
    device = lax.axis_index(("tok", "fs"))
    holders = -(-PROMPT // local_rows)
    prompt_rows = holders * local_rows
    starts = block_start[0]
    offsets = jnp.arange(BLOCK, dtype=jnp.int32)
    local_starts = lax.dynamic_slice_in_dim(
        starts, device * (local_rows // BLOCK), local_rows // BLOCK
    )
    my_pos = (local_starts[:, None] + offsets[None, :]).reshape(local_rows)
    prompt_pos = (starts[: prompt_rows // BLOCK][:, None] + offsets[None, :]).reshape(prompt_rows)
    my_row = device * local_rows + jnp.arange(local_rows, dtype=jnp.int32)
    my_seg = jnp.where(my_row < PROMPT, 0, 1 + (my_row - PROMPT) // CONT)
    prompt_row = jnp.arange(prompt_rows, dtype=jnp.int32)
    prompt_seen = (prompt_row[None, :] < PROMPT) & (prompt_pos[None, :] <= my_pos[:, None])
    local_seen = (
        (my_seg[None, :] == my_seg[:, None])
        & (my_seg[None, :] > 0)
        & (my_pos[None, :] <= my_pos[:, None])
    )
    visible = jnp.concatenate([prompt_seen, local_seen], axis=1)
    cosine, sine = rope_tables(my_pos, head_size)
    hidden = hidden_in.astype(jnp.float32)
    normed_one, pull_one = jax.vjp(row_norm, hidden)
    zero_rows = jnp.zeros((local_rows, width), jnp.float32)
    pieces = (
        lax.all_gather(query_weight, ("tok", "fs"), axis=0, tiled=True),
        lax.all_gather(key_weight, ("tok", "fs"), axis=0, tiled=True),
        lax.all_gather(value_weight, ("tok", "fs"), axis=0, tiled=True),
        lax.all_gather(first_gain, ("tok", "fs"), axis=0, tiled=True),
    )
    normed = normed_one
    scaled = (normed * pieces[3].astype(jnp.float32)[None, :]).astype(jnp.bfloat16)
    kept = scaled
    query_acc = jnp.dot(scaled, pieces[0], preferred_element_type=jnp.float32)
    key_acc = jnp.dot(scaled, pieces[1], preferred_element_type=jnp.float32)
    value_acc = jnp.dot(scaled, pieces[2], preferred_element_type=jnp.float32)
    kept_one = kept
    queries = (
        rotate(query_acc.reshape(local_rows, heads, head_size), cosine, sine)
        .astype(jnp.bfloat16)
        .reshape(local_rows, width)
    )
    keys = (
        rotate(key_acc.reshape(local_rows, heads, head_size), cosine, sine)
        .astype(jnp.bfloat16)
        .reshape(local_rows, width)
    )
    values = value_acc.astype(jnp.bfloat16)
    paired = jnp.stack([keys, values])
    received = []
    for root in range(holders):
        received.append(spread(paired, ("tok", "fs"), root))
    gathered = jnp.concatenate(received, axis=1)
    all_keys = jnp.concatenate([gathered[0], keys], axis=0)
    all_values = jnp.concatenate([gathered[1], values], axis=0)
    total_keys = all_keys.shape[0]

    def head_slice(array, index):
        return lax.dynamic_slice_in_dim(array, index * group_width, group_width, 1).reshape(
            array.shape[0], GROUP_HEADS, head_size
        )

    def scores_of(index):
        raw = (
            jnp.einsum(
                "qhd,khd->hqk",
                head_slice(queries, index),
                head_slice(all_keys, index),
                preferred_element_type=jnp.float32,
            )
            * scale
        )
        return jnp.where(visible[None], raw, NEGATIVE)

    def attend_group(index, carry):
        mixed, peaks, totals = carry
        scores = scores_of(index)
        peak = jnp.max(scores, axis=-1, keepdims=True)
        expo = jnp.exp(scores - peak)
        total = jnp.sum(expo, axis=-1, keepdims=True)
        probs = (expo / total).astype(jnp.bfloat16)
        block_out = jnp.einsum(
            "hqk,khd->qhd", probs, head_slice(all_values, index), preferred_element_type=jnp.float32
        ).reshape(local_rows, group_width)
        mixed = lax.dynamic_update_slice_in_dim(mixed, block_out, index * group_width, 1)
        peaks = lax.dynamic_update_slice_in_dim(peaks, peak[None, :, :, 0], index, 0)
        totals = lax.dynamic_update_slice_in_dim(totals, total[None, :, :, 0], index, 0)
        return (mixed, peaks, totals)

    stats_zero = jnp.zeros((group_count, GROUP_HEADS, local_rows), jnp.float32)
    mixed, peaks, totals = lax.fori_loop(
        0, group_count, attend_group, (zero_rows, stats_zero, stats_zero)
    )
    attention_out = mixed.astype(jnp.bfloat16)
    branch = jnp.dot(
        attention_out,
        lax.all_gather(output_weight, ("tok", "fs"), axis=0, tiled=True),
        preferred_element_type=jnp.float32,
    )
    second_in = hidden + RESIDUAL * branch
    normed_two, pull_two = jax.vjp(row_norm, second_in)
    retained = ()
    pieces = (
        lax.all_gather(gate_weight, ("tok", "fs"), axis=0, tiled=True),
        lax.all_gather(up_weight, ("tok", "fs"), axis=0, tiled=True),
        lax.all_gather(second_gain, ("tok", "fs"), axis=0, tiled=True),
    )
    start = jnp.int32(0)
    stored = retained
    normed = normed_two
    scaled = (normed * pieces[2].astype(jnp.float32)[None, :]).astype(jnp.bfloat16)
    kept = scaled
    stored = tuple(
        (
            lax.dynamic_update_slice_in_dim(buffer, piece, start, 0)
            for buffer, piece in zip(stored, pieces)
        )
    )
    gate_acc, up_acc, kept_two, stored = (
        jnp.dot(scaled, pieces[0], preferred_element_type=jnp.float32),
        jnp.dot(scaled, pieces[1], preferred_element_type=jnp.float32),
        kept,
        stored,
    )
    swish, pull_swish = jax.vjp(swish_product, gate_acc, up_acc)
    act = swish.astype(jnp.bfloat16)
    down_store = ()
    piece = lax.all_gather(down_weight, ("tok", "fs"), axis=0, tiled=True)
    start = jnp.int32(0)
    stored_down = down_store
    total_acc = jnp.dot(act, piece, preferred_element_type=jnp.float32)
    stored_down = tuple(
        (lax.dynamic_update_slice_in_dim(buffer, piece, start, 0) for buffer in stored_down)
    )
    feed, stored_down = (total_acc, stored_down)
    layer_output = (second_in + RESIDUAL * feed).astype(jnp.bfloat16)
    grad_out = cotangent.astype(jnp.float32)
    grad_m = (RESIDUAL * grad_out).astype(jnp.bfloat16)
    grad_act = contract_cols(grad_m, lax.all_gather(down_weight, ("tok", "fs"), axis=0, tiled=True))
    down_grad = weight_sums(act, grad_m)
    grad_gate_f, grad_up_f = pull_swish(grad_act)
    grad_gate = grad_gate_f.astype(jnp.bfloat16)
    grad_up = grad_up_f.astype(jnp.bfloat16)
    pieces = (
        lax.all_gather(gate_weight, ("tok", "fs"), axis=0, tiled=True),
        lax.all_gather(up_weight, ("tok", "fs"), axis=0, tiled=True),
        lax.all_gather(second_gain, ("tok", "fs"), axis=0, tiled=True),
    )
    section = contract_cols(grad_gate, pieces[0]) + contract_cols(grad_up, pieces[1])
    normed = normed_two
    grad_normed = section * pieces[2].astype(jnp.float32)[None, :]
    gain_sum = jnp.sum(section * normed, axis=0)
    grad_n2 = grad_normed
    gain_two = gain_sum
    both_grads = jnp.concatenate([grad_gate, grad_up], axis=1)
    mixer_grad = weight_sums(kept_two, both_grads)
    grad_second = grad_out + pull_two(grad_n2)[0]
    grad_z = (RESIDUAL * grad_second).astype(jnp.bfloat16)
    output_full = contract_rows(attention_out, grad_z)
    grad_attn = contract_cols(
        grad_z, lax.all_gather(output_weight, ("tok", "fs"), axis=0, tiled=True)
    ).astype(jnp.bfloat16)

    def attend_back(index, carry):
        grad_q, grad_k, grad_v = carry
        query_g = head_slice(queries, index)
        key_g = head_slice(all_keys, index)
        value_g = head_slice(all_values, index)
        outer_g = head_slice(grad_attn, index)
        scores = scores_of(index)
        peak = lax.dynamic_index_in_dim(peaks, index, 0, keepdims=False)[:, :, None]
        total = lax.dynamic_index_in_dim(totals, index, 0, keepdims=False)[:, :, None]
        probs = jnp.exp(scores - peak) / total
        grad_probs = jnp.einsum(
            "qhd,khd->hqk", outer_g, value_g, preferred_element_type=jnp.float32
        )
        grad_scores = (
            probs * (grad_probs - jnp.sum(grad_probs * probs, axis=-1, keepdims=True))
        ).astype(jnp.bfloat16)
        query_part = (
            jnp.einsum("hqk,khd->qhd", grad_scores, key_g, preferred_element_type=jnp.float32)
            * scale
        )
        key_part = (
            jnp.einsum("hqk,qhd->khd", grad_scores, query_g, preferred_element_type=jnp.float32)
            * scale
        )
        value_part = jnp.einsum(
            "hqk,qhd->khd", probs.astype(jnp.bfloat16), outer_g, preferred_element_type=jnp.float32
        )
        grad_q = lax.dynamic_update_slice_in_dim(
            grad_q, query_part.reshape(local_rows, group_width), index * group_width, 1
        )
        grad_k = lax.dynamic_update_slice_in_dim(
            grad_k, key_part.reshape(total_keys, group_width), index * group_width, 1
        )
        grad_v = lax.dynamic_update_slice_in_dim(
            grad_v, value_part.reshape(total_keys, group_width), index * group_width, 1
        )
        return (grad_q, grad_k, grad_v)

    zero_keys = jnp.zeros((total_keys, width), jnp.float32)
    grad_q, grad_k, grad_v = lax.fori_loop(
        0, group_count, attend_back, (zero_rows, zero_keys, zero_keys)
    )
    share_k, share_v = (
        lax.psum_scatter(
            grad_k[:prompt_rows].astype(jnp.bfloat16),
            ("tok", "fs"),
            scatter_dimension=1,
            tiled=True,
        ).astype(jnp.float32),
        lax.psum_scatter(
            grad_v[:prompt_rows].astype(jnp.bfloat16),
            ("tok", "fs"),
            scatter_dimension=1,
            tiled=True,
        ).astype(jnp.float32),
    )
    prompt_dk, prompt_dv = (
        lax.all_gather(share_k.astype(jnp.bfloat16), ("tok", "fs"), axis=1, tiled=True).astype(
            share_k.dtype
        ),
        lax.all_gather(share_v.astype(jnp.bfloat16), ("tok", "fs"), axis=1, tiled=True).astype(
            share_v.dtype
        ),
    )
    holder = jnp.minimum(device, holders - 1)
    owned = device < holders
    mine_k = (
        jnp.where(
            owned, lax.dynamic_slice_in_dim(prompt_dk, holder * local_rows, local_rows, 0), 0.0
        )
        + grad_k[prompt_rows:]
    )
    mine_v = (
        jnp.where(
            owned, lax.dynamic_slice_in_dim(prompt_dv, holder * local_rows, local_rows, 0), 0.0
        )
        + grad_v[prompt_rows:]
    )
    grad_qraw = (
        unrotate(grad_q.reshape(local_rows, heads, head_size), cosine, sine)
        .reshape(local_rows, width)
        .astype(jnp.bfloat16)
    )
    grad_kraw = (
        unrotate(mine_k.reshape(local_rows, heads, head_size), cosine, sine)
        .reshape(local_rows, width)
        .astype(jnp.bfloat16)
    )
    grad_vraw = mine_v.astype(jnp.bfloat16)
    pieces = (
        lax.all_gather(query_weight, ("tok", "fs"), axis=0, tiled=True),
        lax.all_gather(key_weight, ("tok", "fs"), axis=0, tiled=True),
        lax.all_gather(value_weight, ("tok", "fs"), axis=0, tiled=True),
        lax.all_gather(first_gain, ("tok", "fs"), axis=0, tiled=True),
    )
    section = (
        contract_cols(grad_qraw, pieces[0])
        + contract_cols(grad_kraw, pieces[1])
        + contract_cols(grad_vraw, pieces[2])
    )
    normed = normed_one
    grad_normed = section * pieces[3].astype(jnp.float32)[None, :]
    gain_sum = jnp.sum(section * normed, axis=0)
    three_grads = jnp.concatenate([grad_qraw, grad_kraw, grad_vraw], axis=1)
    attention_grad = weight_sums(kept_one, three_grads)
    input_grad = grad_second + pull_one(grad_normed)[0]
    output_grad, first_gain_grad, second_gain_grad = (
        lax.psum_scatter(output_full, ("grp", "tok", "fs"), scatter_dimension=0, tiled=True),
        lax.psum_scatter(gain_sum, ("grp", "tok", "fs"), scatter_dimension=0, tiled=True),
        lax.psum_scatter(gain_two, ("grp", "tok", "fs"), scatter_dimension=0, tiled=True),
    )
    return (
        layer_output,
        input_grad,
        attention_grad[:, :width],
        attention_grad[:, width : 2 * width],
        attention_grad[:, 2 * width :],
        output_grad,
        mixer_grad[:, :ff_width],
        mixer_grad[:, ff_width:],
        down_grad,
        first_gain_grad,
        second_gain_grad,
    )


def solution(mesh):
    layered = mesh.shape["grp"] == mesh.shape["tok"] == 4 and mesh.shape["fs"] == 2
    return jax.shard_map(
        make_layered(mesh) if layered else spread_local,
        mesh=mesh,
        in_specs=(
            P(("grp", "tok", "fs"), None),
            P(("grp", "tok", "fs"), None),
            P("grp", None),
            P(("tok", "fs"), None),
            P(("tok", "fs"), None),
            P(("tok", "fs"), None),
            P(("tok", "fs"), None),
            P(("tok", "fs"), None),
            P(("tok", "fs"), None),
            P(("tok", "fs"), None),
            P(("tok", "fs")),
            P(("tok", "fs")),
        ),
        out_specs=(
            P(("grp", "tok", "fs"), None),
            P(("grp", "tok", "fs"), None),
            P(("grp", "tok", "fs"), None),
            P(("grp", "tok", "fs"), None),
            P(("grp", "tok", "fs"), None),
            P(("grp", "tok", "fs"), None),
            P(("grp", "tok", "fs"), None),
            P(("grp", "tok", "fs"), None),
            P(("grp", "tok", "fs"), None),
            P(("grp", "tok", "fs")),
            P(("grp", "tok", "fs")),
        ),
        check_vma=False,
    )
```
